32 devices in a mesh: seq: 8 (over z, x), round: 4 (over y, core).
Axes of the slice: x: 2, y: 2, z: 4, core: 2. Of those that a mesh axis runs over, the one named last changes fastest.
Arguments:
- first_half: bfloat16 [8192, 1024], P(('seq', 'round')), may hold values from -6 to 6
- second_half: bfloat16 [8192, 1024], P(('seq', 'round')), may hold values from -6 to 6
- qk_weight: bfloat16 [1024, 1024], P(('seq', 'round')), may hold values from -0.1875 to 0.1875
- value_weight: bfloat16 [1024, 1024], P(('seq', 'round')), may hold values from -0.1875 to 0.1875
- output_weight: bfloat16 [1024, 1024], P(('seq', 'round')), may hold values from -1 to 1
- inner_weight: bfloat16 [1024, 4096], P(('seq', 'round')), may hold values from -0.1875 to 0.1875
- outer_weight: bfloat16 [4096, 1024], P(('seq', 'round')), may hold values from -0.09375 to 0.09375
- attn_gain: bfloat16 [1024], P(('seq', 'round')), may hold values from 0.5 to 1.5
- attn_shift: bfloat16 [1024], P(('seq', 'round')), may hold values from -1 to 1
- ffn_gain: bfloat16 [1024], P(('seq', 'round')), may hold values from 0.5 to 1.5
- ffn_shift: bfloat16 [1024], P(('seq', 'round')), may hold values from -1 to 1
- buckets: int32 [4, 8192], P('round', 'seq'), may hold values from 0 to 256, as said below
- slots: int32 [4, 8192], P('round', 'seq'), may hold values from 0 to 16383, as said below
- first_grad: bfloat16 [8192, 1024], P(('seq', 'round')), may hold values from -6 to 6
- second_grad: bfloat16 [8192, 1024], P(('seq', 'round')), may hold values from -6 to 6
Outputs:
- first_out: bfloat16 [8192, 1024], P(('seq', 'round'))
- second_out: bfloat16 [8192, 1024], P(('seq', 'round'))
- first_back: bfloat16 [8192, 1024], P(('seq', 'round'))
- second_back: bfloat16 [8192, 1024], P(('seq', 'round'))
- qk_grad: float32 [1024, 1024], P(('seq', 'round'))
- value_grad: float32 [1024, 1024], P(('seq', 'round'))
- output_grad: float32 [1024, 1024], P(('seq', 'round'))
- inner_grad: float32 [1024, 4096], P(('seq', 'round'))
- outer_grad: float32 [4096, 1024], P(('seq', 'round'))
- attn_gain_grad: float32 [1024], P(('seq', 'round'))
- attn_shift_grad: float32 [1024], P(('seq', 'round'))
- ffn_gain_grad: float32 [1024], P(('seq', 'round'))
- ffn_shift_grad: float32 [1024], P(('seq', 'round'))
The draws below stay inside these ranges and needn't reach their ends.
Inputs may be any that keep to these rules, and one draw needn't show every extreme that they name: `buckets`: in each round a token's bucket b lies in the range of the block slots // 2048 that it goes to: from that block's index times 32 to that index times 32 plus 32. `slots`: in each round the values are distinct. The tokens that go to one block of 2048 places fill its first places, ordered by bucket and then by token. Of the 1024 tokens of one seq index at most 256 go to one block, and in every round some block receives exactly 256 from every seq index.
All inputs are finite; a program needn't handle non-finite values.
Results may differ from the reference program's by a relative error of at most 0.03.
Values may be sent and summed in bfloat16 or wider, within the bound.
No kernel may reach another device: no remote copies, remote signals or barrier semaphores. Data moves between devices by JAX's collectives and lax.ppermute only.
A program may use at most 256 MiB of HBM per device.

```python
import jax
import jax.numpy as jnp
from jax import lax

D = 1024
HEADS = 8
FF = 4096
SPAN = 64
BUCKETS_DEV = 32
ROUNDS = 4
SEQ_TOK = 1024
TOKENS = 8192
CAP = 256
SLOT_DEV = 2048
N_SEQ = 8


def bucket_layout(key):

    def one_round(round_key, round_number):
        heavy_key, source_key, bucket_key, lone_key, count_key = jax.random.split(round_key, 5)
        drawn_dest = jax.random.randint(heavy_key, (), 0, N_SEQ).astype(jnp.int32)
        heavy_dest = jnp.where(round_number == 0, N_SEQ - 1, drawn_dest).astype(jnp.int32)

        def one_source(block_key):
            order_key, spot_key = jax.random.split(block_key)
            token_order = jax.random.permutation(order_key, SEQ_TOK).astype(jnp.int32)
            spare_spots = jax.random.permutation(spot_key, (N_SEQ - 1) * CAP)[:SEQ_TOK - CAP].astype(jnp.int32)
            other_dest = spare_spots // CAP
            other_dest = other_dest + (other_dest >= heavy_dest).astype(jnp.int32)
            by_order = jnp.concatenate([jnp.full((CAP,), heavy_dest, jnp.int32), other_dest])
            return jnp.zeros((SEQ_TOK,), jnp.int32).at[token_order].set(by_order)
        target = jax.vmap(one_source)(jax.random.split(source_key, N_SEQ)).reshape(TOKENS)
        token_ids = jnp.arange(TOKENS, dtype=jnp.int32)
        per_dest = jnp.sum((target[:, None] == jnp.arange(N_SEQ, dtype=jnp.int32)[None, :]).astype(jnp.int32), axis=0)
        starts = jnp.cumsum(per_dest) - per_dest
        mixing = jax.random.permutation(lone_key, TOKENS).astype(jnp.int32)
        lone_order = jnp.argsort(target * TOKENS + mixing).astype(jnp.int32)
        lone_rank = jnp.zeros((TOKENS,), jnp.int32).at[lone_order].set(token_ids) - starts[target]
        lone_count = jax.random.randint(count_key, (), 1, 4).astype(jnp.int32)
        drawn_bucket = jax.random.randint(bucket_key, (TOKENS,), 0, BUCKETS_DEV - 2).astype(jnp.int32)
        common_bucket = jnp.where(drawn_bucket == 0, 0, drawn_bucket + 3).astype(jnp.int32)
        local_bucket = jnp.where(lone_rank < lone_count, lone_rank + 1, common_bucket).astype(jnp.int32)
        sort_key = (target * (BUCKETS_DEV + 1) + local_bucket) * TOKENS + token_ids
        sorted_order = jnp.argsort(sort_key).astype(jnp.int32)
        ranking = jnp.zeros((TOKENS,), jnp.int32).at[sorted_order].set(token_ids)
        slot_index = target * SLOT_DEV + ranking - starts[target]
        return (target * BUCKETS_DEV + local_bucket, slot_index.astype(jnp.int32))
    return jax.vmap(one_round)(jax.random.split(key, ROUNDS), jnp.arange(ROUNDS, dtype=jnp.int32))


def draw_buckets(key, part):
    return bucket_layout(key)[0]


def draw_slots(key, part):
    return bucket_layout(key)[1]


def steps_of(key, shape, cuts, smallest, top_value):
    factor_of = 1.0
    for dim, parts in cuts:
        heights = jax.random.uniform(jax.random.fold_in(jax.random.fold_in(key, 6), dim), (parts,), jnp.float32, smallest / len(cuts), top_value / len(cuts))
        factor_of = factor_of * jnp.repeat(jnp.exp(heights), shape[dim] // parts).reshape((-1,) + (1,) * (len(shape) - 1 - dim))
    return factor_of


def bell_draw(stream_key, dims, scale, limit, cuts=(), held_as=jnp.bfloat16):
    level = steps_of(stream_key, dims, cuts, -0.22, 0.18) if cuts else 1.0
    values = jax.random.normal(stream_key, dims, jnp.float32) * scale * level
    return jnp.minimum(jnp.maximum(values, -limit), limit).astype(held_as)


def setup_inputs(seed: int = 0) -> dict:
    keys = jax.random.split(jax.random.key(seed), 16)
    first_half = bell_draw(keys[0], (TOKENS, D), 1.0, 6.0, ((0, 32),))
    second_half = bell_draw(keys[1], (TOKENS, D), 1.0, 6.0, ((0, 32),))
    qk_weight = bell_draw(keys[2], (D, D), D ** -0.5, 0.1875, ((0, 32),))
    value_weight = bell_draw(keys[3], (D, D), D ** -0.5, 0.1875, ((0, 32),))
    output_weight = bell_draw(keys[4], (D, D), (D // 32) ** -0.5, 1.0, ((0, 32),))
    inner_weight = bell_draw(keys[5], (D, FF), D ** -0.5, 0.1875, ((0, 32),))
    outer_weight = bell_draw(keys[6], (FF, D), FF ** -0.5, 0.09375, ((0, 32),))
    attn_gain = jnp.clip(1.0 + 0.1 * jax.random.normal(keys[7], (D,), jnp.float32), 0.5, 1.5).astype(jnp.bfloat16)
    attn_shift = bell_draw(keys[8], (D,), 0.2, 1.0, ((0, 32),))
    ffn_gain = jnp.clip(1.0 + 0.1 * jax.random.normal(keys[9], (D,), jnp.float32), 0.5, 1.5).astype(jnp.bfloat16)
    ffn_shift = bell_draw(keys[10], (D,), 0.2, 1.0, ((0, 32),))
    buckets = draw_buckets(jax.random.fold_in(keys[15], 71), 0)
    slots = draw_slots(jax.random.fold_in(keys[15], 71), 0)
    first_grad = bell_draw(keys[13], (TOKENS, D), 1.0, 6.0, ((0, 32),))
    second_grad = bell_draw(keys[14], (TOKENS, D), 1.0, 6.0, ((0, 32),))
    return dict(first_half=first_half, second_half=second_half, qk_weight=qk_weight, value_weight=value_weight, output_weight=output_weight, inner_weight=inner_weight, outer_weight=outer_weight, attn_gain=attn_gain, attn_shift=attn_shift, ffn_gain=ffn_gain, ffn_shift=ffn_shift, buckets=buckets, slots=slots, first_grad=first_grad, second_grad=second_grad)


@jax.custom_vjp
def low(v):
    return lax.optimization_barrier(v.astype(jnp.bfloat16)).astype(jnp.float32)

@jax.custom_vjp
def low_back(v):
    return v

def low_keep(v):
    return (low(v), None)

def low_pass(kept, grad):
    return (grad,)

def back_keep(v):
    return (v, None)

def back_low(kept, grad):
    return (low(grad),)
low.defvjp(low_keep, low_pass)
low_back.defvjp(back_keep, back_low)
EXACT_PRECISION = lax.Precision.HIGHEST
NORM_EPS = 1e-05
KEY_EPS = 1e-06
MASKED = -1000000000.0

def matmul(left_side, right_side):
    return jnp.dot(left_side, right_side, precision=EXACT_PRECISION, preferred_element_type=jnp.float32)

def layer_norm(values, norm_gain, norm_shift):
    centre = values - lax.optimization_barrier(jnp.mean(values, axis=-1, keepdims=True))
    spread = lax.optimization_barrier(jnp.mean(centre * centre, axis=-1, keepdims=True))
    return centre * lax.rsqrt(spread + NORM_EPS) * norm_gain + norm_shift

def unit_keys(query_rows):
    head_view = query_rows.reshape(query_rows.shape[0], HEADS, -1)
    key_scale = lax.rsqrt(lax.optimization_barrier(jnp.mean(head_view * head_view, axis=-1, keepdims=True)) + KEY_EPS)
    return (head_view * key_scale * head_view.shape[-1] ** (-0.5)).reshape(query_rows.shape)

def with_previous(current, leading):
    earlier = jnp.concatenate([leading[None], current[:-1]], axis=0)
    return jnp.concatenate([earlier, current], axis=1)

def permitted(query_bucket, key_bucket, key_valid):
    span_width = query_bucket.shape[1]
    allowed = (query_bucket[:, :, None] == key_bucket[:, None, :]) & (key_valid[:, None, :] > 0)
    itself = jnp.arange(2 * span_width)[None, :] == jnp.arange(span_width)[:, None] + span_width
    others = allowed & jnp.logical_not(itself[None])
    lonely = jnp.logical_not(jnp.any(others, axis=-1, keepdims=True))
    return others | allowed & itself[None] & lonely

def device_attention(pieces):
    query_rows, key_rows, value_rows, bucket_rows, valid_rows, halo_keys, halo_value, halo_bucket, halo_valid = pieces
    span_total = query_rows.shape[0] // SPAN
    spanned = (span_total, SPAN, HEADS, -1)
    query_spans = query_rows.reshape(spanned)
    key_spans = with_previous(key_rows.reshape(spanned), halo_keys.reshape(spanned[1:]))
    value_spans = with_previous(value_rows.reshape(spanned), halo_value.reshape(spanned[1:]))
    query_bucket = bucket_rows.reshape(span_total, SPAN)
    key_bucket = with_previous(query_bucket, halo_bucket)
    key_valid = with_previous(valid_rows.reshape(span_total, SPAN), halo_valid)
    allowed = permitted(query_bucket, key_bucket, key_valid)
    scores = low_back(jnp.einsum('cqhd,ckhd->chqk', query_spans, key_spans, precision=EXACT_PRECISION))
    masked = jnp.where(allowed[:, None], scores, MASKED)
    log_totals = jax.nn.logsumexp(masked, axis=-1)
    probabilities = low(jax.nn.softmax(masked, axis=-1))
    outputs = jnp.einsum('chqk,ckhd->cqhd', probabilities, value_spans, precision=EXACT_PRECISION)
    return (outputs.reshape(query_rows.shape), jnp.transpose(log_totals, (0, 2, 1)).reshape(query_rows.shape[0], HEADS))

def round_attention(query, value, bucket_row, slot_row):
    query = low_back(query)
    value = low_back(value)
    places = N_SEQ * SLOT_DEV
    token_ids = jnp.arange(TOKENS, dtype=jnp.int32)
    owner_token = jnp.full((places,), TOKENS, jnp.int32).at[slot_row].set(token_ids)
    filled = owner_token < TOKENS
    picked = jnp.minimum(owner_token, TOKENS - 1)
    sorted_query = jnp.where(filled[:, None], query[picked], 0.0)
    sorted_value = jnp.where(filled[:, None], value[picked], 0.0)
    sorted_bucket = jnp.where(filled, bucket_row[picked], -1).astype(jnp.int32)
    valid_flag = filled.astype(jnp.int32)
    key_rows = low(unit_keys(sorted_query))
    blocks = (N_SEQ, SLOT_DEV)
    filled_count = lax.optimization_barrier(jnp.sum(valid_flag.reshape(blocks), axis=1))
    last_span = (jnp.maximum(filled_count - 1, 0) // SPAN).astype(jnp.int32)

    def tail_span(values):
        per_block = values.reshape(blocks + values.shape[1:])
        taken_rows = jax.vmap(lambda rows, chosen: lax.dynamic_slice_in_dim(rows, (chosen * SPAN).astype(jnp.int32), SPAN, 0))(per_block, last_span)
        return jnp.concatenate([jnp.zeros_like(taken_rows[:1]), taken_rows[:-1]], axis=0)
    pieces = (sorted_query.reshape(N_SEQ, SLOT_DEV, D), key_rows.reshape(N_SEQ, SLOT_DEV, D), sorted_value.reshape(N_SEQ, SLOT_DEV, D), sorted_bucket.reshape(blocks), valid_flag.reshape(blocks), tail_span(key_rows), tail_span(sorted_value), tail_span(sorted_bucket), tail_span(valid_flag))
    round_outs, log_totals = lax.map(jax.checkpoint(device_attention), pieces)
    out_tokens = round_outs.reshape(places, D)[slot_row]
    lse_tokens = log_totals.reshape(places, HEADS)[slot_row]
    return (low_back(low(out_tokens)), lse_tokens)

def forward(first_half, second_half, qk_weight, value_weight, output_weight, inner_weight, outer_weight, attn_gain, attn_shift, ffn_gain, ffn_shift, buckets, slots):
    normed = low(layer_norm(second_half, attn_gain, attn_shift))
    query = low_back(low(matmul(normed, qk_weight)))
    value = low_back(low(matmul(normed, value_weight)))

    def one_round(pair):
        return round_attention(query, value, pair[0], pair[1])
    round_outs, log_totals = lax.map(jax.checkpoint(one_round), (buckets, slots))
    weights = jnp.exp(log_totals)
    weight_sum = lax.optimization_barrier(jnp.sum(weights, axis=0))
    head_outs = round_outs.reshape(ROUNDS, TOKENS, HEADS, -1)
    mixed_heads = lax.optimization_barrier(jnp.sum(weights[..., None] * head_outs, axis=0)) / weight_sum[..., None]
    attn_branch = low_back(matmul(low(mixed_heads.reshape(TOKENS, D)), output_weight))
    first_sum = first_half + attn_branch
    ffn_normed = low(layer_norm(first_sum, ffn_gain, ffn_shift))
    inner_act = low_back(matmul(ffn_normed, inner_weight))
    hidden = low(jax.nn.gelu(inner_act, approximate=False))
    second_sum = second_half + low_back(matmul(hidden, outer_weight))
    return (first_sum, second_sum)

def reference(first_half, second_half, qk_weight, value_weight, output_weight, inner_weight, outer_weight, attn_gain, attn_shift, ffn_gain, ffn_shift, buckets, slots, first_grad, second_grad):
    floats = tuple((member.astype(jnp.float32) for member in (first_half, second_half, qk_weight, value_weight, output_weight, inner_weight, outer_weight, attn_gain, attn_shift, ffn_gain, ffn_shift)))

    def forward_run(*params):
        return forward(*params, buckets, slots)
    (first_sum, second_sum), pull_back = jax.vjp(forward_run, *floats)
    gradients = pull_back((first_grad.astype(jnp.float32), second_grad.astype(jnp.float32)))
    return (first_sum.astype(jnp.bfloat16), second_sum.astype(jnp.bfloat16), gradients[0].astype(jnp.bfloat16), gradients[1].astype(jnp.bfloat16), gradients[2], gradients[3], gradients[4], gradients[5], gradients[6], gradients[7], gradients[8], gradients[9], gradients[10])
```

```python
import functools
import math

import jax
import jax.numpy as jnp
from jax import lax
from jax.experimental import pallas as pl
from jax.experimental.pallas import tpu as pltpu
from jax.sharding import Mesh
from jax.sharding import PartitionSpec as P

HEADS = 8
NORM_EPS = 1e-05
MASKED = -1000000000.0
SPAN = 64
HEADD = 128
PAD = 16
UNROLL = 17
TOKB = 128
CHUNK = 4096
VMEM_LIMIT = 60 * 2**20
KEY_EPS = 1e-06
bf = jnp.bfloat16
f32 = jnp.float32


def product(left_side, right_side):
    return jnp.dot(left_side, right_side, preferred_element_type=f32)


def against(left_side, right_side):
    return lax.dot_general(
        left_side, right_side, (((0,), (0,)), ((), ())), preferred_element_type=f32
    )


def through(left_side, right_side):
    return lax.dot_general(
        left_side, right_side, (((1,), (1,)), ((), ())), preferred_element_type=f32
    )


def aligned(start, size, step=SPAN):
    return pl.ds(pl.multiple_of(start, step), size)


def fill_zero(ref, first=0, rows=None):
    rows = ref.shape[0] if rows is None else rows

    def body(step, carry):
        ref[aligned(first + step * SPAN, SPAN), :] = jnp.zeros((SPAN, ref.shape[1]), ref.dtype)
        return carry

    lax.fori_loop(0, rows // SPAN, body, 0)


def diagonal():
    rows = lax.broadcasted_iota(jnp.int32, (TOKB, TOKB), 0)
    return rows == lax.broadcasted_iota(jnp.int32, (TOKB, TOKB), 1)


def forward_kernel(
    own_rows,
    load_steps,
    place_ref,
    token_ref,
    bias_ref,
    pay_ref,
    query_ref,
    key_ref,
    value_ref,
    prob_ref,
    sum_ref,
    wide_a,
    wide_b,
    stage_a,
    stage_b,
):
    step = pl.program_id(0)
    own_spans = bias_ref.shape[0] // SPAN
    tail = SPAN * (own_spans + 1)

    @pl.when(step == 0)
    def _():
        fill_zero(wide_a)
        fill_zero(wide_b)

    @pl.when(step < load_steps)
    def _():
        def scatter(block, carry):
            both = token_ref[aligned(block * TOKB, TOKB, TOKB), :].astype(f32)
            stage_a[...] = both[:, :HEADD]
            stage_b[...] = both[:, HEADD:]
            for row in range(TOKB):
                place = place_ref[step * CHUNK + block * TOKB + row]
                wide_a[pl.ds(place, 1), :] = stage_a[row : row + 1, :]
                wide_b[pl.ds(place, 1), :] = stage_b[row : row + 1, :]
            return carry

        lax.fori_loop(0, CHUNK // TOKB, scatter, 0)

    def unit_keys(query):
        square = jnp.sum(query * query, axis=-1, keepdims=True)
        scale = lax.rsqrt(square * (1.0 / HEADD) + KEY_EPS) * HEADD**-0.5
        return (query * scale).astype(bf)

    @pl.when(step == load_steps)
    def _():
        query_ref[:SPAN, :] = wide_a[:SPAN, :].astype(bf)
        key_ref[:SPAN, :] = unit_keys(wide_a[:SPAN, :])
        value_ref[:SPAN, :] = wide_b[:SPAN, :].astype(bf)
        wide_a[:SPAN, :] = jnp.zeros((SPAN, HEADD), f32)
        wide_b[:SPAN, :] = jnp.zeros((SPAN, HEADD), f32)
        for ref in (query_ref, key_ref, value_ref):
            ref[pl.ds(tail, SPAN), :] = jnp.zeros((SPAN, HEADD), bf)
        ones = jnp.ones((2 * SPAN, HEADD), bf)

        def spans(group, carry):
            first = group * (UNROLL * SPAN)
            prev = aligned(first, SPAN)
            own = aligned(first, UNROLL * SPAN)
            here = aligned(first + SPAN, UNROLL * SPAN)
            query_wide = wide_a[here, :]
            values = wide_b[here, :].astype(bf)
            bias = bias_ref[own, :]
            keys = jnp.concatenate([key_ref[prev, :], unit_keys(query_wide)], axis=0)
            seen = jnp.concatenate([value_ref[prev, :], values], axis=0)
            query = query_wide.astype(bf)
            results = []
            for span in range(UNROLL):
                mine = slice(span * SPAN, (span + 1) * SPAN)
                both = slice(span * SPAN, (span + 2) * SPAN)
                raised = jnp.exp(through(query[mine], keys[both]) + bias[mine])
                low = raised.astype(bf)
                total = product(low, ones)
                inverse = jnp.where(total > 0.0, 1.0 / total, 0.0)
                results.append((product(low, seen[both]), total, (raised * inverse).astype(bf)))
            query_ref[here, :] = query
            key_ref[here, :] = keys[SPAN:]
            value_ref[here, :] = values
            for span, (weighted, total, probs) in enumerate(results):
                at = aligned(first + (span + 1) * SPAN, SPAN)
                wide_a[at, :] = weighted
                wide_b[at, :] = total
                prob_ref[aligned(first + span * SPAN, SPAN), :] = probs
            return carry

        lax.fori_loop(0, own_spans // UNROLL, spans, 0)
        wide_a[pl.ds(tail, SPAN), :] = jnp.zeros((SPAN, HEADD), f32)
        wide_b[pl.ds(tail, SPAN), :] = jnp.zeros((SPAN, HEADD), f32)

    @pl.when(step > load_steps)
    def _():
        blocks = own_rows // TOKB
        per_step = CHUNK // own_rows
        eye = diagonal()
        sum_rows = lax.broadcasted_iota(jnp.int32, (PAD, TOKB), 0)
        offset = (step - load_steps - 1) * CHUNK

        def collect(chunk, carry):
            first = chunk * (own_rows + PAD)
            sums = jnp.zeros((PAD, TOKB), f32)
            for block in range(blocks):
                start = offset + chunk * own_rows + block * TOKB
                for row in range(TOKB):
                    place = place_ref[start + row]
                    stage_a[row : row + 1, :] = wide_a[pl.ds(place, 1), :]
                    stage_b[row : row + 1, :] = wide_b[pl.ds(place, 1), :]
                pay_ref[aligned(first + block * TOKB, TOKB, PAD), :] = stage_a[...].astype(bf)
                packed = jnp.sum(jnp.where(eye, stage_b[...], 0.0), axis=0, keepdims=True)
                sum_ref[pl.ds(chunk * blocks + block, 1), :] = packed
                sums = jnp.where(sum_rows == block, packed, sums)
            pay_ref[aligned(first + own_rows, PAD, PAD), :] = sums.astype(bf)
            return carry

        lax.fori_loop(0, per_step, collect, 0)


def attend_forward(place, tokens_in, bias, own_rows):
    tokens = tokens_in.shape[0]
    steps = tokens // CHUNK
    own_spans = bias.shape[0] // SPAN
    rows = SPAN * (own_spans + 2)
    pay_rows = CHUNK // own_rows * (own_rows + PAD)
    once = pl.Buffered(1)

    def whole(shape):
        return pl.BlockSpec(shape, lambda step: (0, 0), pipeline_mode=once)

    def first_part(shape):
        return pl.BlockSpec(shape, lambda step: (jnp.minimum(step, steps - 1), 0))

    def last_part(shape):
        return pl.BlockSpec(shape, lambda step: (jnp.maximum(step - steps - 1, 0), 0))

    sorted_rows = jax.ShapeDtypeStruct((rows, HEADD), bf)
    return pl.pallas_call(
        functools.partial(forward_kernel, own_rows, steps),
        grid=(2 * steps + 1,),
        out_shape=(
            jax.ShapeDtypeStruct((steps * pay_rows, HEADD), bf),
            sorted_rows,
            sorted_rows,
            sorted_rows,
            jax.ShapeDtypeStruct((own_spans * SPAN, 2 * SPAN), bf),
            jax.ShapeDtypeStruct((tokens // TOKB, TOKB), f32),
        ),
        in_specs=[
            pl.BlockSpec(memory_space=pltpu.SMEM),
            first_part((CHUNK, 2 * HEADD)),
            whole(bias.shape),
        ],
        out_specs=(
            last_part((pay_rows, HEADD)),
            whole((rows, HEADD)),
            whole((rows, HEADD)),
            whole((rows, HEADD)),
            whole((own_spans * SPAN, 2 * SPAN)),
            last_part((CHUNK // TOKB, TOKB)),
        ),
        scratch_shapes=[pltpu.VMEM((rows, HEADD), f32)] * 2 + [pltpu.VMEM((TOKB, HEADD), f32)] * 2,
        compiler_params=pltpu.CompilerParams(vmem_limit_bytes=VMEM_LIMIT),
        name="attend_forward",
    )(place, tokens_in, bias)


def backward_kernel(
    own_rows,
    load_steps,
    place_ref,
    pay_ref,
    sum_ref,
    query_ref,
    key_ref,
    value_ref,
    prob_ref,
    out_ref,
    wide_a,
    wide_b,
    wide_c,
    stage_a,
    stage_b,
):
    step = pl.program_id(0)
    own_spans = prob_ref.shape[0] // SPAN
    tail = SPAN * (own_spans + 1)

    @pl.when(step == 0)
    def _():
        fill_zero(wide_a)
        fill_zero(wide_b)

    @pl.when(step < load_steps)
    def _():
        blocks = own_rows // TOKB
        eye = diagonal()
        ones = jnp.ones((2 * TOKB, TOKB), bf)

        def lanes(row):
            high = row.astype(bf).astype(f32)
            parts = [jnp.where(eye, high, 0.0), jnp.where(eye, row - high, 0.0)]
            return product(jnp.concatenate(parts, axis=1).astype(bf), ones)

        def scatter(chunk, carry):
            first = chunk * (own_rows + PAD)
            extra = pay_ref[aligned(first + own_rows, PAD, PAD), :].astype(f32)
            for block in range(blocks):
                share = sum_ref[pl.ds(chunk * blocks + block, 1), :]
                share = share / extra[blocks + block : blocks + block + 1, :]
                rows = pay_ref[aligned(first + block * TOKB, TOKB, PAD), :].astype(f32)
                stage_a[...] = rows * lanes(share)
                stage_b[...] = lanes(share * extra[block : block + 1, :])
                start = step * CHUNK + chunk * own_rows + block * TOKB
                for row in range(TOKB):
                    place = place_ref[start + row]
                    wide_a[pl.ds(place, 1), :] = stage_a[row : row + 1, :]
                    wide_b[pl.ds(place, 1), :] = stage_b[row : row + 1, :]
            return carry

        lax.fori_loop(0, CHUNK // own_rows, scatter, 0)

    def pulled(query_low, d_query, d_keys):
        query = query_low.astype(f32)
        inverse = lax.rsqrt(
            jnp.sum(query * query, axis=-1, keepdims=True) * (1.0 / HEADD) + KEY_EPS
        )
        along = jnp.sum(query * d_keys, axis=-1, keepdims=True)
        scale = inverse * HEADD**-0.5
        return d_query + scale * d_keys - (scale * inverse * inverse * along * (1.0 / HEADD)) * query

    @pl.when(step == load_steps)
    def _():
        for ref in (wide_a, wide_b, wide_c):
            ref[:SPAN, :] = jnp.zeros((SPAN, HEADD), f32)
        zero = jnp.zeros((SPAN, HEADD), bf)

        def spans(group, carry):
            first = group * (UNROLL * SPAN)
            prev = aligned(first, SPAN)
            own = aligned(first, UNROLL * SPAN)
            here = aligned(first + SPAN, UNROLL * SPAN)
            around = aligned(first, (UNROLL + 1) * SPAN)
            query = query_ref[around, :]
            keys = key_ref[around, :]
            values = value_ref[around, :]
            probs = prob_ref[own, :]
            d_out = wide_a[here, :].astype(bf)
            delta = wide_b[here, :]
            d_query = [wide_a[prev, :]]
            d_keys = [wide_b[prev, :]]
            d_values = [wide_c[prev, :]]
            for span in range(UNROLL):
                mine = slice(span * SPAN, (span + 1) * SPAN)
                after = slice((span + 1) * SPAN, (span + 2) * SPAN)
                both = slice(span * SPAN, (span + 2) * SPAN)
                d_probs = through(d_out[mine], values[both])
                prob = probs[mine]
                d_scores = (prob.astype(f32) * (d_probs - delta[mine])).astype(bf)
                d_query.append(product(d_scores, keys[both]))
                right = jnp.concatenate(
                    [
                        jnp.concatenate([query[after], zero], axis=1),
                        jnp.concatenate([zero, d_out[mine]], axis=1),
                    ],
                    axis=0,
                )
                pair = against(jnp.concatenate([d_scores, prob], axis=0), right)
                d_keys[-1] = d_keys[-1] + pair[:SPAN, :HEADD]
                d_values[-1] = d_values[-1] + pair[:SPAN, HEADD:]
                d_keys.append(pair[SPAN:, :HEADD])
                d_values.append(pair[SPAN:, HEADD:])
            for span in range(UNROLL + 1):
                at = aligned(first + span * SPAN, SPAN)
                wide_c[at, :] = d_values[span]
                if span < UNROLL:
                    rows = slice(span * SPAN, (span + 1) * SPAN)
                    wide_a[at, :] = pulled(query[rows], d_query[span], d_keys[span])
                else:
                    wide_a[at, :] = d_query[span]
                    wide_b[at, :] = d_keys[span]
            return carry

        lax.fori_loop(0, own_spans // UNROLL, spans, 0)
        last = pl.ds(tail - SPAN, SPAN)
        wide_a[last, :] = pulled(query_ref[last, :], wide_a[last, :], wide_b[last, :])
        wide_a[pl.ds(tail, SPAN), :] = jnp.zeros((SPAN, HEADD), f32)
        wide_c[pl.ds(tail, SPAN), :] = jnp.zeros((SPAN, HEADD), f32)

    @pl.when(step > load_steps)
    def _():
        offset = (step - load_steps - 1) * CHUNK

        def collect(block, carry):
            for row in range(TOKB):
                place = place_ref[offset + block * TOKB + row]
                stage_a[row : row + 1, :] = wide_a[pl.ds(place, 1), :]
                stage_b[row : row + 1, :] = wide_c[pl.ds(place, 1), :]
            here = aligned(block * TOKB, TOKB, TOKB)
            out_ref[here, :HEADD] = stage_a[...].astype(bf)
            out_ref[here, HEADD:] = stage_b[...].astype(bf)
            return carry

        lax.fori_loop(0, CHUNK // TOKB, collect, 0)


def attend_backward(place, pay, sums, query, keys, values, probs, own_rows):
    tokens = place.shape[0]
    steps = tokens // CHUNK
    rows = query.shape[0]
    pay_rows = CHUNK // own_rows * (own_rows + PAD)
    once = pl.Buffered(1)

    def whole(shape):
        return pl.BlockSpec(shape, lambda step: (0, 0), pipeline_mode=once)

    def first_part(shape):
        return pl.BlockSpec(shape, lambda step: (jnp.minimum(step, steps - 1), 0))

    def last_part(shape):
        return pl.BlockSpec(shape, lambda step: (jnp.maximum(step - steps - 1, 0), 0))

    return pl.pallas_call(
        functools.partial(backward_kernel, own_rows, steps),
        grid=(2 * steps + 1,),
        out_shape=jax.ShapeDtypeStruct((tokens, 2 * HEADD), bf),
        in_specs=[
            pl.BlockSpec(memory_space=pltpu.SMEM),
            first_part((pay_rows, HEADD)),
            first_part((CHUNK // TOKB, TOKB)),
            whole((rows, HEADD)),
            whole((rows, HEADD)),
            whole((rows, HEADD)),
            whole(probs.shape),
        ],
        out_specs=last_part((CHUNK, 2 * HEADD)),
        scratch_shapes=[pltpu.VMEM((rows, HEADD), f32)] * 3 + [pltpu.VMEM((TOKB, HEADD), f32)] * 2,
        compiler_params=pltpu.CompilerParams(vmem_limit_bytes=VMEM_LIMIT),
        name="attend_backward",
    )(place, pay, sums, query, keys, values, probs)


ALL = ("hd", "kk", "ry", "rc")
SWAP = [(0, 1), (1, 0)]


def layer_norm(values, norm_gain, norm_shift):
    centre = values - jnp.mean(values, axis=-1, keepdims=True)
    spread = jnp.mean(centre * centre, axis=-1, keepdims=True)
    return centre * lax.rsqrt(spread + NORM_EPS) * norm_gain + norm_shift


def exact_gelu(values):
    return jax.nn.gelu(values, approximate=False)


def exchange(parts):
    return lax.all_to_all(parts, "hd", split_axis=0, concat_axis=0, tiled=True)


def spread_round(mine):
    if lax.axis_size("kk") > 1:
        mine = lax.all_gather(mine, "kk", axis=0, tiled=False)
    else:
        mine = mine[None]
    pair = jnp.stack([mine, lax.ppermute(mine, "ry", SWAP)])
    return jnp.stack([pair, lax.ppermute(pair, "rc", SWAP)])


def sum_round(parts):
    def folded(both, axis):
        got = lax.ppermute(both[1], axis, SWAP)
        return (both[0].astype(f32) + got.astype(f32)).astype(bf)

    total = folded(folded(parts, "rc"), "ry")
    if lax.axis_size("kk") > 1:
        return lax.psum_scatter(total, "kk", scatter_dimension=0, tiled=False)
    return total[0]


def reduce_rows(part):
    return lax.psum_scatter(part.astype(bf), ALL, scatter_dimension=0, tiled=True).astype(f32)


def per_device(
    first_half,
    second_half,
    qk_weight,
    value_weight,
    output_weight,
    inner_weight,
    outer_weight,
    attn_gain,
    attn_shift,
    ffn_gain,
    ffn_shift,
    buckets,
    slots,
    first_grad,
    second_grad,
):
    heads = lax.axis_size("hd")
    groups = lax.axis_size("kk")
    seq_count = heads * groups
    round_count = lax.axis_size("ry") * lax.axis_size("rc")
    own_rows, model_width = first_half.shape
    group_rows = own_rows * round_count
    slot_rows = 2 * group_rows
    tokens = group_rows * seq_count
    own_spans = min((tokens + (SPAN - 1) * heads) // SPAN, heads * slot_rows // SPAN)
    own_spans = -(-own_spans // UNROLL) * UNROLL

    vectors = jnp.stack([attn_gain, attn_shift, ffn_gain, ffn_shift], axis=1)
    vectors = jnp.pad(vectors, ((0, 0), (0, 124)))
    qkv_shard = jnp.concatenate([qk_weight, value_weight, vectors], axis=1)
    qkv_all = lax.all_gather(qkv_shard, ALL, axis=0, tiled=True)
    qkv_full = qkv_all[:, : 2 * model_width]
    vectors_full = qkv_all[:, 2 * model_width : 2 * model_width + 4].astype(f32).T
    output_full = lax.all_gather(output_weight, ALL, axis=0, tiled=True)
    inner_full = lax.all_gather(inner_weight, ALL, axis=0, tiled=True)
    outer_full = lax.all_gather(outer_weight, ALL, axis=0, tiled=True)

    index_rows = jnp.stack([slots[0], buckets[0]])
    index_all = exchange(jnp.broadcast_to(index_rows[None], (heads,) + index_rows.shape))
    if groups > 1:
        index_all = lax.all_gather(index_all, "kk", axis=1, tiled=False)
    else:
        index_all = index_all[:, None]
    index_all = index_all.reshape(heads, groups, 2, 2, 2, own_rows)
    index_all = jnp.where(lax.axis_index("ry") == 0, index_all, jnp.flip(index_all, 3))
    index_all = jnp.where(lax.axis_index("rc") == 0, index_all, jnp.flip(index_all, 4))
    index_all = jnp.transpose(index_all, (2, 4, 3, 1, 0, 5)).reshape(2, tokens)
    slot_row, bucket_row = index_all[0], index_all[1]
    target = slot_row // slot_rows
    local_place = slot_row - target * slot_rows
    onehot = (target[None, :] == jnp.arange(seq_count, dtype=jnp.int32)[:, None]).astype(jnp.int32)
    counts = jnp.sum(onehot, axis=1)
    first_block = lax.axis_index("kk") * heads
    block_ids = jnp.arange(seq_count, dtype=jnp.int32)
    is_own = (block_ids >= first_block) & (block_ids < first_block + heads)
    span_counts = jnp.where(is_own, -(-counts // SPAN), 0)
    shift = (1 + jnp.cumsum(span_counts) - span_counts) * SPAN
    last_start = jnp.maximum(counts - 1, 0) // SPAN * SPAN
    is_halo = block_ids == first_block - 1
    shift = jnp.where(is_halo, -last_start, shift)
    lowest = jnp.where(is_own, 0, jnp.where(is_halo, last_start, slot_rows))
    token_shift = jnp.sum(onehot * shift[:, None], axis=0)
    token_lowest = jnp.sum(onehot * lowest[:, None], axis=0)
    dump = (own_spans + 1) * SPAN
    place = jnp.where(local_place >= token_lowest, local_place + token_shift, dump)
    place_bucket = jnp.full((dump + SPAN,), -1, jnp.int32).at[place].set(bucket_row)
    span_bucket = place_bucket.reshape(-1, SPAN)[: own_spans + 1]
    key_bucket = jnp.concatenate([span_bucket[:-1], span_bucket[1:]], axis=1)
    query_bucket = span_bucket[1:]
    matching = (query_bucket[:, :, None] == key_bucket[:, None, :]) & (key_bucket[:, None, :] >= 0)
    itself = jnp.arange(2 * SPAN)[None, :] == jnp.arange(SPAN)[:, None] + SPAN
    others = matching & jnp.logical_not(itself[None])
    lonely = jnp.logical_not(jnp.any(others, axis=-1, keepdims=True))
    allowed = others | matching & itself[None] & lonely
    bias = jnp.where(allowed, 0.0, MASKED).astype(f32).reshape(own_spans * SPAN, 2 * SPAN)

    first_in = first_half.astype(f32)
    second_in = second_half.astype(f32)
    normed, attn_norm_pull = jax.vjp(layer_norm, second_in, vectors_full[0], vectors_full[1])
    normed_low = normed.astype(bf)
    qkv_own = product(normed_low, qkv_full).astype(bf)
    head_rows = jnp.transpose(qkv_own.reshape(own_rows, 2, heads, HEADD), (2, 0, 1, 3))
    qkv_group = spread_round(exchange(head_rows.reshape(heads, own_rows, 2 * HEADD)))
    payload, sorted_q, sorted_k, sorted_v, probs, token_sums = attend_forward(
        place, qkv_group.reshape(tokens, 2 * HEADD), bias, own_rows
    )
    packed_rows = own_rows + PAD
    packed = (2, 2, groups, heads, packed_rows, HEADD)
    mixed_parts = exchange(sum_round(payload.reshape(packed)))
    blocks = own_rows // TOKB
    weight_sum = mixed_parts[:, own_rows : own_rows + blocks].reshape(heads, own_rows)
    mixed_heads = mixed_parts[:, :own_rows].astype(f32) / weight_sum.astype(f32)[..., None]
    mixed_low = jnp.transpose(mixed_heads, (1, 0, 2)).reshape(own_rows, model_width).astype(bf)

    first_sum = first_in + product(mixed_low, output_full)
    ffn_normed, ffn_norm_pull = jax.vjp(layer_norm, first_sum, vectors_full[2], vectors_full[3])
    ffn_low = ffn_normed.astype(bf)
    inner_act = product(ffn_low, inner_full)
    hidden, gelu_pull = jax.vjp(exact_gelu, inner_act)
    hidden_low = hidden.astype(bf)
    second_sum = second_in + product(hidden_low, outer_full)
    outer_part = against(hidden_low, second_grad)
    (inner_back,) = gelu_pull(through(second_grad, outer_full))
    inner_back_low = inner_back.astype(bf)
    inner_part = against(ffn_low, inner_back_low)
    first_from_ffn, ffn_gain_part, ffn_shift_part = ffn_norm_pull(
        through(inner_back_low, inner_full)
    )
    first_carry = first_grad.astype(f32) + first_from_ffn
    carry_low = first_carry.astype(bf)
    output_part = against(mixed_low, carry_low)
    mixed_back = through(carry_low, output_full).reshape(own_rows, heads, HEADD)
    mixed_back = jnp.transpose(mixed_back, (1, 0, 2))
    mixed_dot = jnp.sum(mixed_back * mixed_heads, axis=-1).astype(bf)
    tails = jnp.concatenate(
        [
            mixed_dot.reshape(heads, blocks, TOKB),
            weight_sum.reshape(heads, blocks, TOKB),
            jnp.zeros((heads, PAD - 2 * blocks, TOKB), bf),
        ],
        axis=1,
    )
    back_parts = jnp.concatenate([mixed_back.astype(bf), tails], axis=1)
    back_group = spread_round(exchange(back_parts)).reshape(-1, HEADD)
    query_value_back = attend_backward(
        place, back_group, token_sums, sorted_q, sorted_k, sorted_v, probs, own_rows
    )
    back_shape = (2, 2, groups, heads, own_rows, 2 * HEADD)
    own_back = exchange(sum_round(query_value_back.reshape(back_shape)))
    own_back = jnp.transpose(own_back.reshape(heads, own_rows, 2, HEADD), (1, 2, 0, 3))
    own_back = own_back.reshape(own_rows, 2 * model_width)
    qkv_part = against(normed_low, own_back)
    normed_back = through(own_back, qkv_full)
    second_from_attn, attn_gain_part, attn_shift_part = attn_norm_pull(normed_back)
    second_carry = second_grad.astype(f32) + second_from_attn

    inner_grad = reduce_rows(inner_part)
    outer_grad = reduce_rows(outer_part)
    output_grad = reduce_rows(output_part)
    qkv_grad = reduce_rows(qkv_part)
    vector_parts = jnp.stack([attn_gain_part, attn_shift_part, ffn_gain_part, ffn_shift_part])
    device_count = seq_count * round_count
    vector_parts = jnp.transpose(vector_parts.reshape(4, device_count, -1), (1, 0, 2))
    vector_rows = lax.all_to_all(
        vector_parts.reshape(device_count, -1), ALL, split_axis=0, concat_axis=0, tiled=True
    )
    vector_grads = jnp.sum(vector_rows, axis=0).reshape(4, -1)
    return (
        first_sum.astype(bf),
        second_sum.astype(bf),
        carry_low,
        second_carry.astype(bf),
        qkv_grad[:, :model_width],
        qkv_grad[:, model_width:],
        output_grad,
        inner_grad,
        outer_grad,
        vector_grads[0],
        vector_grads[1],
        vector_grads[2],
        vector_grads[3],
    )


def solution(mesh):
    seq_count, round_count = mesh.devices.shape
    shape = (HEADS, seq_count // HEADS, round_count // 2, 2)
    split_mesh = Mesh(mesh.devices.reshape(shape), ALL)
    rows = P(ALL, None)
    vector = P(ALL)
    table = P(("ry", "rc"), ("hd", "kk"))
    in_specs = (rows,) * 7 + (vector,) * 4 + (table,) * 2 + (rows,) * 2
    out_specs = (rows,) * 9 + (vector,) * 4
    return jax.shard_map(
        per_device, mesh=split_mesh, in_specs=in_specs, out_specs=out_specs, check_vma=False
    )
```

```python
import functools

import jax
import jax.numpy as jnp
from jax import lax
from jax.experimental import pallas as pl
from jax.experimental.pallas import tpu as pltpu
from jax.sharding import Mesh
from jax.sharding import PartitionSpec as P

HEADS = 8
NORM_EPS = 1e-05
MASKED = -1000000000.0
SPAN = 64
HEADD = 128
PAD = 16
UNROLL = 17
TOKB = 128
CHUNK = 4096
VMEM_LIMIT = 60 * 2**20
KEY_EPS = 1e-06
bf = jnp.bfloat16
f32 = jnp.float32


def product(left_side, right_side):
    return jnp.dot(left_side, right_side, preferred_element_type=f32)


def against(left_side, right_side):
    return lax.dot_general(
        left_side, right_side, (((0,), (0,)), ((), ())), preferred_element_type=f32
    )


def through(left_side, right_side):
    return lax.dot_general(
        left_side, right_side, (((1,), (1,)), ((), ())), preferred_element_type=f32
    )


def aligned(start, size, step=SPAN):
    return pl.ds(pl.multiple_of(start, step), size)


def fill_zero(ref, first=0, rows=None):
    rows = ref.shape[0] if rows is None else rows

    def body(step, carry):
        ref[aligned(first + step * SPAN, SPAN), :] = jnp.zeros((SPAN, ref.shape[1]), ref.dtype)
        return carry

    lax.fori_loop(0, rows // SPAN, body, 0)


def diagonal():
    rows = lax.broadcasted_iota(jnp.int32, (TOKB, TOKB), 0)
    return rows == lax.broadcasted_iota(jnp.int32, (TOKB, TOKB), 1)


def forward_kernel(
    own_rows,
    load_steps,
    place_ref,
    token_ref,
    bias_ref,
    pay_ref,
    query_ref,
    key_ref,
    value_ref,
    prob_ref,
    sum_ref,
    wide_a,
    wide_b,
    stage_a,
    stage_b,
):
    step = pl.program_id(0)
    own_spans = bias_ref.shape[0] // SPAN
    tail = SPAN * (own_spans + 1)

    @pl.when(step == 0)
    def _():
        fill_zero(wide_a)
        fill_zero(wide_b)

    @pl.when(step < load_steps)
    def _():
        def scatter(block, carry):
            both = token_ref[aligned(block * TOKB, TOKB, TOKB), :].astype(f32)
            stage_a[...] = both[:, :HEADD]
            stage_b[...] = both[:, HEADD:]
            for row in range(TOKB):
                place = place_ref[step * CHUNK + block * TOKB + row]
                wide_a[pl.ds(place, 1), :] = stage_a[row : row + 1, :]
                wide_b[pl.ds(place, 1), :] = stage_b[row : row + 1, :]
            return carry

        lax.fori_loop(0, CHUNK // TOKB, scatter, 0)

    def unit_keys(query):
        square = jnp.sum(query * query, axis=-1, keepdims=True)
        scale = lax.rsqrt(square * (1.0 / HEADD) + KEY_EPS) * HEADD**-0.5
        return (query * scale).astype(bf)

    @pl.when(step == load_steps)
    def _():
        query_ref[:SPAN, :] = wide_a[:SPAN, :].astype(bf)
        key_ref[:SPAN, :] = unit_keys(wide_a[:SPAN, :])
        value_ref[:SPAN, :] = wide_b[:SPAN, :].astype(bf)
        wide_a[:SPAN, :] = jnp.zeros((SPAN, HEADD), f32)
        wide_b[:SPAN, :] = jnp.zeros((SPAN, HEADD), f32)
        for ref in (query_ref, key_ref, value_ref):
            ref[pl.ds(tail, SPAN), :] = jnp.zeros((SPAN, HEADD), bf)
        ones = jnp.ones((2 * SPAN, HEADD), bf)

        def spans(group, carry):
            first = group * (UNROLL * SPAN)
            prev = aligned(first, SPAN)
            own = aligned(first, UNROLL * SPAN)
            here = aligned(first + SPAN, UNROLL * SPAN)
            query_wide = wide_a[here, :]
            values = wide_b[here, :].astype(bf)
            bias = bias_ref[own, :]
            keys = jnp.concatenate([key_ref[prev, :], unit_keys(query_wide)], axis=0)
            seen = jnp.concatenate([value_ref[prev, :], values], axis=0)
            query = query_wide.astype(bf)
            results = []
            for span in range(UNROLL):
                mine = slice(span * SPAN, (span + 1) * SPAN)
                both = slice(span * SPAN, (span + 2) * SPAN)
                raised = jnp.exp(through(query[mine], keys[both]) + bias[mine])
                low = raised.astype(bf)
                total = product(low, ones)
                inverse = jnp.where(total > 0.0, 1.0 / total, 0.0)
                results.append((product(low, seen[both]), total, (raised * inverse).astype(bf)))
            query_ref[here, :] = query
            key_ref[here, :] = keys[SPAN:]
            value_ref[here, :] = values
            for span, (weighted, total, probs) in enumerate(results):
                at = aligned(first + (span + 1) * SPAN, SPAN)
                wide_a[at, :] = weighted
                wide_b[at, :] = total
                prob_ref[aligned(first + span * SPAN, SPAN), :] = probs
            return carry

        lax.fori_loop(0, own_spans // UNROLL, spans, 0)
        wide_a[pl.ds(tail, SPAN), :] = jnp.zeros((SPAN, HEADD), f32)
        wide_b[pl.ds(tail, SPAN), :] = jnp.zeros((SPAN, HEADD), f32)

    @pl.when(step > load_steps)
    def _():
        blocks = own_rows // TOKB
        per_step = CHUNK // own_rows
        eye = diagonal()
        sum_rows = lax.broadcasted_iota(jnp.int32, (PAD, TOKB), 0)
        offset = (step - load_steps - 1) * CHUNK

        def collect(chunk, carry):
            first = chunk * (own_rows + PAD)
            sums = jnp.zeros((PAD, TOKB), f32)
            for block in range(blocks):
                start = offset + chunk * own_rows + block * TOKB
                for row in range(TOKB):
                    place = place_ref[start + row]
                    stage_a[row : row + 1, :] = wide_a[pl.ds(place, 1), :]
                    stage_b[row : row + 1, :] = wide_b[pl.ds(place, 1), :]
                pay_ref[aligned(first + block * TOKB, TOKB, PAD), :] = stage_a[...].astype(bf)
                packed = jnp.sum(jnp.where(eye, stage_b[...], 0.0), axis=0, keepdims=True)
                sum_ref[pl.ds(chunk * blocks + block, 1), :] = packed
                sums = jnp.where(sum_rows == block, packed, sums)
            pay_ref[aligned(first + own_rows, PAD, PAD), :] = sums.astype(bf)
            return carry

        lax.fori_loop(0, per_step, collect, 0)


def attend_forward(place, tokens_in, bias, own_rows):
    tokens = tokens_in.shape[0]
    steps = tokens // CHUNK
    own_spans = bias.shape[0] // SPAN
    rows = SPAN * (own_spans + 2)
    pay_rows = CHUNK // own_rows * (own_rows + PAD)
    once = pl.Buffered(1)

    def whole(shape):
        return pl.BlockSpec(shape, lambda step: (0, 0), pipeline_mode=once)

    def first_part(shape):
        return pl.BlockSpec(shape, lambda step: (jnp.minimum(step, steps - 1), 0))

    def last_part(shape):
        return pl.BlockSpec(shape, lambda step: (jnp.maximum(step - steps - 1, 0), 0))

    sorted_rows = jax.ShapeDtypeStruct((rows, HEADD), bf)
    return pl.pallas_call(
        functools.partial(forward_kernel, own_rows, steps),
        grid=(2 * steps + 1,),
        out_shape=(
            jax.ShapeDtypeStruct((steps * pay_rows, HEADD), bf),
            sorted_rows,
            sorted_rows,
            sorted_rows,
            jax.ShapeDtypeStruct((own_spans * SPAN, 2 * SPAN), bf),
            jax.ShapeDtypeStruct((tokens // TOKB, TOKB), f32),
        ),
        in_specs=[
            pl.BlockSpec(memory_space=pltpu.SMEM),
            first_part((CHUNK, 2 * HEADD)),
            whole(bias.shape),
        ],
        out_specs=(
            last_part((pay_rows, HEADD)),
            whole((rows, HEADD)),
            whole((rows, HEADD)),
            whole((rows, HEADD)),
            whole((own_spans * SPAN, 2 * SPAN)),
            last_part((CHUNK // TOKB, TOKB)),
        ),
        scratch_shapes=[pltpu.VMEM((rows, HEADD), f32)] * 2 + [pltpu.VMEM((TOKB, HEADD), f32)] * 2,
        compiler_params=pltpu.CompilerParams(vmem_limit_bytes=VMEM_LIMIT),
        name="attend_forward",
    )(place, tokens_in, bias)


def backward_kernel(
    own_rows,
    load_steps,
    place_ref,
    pay_ref,
    sum_ref,
    query_ref,
    key_ref,
    value_ref,
    prob_ref,
    out_ref,
    wide_a,
    wide_b,
    wide_c,
    stage_a,
    stage_b,
):
    step = pl.program_id(0)
    own_spans = prob_ref.shape[0] // SPAN
    tail = SPAN * (own_spans + 1)

    @pl.when(step == 0)
    def _():
        fill_zero(wide_a)
        fill_zero(wide_b)

    @pl.when(step < load_steps)
    def _():
        blocks = own_rows // TOKB
        eye = diagonal()
        ones = jnp.ones((2 * TOKB, TOKB), bf)

        def lanes(row):
            high = row.astype(bf).astype(f32)
            parts = [jnp.where(eye, high, 0.0), jnp.where(eye, row - high, 0.0)]
            return product(jnp.concatenate(parts, axis=1).astype(bf), ones)

        def scatter(chunk, carry):
            first = chunk * (own_rows + PAD)
            extra = pay_ref[aligned(first + own_rows, PAD, PAD), :].astype(f32)
            for block in range(blocks):
                share = sum_ref[pl.ds(chunk * blocks + block, 1), :]
                share = share / extra[blocks + block : blocks + block + 1, :]
                rows = pay_ref[aligned(first + block * TOKB, TOKB, PAD), :].astype(f32)
                stage_a[...] = rows * lanes(share)
                stage_b[...] = lanes(share * extra[block : block + 1, :])
                start = step * CHUNK + chunk * own_rows + block * TOKB
                for row in range(TOKB):
                    place = place_ref[start + row]
                    wide_a[pl.ds(place, 1), :] = stage_a[row : row + 1, :]
                    wide_b[pl.ds(place, 1), :] = stage_b[row : row + 1, :]
            return carry

        lax.fori_loop(0, CHUNK // own_rows, scatter, 0)

    def pulled(query_low, d_query, d_keys):
        query = query_low.astype(f32)
        inverse = lax.rsqrt(
            jnp.sum(query * query, axis=-1, keepdims=True) * (1.0 / HEADD) + KEY_EPS
        )
        along = jnp.sum(query * d_keys, axis=-1, keepdims=True)
        scale = inverse * HEADD**-0.5
        return d_query + scale * d_keys - (scale * inverse * inverse * along * (1.0 / HEADD)) * query

    @pl.when(step == load_steps)
    def _():
        for ref in (wide_a, wide_b, wide_c):
            ref[:SPAN, :] = jnp.zeros((SPAN, HEADD), f32)
        zero = jnp.zeros((SPAN, HEADD), bf)

        def spans(group, carry):
            first = group * (UNROLL * SPAN)
            prev = aligned(first, SPAN)
            own = aligned(first, UNROLL * SPAN)
            here = aligned(first + SPAN, UNROLL * SPAN)
            around = aligned(first, (UNROLL + 1) * SPAN)
            query = query_ref[around, :]
            keys = key_ref[around, :]
            values = value_ref[around, :]
            probs = prob_ref[own, :]
            d_out = wide_a[here, :].astype(bf)
            delta = wide_b[here, :]
            d_query = [wide_a[prev, :]]
            d_keys = [wide_b[prev, :]]
            d_values = [wide_c[prev, :]]
            for span in range(UNROLL):
                mine = slice(span * SPAN, (span + 1) * SPAN)
                after = slice((span + 1) * SPAN, (span + 2) * SPAN)
                both = slice(span * SPAN, (span + 2) * SPAN)
                d_probs = through(d_out[mine], values[both])
                prob = probs[mine]
                d_scores = (prob.astype(f32) * (d_probs - delta[mine])).astype(bf)
                d_query.append(product(d_scores, keys[both]))
                right = jnp.concatenate(
                    [
                        jnp.concatenate([query[after], zero], axis=1),
                        jnp.concatenate([zero, d_out[mine]], axis=1),
                    ],
                    axis=0,
                )
                pair = against(jnp.concatenate([d_scores, prob], axis=0), right)
                d_keys[-1] = d_keys[-1] + pair[:SPAN, :HEADD]
                d_values[-1] = d_values[-1] + pair[:SPAN, HEADD:]
                d_keys.append(pair[SPAN:, :HEADD])
                d_values.append(pair[SPAN:, HEADD:])
            for span in range(UNROLL + 1):
                at = aligned(first + span * SPAN, SPAN)
                wide_c[at, :] = d_values[span]
                if span < UNROLL:
                    rows = slice(span * SPAN, (span + 1) * SPAN)
                    wide_a[at, :] = pulled(query[rows], d_query[span], d_keys[span])
                else:
                    wide_a[at, :] = d_query[span]
                    wide_b[at, :] = d_keys[span]
            return carry

        lax.fori_loop(0, own_spans // UNROLL, spans, 0)
        last = pl.ds(tail - SPAN, SPAN)
        wide_a[last, :] = pulled(query_ref[last, :], wide_a[last, :], wide_b[last, :])
        wide_a[pl.ds(tail, SPAN), :] = jnp.zeros((SPAN, HEADD), f32)
        wide_c[pl.ds(tail, SPAN), :] = jnp.zeros((SPAN, HEADD), f32)

    @pl.when(step > load_steps)
    def _():
        offset = (step - load_steps - 1) * CHUNK

        def collect(block, carry):
            for row in range(TOKB):
                place = place_ref[offset + block * TOKB + row]
                stage_a[row : row + 1, :] = wide_a[pl.ds(place, 1), :]
                stage_b[row : row + 1, :] = wide_c[pl.ds(place, 1), :]
            here = aligned(block * TOKB, TOKB, TOKB)
            out_ref[here, :HEADD] = stage_a[...].astype(bf)
            out_ref[here, HEADD:] = stage_b[...].astype(bf)
            return carry

        lax.fori_loop(0, CHUNK // TOKB, collect, 0)


def attend_backward(place, pay, sums, query, keys, values, probs, own_rows):
    tokens = place.shape[0]
    steps = tokens // CHUNK
    rows = query.shape[0]
    pay_rows = CHUNK // own_rows * (own_rows + PAD)
    once = pl.Buffered(1)

    def whole(shape):
        return pl.BlockSpec(shape, lambda step: (0, 0), pipeline_mode=once)

    def first_part(shape):
        return pl.BlockSpec(shape, lambda step: (jnp.minimum(step, steps - 1), 0))

    def last_part(shape):
        return pl.BlockSpec(shape, lambda step: (jnp.maximum(step - steps - 1, 0), 0))

    return pl.pallas_call(
        functools.partial(backward_kernel, own_rows, steps),
        grid=(2 * steps + 1,),
        out_shape=jax.ShapeDtypeStruct((tokens, 2 * HEADD), bf),
        in_specs=[
            pl.BlockSpec(memory_space=pltpu.SMEM),
            first_part((pay_rows, HEADD)),
            first_part((CHUNK // TOKB, TOKB)),
            whole((rows, HEADD)),
            whole((rows, HEADD)),
            whole((rows, HEADD)),
            whole(probs.shape),
        ],
        out_specs=last_part((CHUNK, 2 * HEADD)),
        scratch_shapes=[pltpu.VMEM((rows, HEADD), f32)] * 3 + [pltpu.VMEM((TOKB, HEADD), f32)] * 2,
        compiler_params=pltpu.CompilerParams(vmem_limit_bytes=VMEM_LIMIT),
        name="attend_backward",
    )(place, pay, sums, query, keys, values, probs)


ALL = ("hd", "kk", "ry", "rc")
SEQ = ("hd", "kk")
ROUND = ("ry", "rc")
SWAP = [(0, 1), (1, 0)]


def layer_norm(values, norm_gain, norm_shift):
    centre = values - jnp.mean(values, axis=-1, keepdims=True)
    spread = jnp.mean(centre * centre, axis=-1, keepdims=True)
    return centre * lax.rsqrt(spread + NORM_EPS) * norm_gain + norm_shift


def exact_gelu(values):
    return jax.nn.gelu(values, approximate=False)


def exchange(parts, axes="hd"):
    return lax.all_to_all(parts, axes, split_axis=0, concat_axis=0, tiled=True)


def swapped(value, axis):
    return lax.ppermute(value, axis, SWAP)


def spread_pair(mine):
    pair = jnp.stack([mine, swapped(mine, "ry")])
    return jnp.stack([pair, swapped(pair, "rc")])


def sum_pair(parts):
    def folded(both, axis):
        got = swapped(both[1], axis)
        return (both[0].astype(f32) + got.astype(f32)).astype(bf)

    return folded(folded(parts, "rc"), "ry")


def spread_round(mine):
    if lax.axis_size("kk") > 1:
        mine = lax.all_gather(mine, "kk", axis=0, tiled=False)
    return spread_pair(mine)


def sum_round(parts):
    total = sum_pair(parts)
    if lax.axis_size("kk") > 1:
        return lax.psum_scatter(total, "kk", scatter_dimension=0, tiled=False)
    return total[0]


def ordered(mine, axis, dim):
    got = swapped(mine, axis)
    is_first = lax.axis_index(axis) == 0
    return jnp.stack([jnp.where(is_first, mine, got), jnp.where(is_first, got, mine)], axis=dim)


def scattered(parts, axis, dim):
    me = lax.axis_index(axis)
    keep = lax.dynamic_index_in_dim(parts, me, dim, keepdims=False)
    give = lax.dynamic_index_in_dim(parts, 1 - me, dim, keepdims=False)
    return (keep.astype(f32) + swapped(give, axis).astype(f32)).astype(bf)


def sorted_places(slots, buckets, own_rows, slot_rows, own_spans):
    heads = lax.axis_size("hd")
    groups = lax.axis_size("kk")
    seq_count = heads * groups
    index_rows = jnp.stack([slots[0], buckets[0]])
    index_all = exchange(jnp.broadcast_to(index_rows[None], (heads,) + index_rows.shape))
    if groups > 1:
        index_all = lax.all_gather(index_all, "kk", axis=1, tiled=False)
    else:
        index_all = index_all[:, None]
    index_all = index_all.reshape(heads, groups, 2, 2, 2, own_rows)
    index_all = jnp.where(lax.axis_index("ry") == 0, index_all, jnp.flip(index_all, 3))
    index_all = jnp.where(lax.axis_index("rc") == 0, index_all, jnp.flip(index_all, 4))
    index_all = jnp.transpose(index_all, (2, 4, 3, 1, 0, 5)).reshape(2, -1)
    slot_row, bucket_row = index_all[0], index_all[1]
    target = slot_row // slot_rows
    local_place = slot_row - target * slot_rows
    onehot = (target[None, :] == jnp.arange(seq_count, dtype=jnp.int32)[:, None]).astype(jnp.int32)
    counts = jnp.sum(onehot, axis=1)
    first_block = lax.axis_index("kk") * heads
    block_ids = jnp.arange(seq_count, dtype=jnp.int32)
    is_own = (block_ids >= first_block) & (block_ids < first_block + heads)
    span_counts = jnp.where(is_own, -(-counts // SPAN), 0)
    shift = (1 + jnp.cumsum(span_counts) - span_counts) * SPAN
    last_start = jnp.maximum(counts - 1, 0) // SPAN * SPAN
    is_halo = block_ids == first_block - 1
    shift = jnp.where(is_halo, -last_start, shift)
    lowest = jnp.where(is_own, 0, jnp.where(is_halo, last_start, slot_rows))
    token_shift = jnp.sum(onehot * shift[:, None], axis=0)
    token_lowest = jnp.sum(onehot * lowest[:, None], axis=0)
    dump = (own_spans + 1) * SPAN
    place = jnp.where(local_place >= token_lowest, local_place + token_shift, dump)
    place_bucket = jnp.full((dump + SPAN,), -1, jnp.int32).at[place].set(bucket_row)
    span_bucket = place_bucket.reshape(-1, SPAN)[: own_spans + 1]
    key_bucket = jnp.concatenate([span_bucket[:-1], span_bucket[1:]], axis=1)
    query_bucket = span_bucket[1:]
    matching = (query_bucket[:, :, None] == key_bucket[:, None, :]) & (key_bucket[:, None, :] >= 0)
    itself = jnp.arange(2 * SPAN)[None, :] == jnp.arange(SPAN)[:, None] + SPAN
    others = matching & jnp.logical_not(itself[None])
    lonely = jnp.logical_not(jnp.any(others, axis=-1, keepdims=True))
    allowed = others | matching & itself[None] & lonely
    bias = jnp.where(allowed, 0.0, MASKED).astype(f32).reshape(own_spans * SPAN, 2 * SPAN)
    return place, bias


def per_device(
    first_half,
    second_half,
    qk_weight,
    value_weight,
    output_weight,
    inner_weight,
    outer_weight,
    attn_gain,
    attn_shift,
    ffn_gain,
    ffn_shift,
    buckets,
    slots,
    first_grad,
    second_grad,
):
    heads = lax.axis_size("hd")
    groups = lax.axis_size("kk")
    seq_count = heads * groups
    round_count = lax.axis_size("ry") * lax.axis_size("rc")
    device_count = seq_count * round_count
    own_rows, model_width = first_half.shape
    weight_rows, hidden_width = inner_weight.shape
    group_rows = own_rows * round_count
    slot_rows = 2 * group_rows
    tokens = group_rows * seq_count
    own_spans = min((tokens + (SPAN - 1) * heads) // SPAN, heads * slot_rows // SPAN)
    own_spans = -(-own_spans // UNROLL) * UNROLL
    piece = hidden_width // device_count
    blocks = own_rows // TOKB

    vectors = jnp.stack([attn_gain, attn_shift, ffn_gain, ffn_shift], axis=1)
    vectors = jnp.pad(vectors, ((0, 0), (0, 124)))
    qkv_shard = jnp.concatenate([qk_weight, value_weight, vectors], axis=1)
    qkv_all = lax.all_gather(qkv_shard, ALL, axis=0, tiled=True)
    qkv_full = qkv_all[:, : 2 * model_width]
    vectors_full = qkv_all[:, 2 * model_width : 2 * model_width + 4].astype(f32).T

    place, bias = sorted_places(slots, buckets, own_rows, slot_rows, own_spans)

    inner_split = inner_weight.reshape(weight_rows, seq_count, round_count, piece)
    inner_split = jnp.transpose(inner_split, (2, 0, 1, 3)).reshape(round_count, weight_rows, -1)
    inner_rows = exchange(inner_split, ROUND).reshape(round_count * weight_rows, -1)
    grad_group = spread_pair(second_grad).reshape(group_rows, model_width)

    first_in = first_half.astype(f32)
    second_in = second_half.astype(f32)
    normed, attn_norm_pull = jax.vjp(layer_norm, second_in, vectors_full[0], vectors_full[1])
    normed_low = normed.astype(bf)
    normed_low, bias, place = lax.optimization_barrier((normed_low, bias, place))
    shard = jnp.concatenate([inner_rows, outer_weight, output_weight, normed_low], axis=0)
    shards = lax.all_gather(shard, SEQ, axis=0, tiled=False)
    cuts = [inner_rows.shape[0], outer_weight.shape[0], weight_rows]
    ends = [cuts[0], cuts[0] + cuts[1], sum(cuts)]
    inner_part_weight = shards[:, : ends[0]].reshape(model_width, -1)
    outer_part_weight = shards[:, ends[0] : ends[1]].reshape(-1, model_width)
    output_full = ordered(ordered(shards[:, ends[1] : ends[2]], "ry", 1), "rc", 2)
    output_full = output_full.reshape(model_width, model_width)
    normed_seq = shards[:, ends[2] :].reshape(heads, groups, own_rows, model_width)
    normed_seq = lax.dynamic_index_in_dim(normed_seq, lax.axis_index("kk"), 1, keepdims=False)
    normed_seq = normed_seq.reshape(heads * own_rows, model_width)

    qkv_own = product(normed_low, qkv_full).astype(bf)
    head_rows = jnp.transpose(qkv_own.reshape(own_rows, 2, heads, HEADD), (2, 0, 1, 3))
    qkv_group = spread_round(exchange(head_rows.reshape(heads, own_rows, 2 * HEADD)))
    payload, sorted_q, sorted_k, sorted_v, probs, token_sums = attend_forward(
        place, qkv_group.reshape(tokens, 2 * HEADD), bias, own_rows
    )
    packed_rows = own_rows + PAD
    packed = (2, 2, groups, heads, packed_rows, HEADD)
    mixed_parts = exchange(sum_round(payload.reshape(packed)))
    d_hidden = through(grad_group, outer_part_weight)
    mixed_parts, d_hidden = lax.optimization_barrier((mixed_parts, d_hidden))
    weight_sum = mixed_parts[:, own_rows : own_rows + blocks].reshape(heads, own_rows)
    mixed_heads = mixed_parts[:, :own_rows].astype(f32) / weight_sum.astype(f32)[..., None]
    mixed_low = jnp.transpose(mixed_heads, (1, 0, 2)).reshape(own_rows, model_width).astype(bf)

    first_sum = first_in + product(mixed_low, output_full)
    ffn_normed, ffn_norm_pull = jax.vjp(layer_norm, first_sum, vectors_full[2], vectors_full[3])
    ffn_group = spread_pair(ffn_normed.astype(bf)).reshape(group_rows, model_width)
    inner_act = product(ffn_group, inner_part_weight)
    hidden, gelu_pull = jax.vjp(exact_gelu, inner_act)
    hidden_low = hidden.astype(bf)
    (inner_back,) = gelu_pull(d_hidden)
    inner_back_low = inner_back.astype(bf)
    pairs = (2, 2, own_rows, model_width)
    ffn_back = through(inner_back_low, inner_part_weight).astype(bf)
    ffn_back = sum_pair(ffn_back.reshape(pairs)).astype(f32)
    second_part = product(hidden_low, outer_part_weight).astype(bf)
    second_sum = second_in + sum_pair(second_part.reshape(pairs)).astype(f32)
    outer_part = against(hidden_low, grad_group).astype(bf).reshape(seq_count, -1, model_width)
    inner_part = against(ffn_group, inner_back_low).astype(bf).reshape(seq_count, cuts[0], -1)
    first_from_ffn, ffn_gain_part, ffn_shift_part = ffn_norm_pull(ffn_back)
    first_carry = first_grad.astype(f32) + first_from_ffn
    carry_low = first_carry.astype(bf)
    output_part = against(mixed_low, carry_low).astype(bf)
    mixed_back = through(carry_low, output_full).reshape(own_rows, heads, HEADD)
    mixed_back = jnp.transpose(mixed_back, (1, 0, 2))
    mixed_dot = jnp.sum(mixed_back * mixed_heads, axis=-1).astype(bf)
    tails = jnp.concatenate(
        [
            mixed_dot.reshape(heads, blocks, TOKB),
            weight_sum.reshape(heads, blocks, TOKB),
            jnp.zeros((heads, PAD - 2 * blocks, TOKB), bf),
        ],
        axis=1,
    )
    back_parts = exchange(jnp.concatenate([mixed_back.astype(bf), tails], axis=1))
    ffn_parts = jnp.concatenate([inner_part, outer_part], axis=1)
    back_parts, ffn_parts, output_part = lax.optimization_barrier(
        (back_parts, ffn_parts, output_part)
    )
    ffn_grads = lax.psum_scatter(ffn_parts, SEQ, scatter_dimension=0, tiled=False)
    inner_cols = ffn_grads[: cuts[0]].reshape(round_count, weight_rows, -1)
    inner_cols = exchange(inner_cols, ROUND)
    inner_cols = inner_cols.reshape(round_count, weight_rows, seq_count, piece)
    inner_grad = jnp.transpose(inner_cols, (1, 2, 0, 3)).reshape(weight_rows, hidden_width)
    outer_grad = ffn_grads[cuts[0] :]

    def rows_of(part):
        part = part.reshape(heads, groups, 2, 2, weight_rows, -1)
        part = scattered(scattered(part, "rc", 3), "ry", 2)
        if groups > 1:
            return lax.psum_scatter(part, "kk", scatter_dimension=1, tiled=False)
        return part[:, 0]

    output_grad = jnp.sum(exchange(rows_of(output_part)).astype(f32), axis=0)

    back_group = spread_round(back_parts).reshape(-1, HEADD)
    query_value_back = attend_backward(
        place, back_group, token_sums, sorted_q, sorted_k, sorted_v, probs, own_rows
    )
    back_shape = (2, 2, groups, heads, own_rows, 2 * HEADD)
    head_back = sum_round(query_value_back.reshape(back_shape))
    qkv_part = against(normed_seq, head_back.reshape(heads * own_rows, 2 * HEADD)).astype(bf)
    qkv_rows = exchange(rows_of(qkv_part)).reshape(heads, weight_rows, 2, HEADD)
    qkv_grad = jnp.transpose(qkv_rows, (2, 1, 0, 3)).reshape(2, weight_rows, model_width)
    own_back = exchange(head_back)
    own_back = jnp.transpose(own_back.reshape(heads, own_rows, 2, HEADD), (1, 2, 0, 3))
    own_back = own_back.reshape(own_rows, 2 * model_width)
    normed_back = through(own_back, qkv_full)
    second_from_attn, attn_gain_part, attn_shift_part = attn_norm_pull(normed_back)
    second_carry = second_grad.astype(f32) + second_from_attn

    vector_parts = jnp.stack([attn_gain_part, attn_shift_part, ffn_gain_part, ffn_shift_part])
    vector_parts = jnp.transpose(vector_parts.reshape(4, device_count, -1), (1, 0, 2))
    vector_rows = exchange(vector_parts.reshape(device_count, -1), ALL)
    vector_grads = jnp.sum(vector_rows, axis=0).reshape(4, -1)
    return (
        first_sum.astype(bf),
        second_sum.astype(bf),
        carry_low,
        second_carry.astype(bf),
        qkv_grad[0].astype(f32),
        qkv_grad[1].astype(f32),
        output_grad,
        inner_grad.astype(f32),
        outer_grad.astype(f32),
        vector_grads[0],
        vector_grads[1],
        vector_grads[2],
        vector_grads[3],
    )


def solution(mesh):
    seq_count, round_count = mesh.devices.shape
    shape = (HEADS, seq_count // HEADS, round_count // 2, 2)
    split_mesh = Mesh(mesh.devices.reshape(shape), ALL)
    rows = P(ALL, None)
    vector = P(ALL)
    table = P(ROUND, SEQ)
    in_specs = (rows,) * 7 + (vector,) * 4 + (table,) * 2 + (rows,) * 2
    out_specs = (rows,) * 9 + (vector,) * 4
    return jax.shard_map(
        per_device, mesh=split_mesh, in_specs=in_specs, out_specs=out_specs, check_vma=False
    )
```

```python
import functools
import math

import jax
import jax.numpy as jnp
from jax import lax
from jax.experimental import pallas as pl
from jax.experimental.pallas import tpu as pltpu
from jax.sharding import Mesh
from jax.sharding import PartitionSpec as P

HEADS = 8
NORM_EPS = 1e-05
SPAN = 64
HEADD = 128
PAD = 16
UNROLL = 17
TOKB = 128
CHUNK = 4096
VMEM_LIMIT = 60 * 2**20
KEY_EPS = 1e-06
bf = jnp.bfloat16
f32 = jnp.float32


def product(left_side, right_side):
    return jnp.dot(left_side, right_side, preferred_element_type=f32)


def against(left_side, right_side):
    return lax.dot_general(
        left_side, right_side, (((0,), (0,)), ((), ())), preferred_element_type=f32
    )


def through(left_side, right_side):
    return lax.dot_general(
        left_side, right_side, (((1,), (1,)), ((), ())), preferred_element_type=f32
    )


def takes(microseconds):
    return pl.CostEstimate(
        flops=int(microseconds * 1e8), bytes_accessed=int(microseconds * 3e6), transcendentals=0
    )


def aligned(start, size, step=SPAN):
    return pl.ds(pl.multiple_of(start, step), size)


def fill(ref, value):
    def body(step, carry):
        ref[aligned(step * SPAN, SPAN), :] = jnp.full((SPAN, ref.shape[1]), value, ref.dtype)
        return carry

    lax.fori_loop(0, ref.shape[0] // SPAN, body, 0)


def diagonal():
    rows = lax.broadcasted_iota(jnp.int32, (TOKB, TOKB), 0)
    return rows == lax.broadcasted_iota(jnp.int32, (TOKB, TOKB), 1)


def chunk_start(table_ref, own_rows, position):
    return table_ref[position // own_rows] * own_rows + position % own_rows


def lanes(row, eye, ones):
    high = row.astype(bf).astype(f32)
    parts = [jnp.where(eye, high, 0.0), jnp.where(eye, row - high, 0.0)]
    return product(jnp.concatenate(parts, axis=1).astype(bf), ones)


def forward_kernel(
    own_rows,
    load_steps,
    in_ref,
    out_ref,
    place_ref,
    bucket_ref,
    own_ref,
    peer_ref,
    pay_own_ref,
    pay_peer_ref,
    query_ref,
    key_ref,
    value_ref,
    prob_ref,
    sum_ref,
    wide_a,
    wide_b,
    stage_a,
    stage_b,
):
    step = pl.program_id(0)
    own_spans = prob_ref.shape[0] // SPAN
    tail = SPAN * (own_spans + 1)

    @pl.when(step == 0)
    def _():
        fill(wide_a, 0.0)
        fill(wide_b, 0.0)

    def scatter_from(token_ref):
        def scatter(block, carry):
            both = token_ref[aligned(block * TOKB, TOKB, TOKB), :].astype(f32)
            stage_a[...] = both[:, :HEADD]
            stage_b[...] = both[:, HEADD:]
            first = chunk_start(in_ref, own_rows, step * CHUNK + block * TOKB)
            for row in range(TOKB):
                place = place_ref[first + row]
                wide_a[pl.ds(place, 1), :] = stage_a[row : row + 1, :]
                wide_b[pl.ds(place, 1), :] = stage_b[row : row + 1, :]
            return carry

        lax.fori_loop(0, CHUNK // TOKB, scatter, 0)

    pl.when(step < load_steps // 2)(lambda: scatter_from(own_ref))
    pl.when((step >= load_steps // 2) & (step < load_steps))(lambda: scatter_from(peer_ref))

    def unit_keys(query):
        square = jnp.sum(query * query, axis=-1, keepdims=True)
        scale = lax.rsqrt(square * (1.0 / HEADD) + KEY_EPS) * HEADD**-0.5
        return (query * scale).astype(bf)

    @pl.when(step == load_steps)
    def _():
        query_ref[:SPAN, :] = wide_a[:SPAN, :].astype(bf)
        key_ref[:SPAN, :] = unit_keys(wide_a[:SPAN, :])
        value_ref[:SPAN, :] = wide_b[:SPAN, :].astype(bf)
        wide_a[:SPAN, :] = jnp.zeros((SPAN, HEADD), f32)
        wide_b[:SPAN, :] = jnp.zeros((SPAN, HEADD), f32)
        for ref in (query_ref, key_ref, value_ref):
            ref[pl.ds(tail, SPAN), :] = jnp.zeros((SPAN, HEADD), bf)
        ones = jnp.ones((2 * SPAN, HEADD), bf)
        row_ids = lax.broadcasted_iota(jnp.int32, (SPAN, 2 * SPAN), 0)
        lane_ids = lax.broadcasted_iota(jnp.int32, (SPAN, 2 * SPAN), 1)
        before, itself = lane_ids == row_ids, lane_ids == row_ids + SPAN

        def spans(group, carry):
            first = group * (UNROLL * SPAN)
            prev = aligned(first, SPAN)
            here = aligned(first + SPAN, UNROLL * SPAN)
            query_wide = wide_a[here, :]
            values = wide_b[here, :].astype(bf)
            keys = jnp.concatenate([key_ref[prev, :], unit_keys(query_wide)], axis=0)
            seen = jnp.concatenate([value_ref[prev, :], values], axis=0)
            query = query_wide.astype(bf)
            key_buckets, columns = [], []
            for span in range(UNROLL):
                row = bucket_ref[pl.ds(group * UNROLL + span, 1), :]
                high = row.astype(bf).astype(f32)
                low = pltpu.roll(row - high, SPAN, 1)
                key_buckets.append(row)
                columns.append(jnp.where(itself, high, jnp.where(before, low, 0.0)).astype(bf))
            columns = product(jnp.concatenate(columns, axis=0), ones)
            raised = []
            for span in range(UNROLL):
                mine = slice(span * SPAN, (span + 1) * SPAN)
                both = slice(span * SPAN, (span + 2) * SPAN)
                same = columns[mine] == key_buckets[span]
                matches = jnp.sum(jnp.where(same, 1.0, 0.0), axis=-1, keepdims=True)
                allowed = same & (jnp.logical_not(itself) | (matches < 1.5))
                scores = through(query[mine], keys[both])
                raised.append(jnp.where(allowed, jnp.exp(scores), 0.0))
            lows = [member.astype(bf) for member in raised]
            totals = product(jnp.concatenate(lows, axis=0), ones)
            results = []
            for span in range(UNROLL):
                mine = slice(span * SPAN, (span + 1) * SPAN)
                both = slice(span * SPAN, (span + 2) * SPAN)
                total = totals[mine]
                inverse = jnp.where(total > 0.0, 1.0 / total, 0.0)
                probs = (raised[span] * inverse).astype(bf)
                results.append((product(lows[span], seen[both]), total, probs))
            query_ref[here, :] = query
            key_ref[here, :] = keys[SPAN:]
            value_ref[here, :] = values
            for span, (weighted, total, probs) in enumerate(results):
                at = aligned(first + (span + 1) * SPAN, SPAN)
                wide_a[at, :] = weighted
                wide_b[at, :] = total
                prob_ref[aligned(first + span * SPAN, SPAN), :] = probs
            return carry

        lax.fori_loop(0, own_spans // UNROLL, spans, 0)
        wide_a[pl.ds(tail, SPAN), :] = jnp.zeros((SPAN, HEADD), f32)
        wide_b[pl.ds(tail, SPAN), :] = jnp.zeros((SPAN, HEADD), f32)

    def collect_to(pay_ref):
        blocks = own_rows // TOKB
        per_step = CHUNK // own_rows
        eye = diagonal()
        sum_rows = lax.broadcasted_iota(jnp.int32, (PAD, TOKB), 0)
        offset = (step - load_steps - 1) * CHUNK

        def collect(chunk, carry):
            first = chunk * (own_rows + PAD)
            sums = jnp.zeros((PAD, TOKB), f32)
            for block in range(blocks):
                start = chunk_start(out_ref, own_rows, offset + chunk * own_rows + block * TOKB)
                for row in range(TOKB):
                    place = place_ref[start + row]
                    stage_a[row : row + 1, :] = wide_a[pl.ds(place, 1), :]
                    stage_b[row : row + 1, :] = wide_b[pl.ds(place, 1), :]
                pay_ref[aligned(first + block * TOKB, TOKB, PAD), :] = stage_a[...].astype(bf)
                packed = jnp.sum(jnp.where(eye, stage_b[...], 0.0), axis=0, keepdims=True)
                sum_ref[pl.ds(chunk * blocks + block, 1), :] = packed
                sums = jnp.where(sum_rows == block, packed, sums)
            pay_ref[aligned(first + own_rows, PAD, PAD), :] = sums.astype(bf)
            return carry

        lax.fori_loop(0, per_step, collect, 0)

    half = load_steps + 1 + load_steps // 2
    pl.when((step > load_steps) & (step < half))(lambda: collect_to(pay_own_ref))
    pl.when(step >= half)(lambda: collect_to(pay_peer_ref))


def part_spec(shape, first, count):
    return pl.BlockSpec(shape, lambda step: (jnp.clip(step - first, 0, count - 1), 0))


def attend_forward(in_table, out_table, place, key_bucket, own, peer, own_rows):
    tokens = place.shape[0]
    steps = tokens // CHUNK
    half = steps // 2
    own_spans = key_bucket.shape[0]
    rows = SPAN * (own_spans + 2)
    pay_rows = CHUNK // own_rows * (own_rows + PAD)
    once = pl.Buffered(1)

    def whole(shape):
        return pl.BlockSpec(shape, lambda step: (0, 0), pipeline_mode=once)

    sorted_rows = jax.ShapeDtypeStruct((rows, HEADD), bf)
    return pl.pallas_call(
        functools.partial(forward_kernel, own_rows, steps),
        grid=(2 * steps + 1,),
        out_shape=(
            jax.ShapeDtypeStruct((half * pay_rows, HEADD), bf),
            jax.ShapeDtypeStruct((half * pay_rows, HEADD), bf),
            sorted_rows,
            sorted_rows,
            sorted_rows,
            jax.ShapeDtypeStruct((own_spans * SPAN, 2 * SPAN), bf),
            jax.ShapeDtypeStruct((tokens // TOKB, TOKB), f32),
        ),
        in_specs=[
            pl.BlockSpec(memory_space=pltpu.SMEM),
            pl.BlockSpec(memory_space=pltpu.SMEM),
            pl.BlockSpec(memory_space=pltpu.SMEM),
            whole(key_bucket.shape),
            part_spec((CHUNK, 2 * HEADD), 0, half),
            part_spec((CHUNK, 2 * HEADD), half, half),
        ],
        out_specs=(
            part_spec((pay_rows, HEADD), steps + 1, half),
            part_spec((pay_rows, HEADD), steps + 1 + half, half),
            whole((rows, HEADD)),
            whole((rows, HEADD)),
            whole((rows, HEADD)),
            whole((own_spans * SPAN, 2 * SPAN)),
            part_spec((CHUNK // TOKB, TOKB), steps + 1, steps),
        ),
        scratch_shapes=[pltpu.VMEM((rows, HEADD), f32)] * 2 + [pltpu.VMEM((TOKB, HEADD), f32)] * 2,
        compiler_params=pltpu.CompilerParams(vmem_limit_bytes=VMEM_LIMIT),
        name="attend_forward",
        cost_estimate=takes(35),
    )(in_table, out_table, place, key_bucket, own, peer)


def backward_kernel(
    own_rows,
    load_steps,
    table_ref,
    place_ref,
    pay_own_ref,
    pay_peer_ref,
    sum_ref,
    query_ref,
    key_ref,
    value_ref,
    prob_ref,
    out_own_ref,
    out_peer_ref,
    wide_a,
    wide_b,
    wide_c,
    stage_a,
    stage_b,
):
    step = pl.program_id(0)
    own_spans = prob_ref.shape[0] // SPAN
    tail = SPAN * (own_spans + 1)

    @pl.when(step == 0)
    def _():
        fill(wide_a, 0.0)
        fill(wide_b, 0.0)

    def scatter_from(pay_ref):
        blocks = own_rows // TOKB
        eye = diagonal()
        ones = jnp.ones((2 * TOKB, TOKB), bf)

        def scatter(chunk, carry):
            first = chunk * (own_rows + PAD)
            extra = pay_ref[aligned(first + own_rows, PAD, PAD), :].astype(f32)
            for block in range(blocks):
                share = sum_ref[pl.ds(chunk * blocks + block, 1), :]
                share = share / extra[blocks + block : blocks + block + 1, :]
                rows = pay_ref[aligned(first + block * TOKB, TOKB, PAD), :].astype(f32)
                stage_a[...] = rows * lanes(share, eye, ones)
                stage_b[...] = lanes(share * extra[block : block + 1, :], eye, ones)
                start = step * CHUNK + chunk * own_rows + block * TOKB
                start = chunk_start(table_ref, own_rows, start)
                for row in range(TOKB):
                    place = place_ref[start + row]
                    wide_a[pl.ds(place, 1), :] = stage_a[row : row + 1, :]
                    wide_b[pl.ds(place, 1), :] = stage_b[row : row + 1, :]
            return carry

        lax.fori_loop(0, CHUNK // own_rows, scatter, 0)

    pl.when(step < load_steps // 2)(lambda: scatter_from(pay_own_ref))
    pl.when((step >= load_steps // 2) & (step < load_steps))(lambda: scatter_from(pay_peer_ref))

    def pulled(query_low, d_query, d_keys):
        query = query_low.astype(f32)
        inverse = lax.rsqrt(
            jnp.sum(query * query, axis=-1, keepdims=True) * (1.0 / HEADD) + KEY_EPS
        )
        along = jnp.sum(query * d_keys, axis=-1, keepdims=True)
        scale = inverse * HEADD**-0.5
        return d_query + scale * d_keys - (scale * inverse * inverse * along * (1.0 / HEADD)) * query

    @pl.when(step == load_steps)
    def _():
        for ref in (wide_a, wide_b, wide_c):
            ref[:SPAN, :] = jnp.zeros((SPAN, HEADD), f32)
        zero = jnp.zeros((SPAN, HEADD), bf)

        def spans(group, carry):
            first = group * (UNROLL * SPAN)
            prev = aligned(first, SPAN)
            own = aligned(first, UNROLL * SPAN)
            here = aligned(first + SPAN, UNROLL * SPAN)
            around = aligned(first, (UNROLL + 1) * SPAN)
            query = query_ref[around, :]
            keys = key_ref[around, :]
            values = value_ref[around, :]
            probs = prob_ref[own, :]
            d_out = wide_a[here, :].astype(bf)
            delta = wide_b[here, :]
            d_query = [wide_a[prev, :]]
            d_keys = [wide_b[prev, :]]
            d_values = [wide_c[prev, :]]
            for span in range(UNROLL):
                mine = slice(span * SPAN, (span + 1) * SPAN)
                after = slice((span + 1) * SPAN, (span + 2) * SPAN)
                both = slice(span * SPAN, (span + 2) * SPAN)
                d_probs = through(d_out[mine], values[both])
                prob = probs[mine]
                d_scores = (prob.astype(f32) * (d_probs - delta[mine])).astype(bf)
                d_query.append(product(d_scores, keys[both]))
                right = jnp.concatenate(
                    [
                        jnp.concatenate([query[after], zero], axis=1),
                        jnp.concatenate([zero, d_out[mine]], axis=1),
                    ],
                    axis=0,
                )
                pair = against(jnp.concatenate([d_scores, prob], axis=0), right)
                d_keys[-1] = d_keys[-1] + pair[:SPAN, :HEADD]
                d_values[-1] = d_values[-1] + pair[:SPAN, HEADD:]
                d_keys.append(pair[SPAN:, :HEADD])
                d_values.append(pair[SPAN:, HEADD:])
            for span in range(UNROLL + 1):
                at = aligned(first + span * SPAN, SPAN)
                wide_c[at, :] = d_values[span]
                if span < UNROLL:
                    rows = slice(span * SPAN, (span + 1) * SPAN)
                    wide_a[at, :] = pulled(query[rows], d_query[span], d_keys[span])
                else:
                    wide_a[at, :] = d_query[span]
                    wide_b[at, :] = d_keys[span]
            return carry

        lax.fori_loop(0, own_spans // UNROLL, spans, 0)
        last = pl.ds(tail - SPAN, SPAN)
        wide_a[last, :] = pulled(query_ref[last, :], wide_a[last, :], wide_b[last, :])
        wide_a[pl.ds(tail, SPAN), :] = jnp.zeros((SPAN, HEADD), f32)
        wide_c[pl.ds(tail, SPAN), :] = jnp.zeros((SPAN, HEADD), f32)

    def collect_to(out_ref):
        offset = (step - load_steps - 1) * CHUNK

        def collect(block, carry):
            start = chunk_start(table_ref, own_rows, offset + block * TOKB)
            for row in range(TOKB):
                place = place_ref[start + row]
                stage_a[row : row + 1, :] = wide_a[pl.ds(place, 1), :]
                stage_b[row : row + 1, :] = wide_c[pl.ds(place, 1), :]
            here = aligned(block * TOKB, TOKB, TOKB)
            out_ref[here, :HEADD] = stage_a[...].astype(bf)
            out_ref[here, HEADD:] = stage_b[...].astype(bf)
            return carry

        lax.fori_loop(0, CHUNK // TOKB, collect, 0)

    half = load_steps + 1 + load_steps // 2
    pl.when((step > load_steps) & (step < half))(lambda: collect_to(out_own_ref))
    pl.when(step >= half)(lambda: collect_to(out_peer_ref))


def attend_backward(out_table, place, pay_own, pay_peer, sums, query, keys, values, probs, own_rows):
    tokens = place.shape[0]
    steps = tokens // CHUNK
    half = steps // 2
    rows = query.shape[0]
    pay_rows = CHUNK // own_rows * (own_rows + PAD)
    once = pl.Buffered(1)

    def whole(shape):
        return pl.BlockSpec(shape, lambda step: (0, 0), pipeline_mode=once)

    out_half = jax.ShapeDtypeStruct((tokens // 2, 2 * HEADD), bf)
    return pl.pallas_call(
        functools.partial(backward_kernel, own_rows, steps),
        grid=(2 * steps + 1,),
        out_shape=(out_half, out_half),
        in_specs=[
            pl.BlockSpec(memory_space=pltpu.SMEM),
            pl.BlockSpec(memory_space=pltpu.SMEM),
            part_spec((pay_rows, HEADD), 0, half),
            part_spec((pay_rows, HEADD), half, half),
            part_spec((CHUNK // TOKB, TOKB), 0, steps),
            whole((rows, HEADD)),
            whole((rows, HEADD)),
            whole((rows, HEADD)),
            whole(probs.shape),
        ],
        out_specs=(
            part_spec((CHUNK, 2 * HEADD), steps + 1, half),
            part_spec((CHUNK, 2 * HEADD), steps + 1 + half, half),
        ),
        scratch_shapes=[pltpu.VMEM((rows, HEADD), f32)] * 3 + [pltpu.VMEM((TOKB, HEADD), f32)] * 2,
        compiler_params=pltpu.CompilerParams(vmem_limit_bytes=VMEM_LIMIT),
        name="attend_backward",
        cost_estimate=takes(44),
    )(out_table, place, pay_own, pay_peer, sums, query, keys, values, probs)


def shard_spec(shards, number):
    block = (shards.shape[0], 1) + shards.shape[2:]
    return pl.BlockSpec(block, lambda *_: (0, number, 0, 0), pipeline_mode=pl.Buffered(1))


def whole_weight(ref):
    value = ref[...]
    return value.reshape(-1, value.shape[-1])


def feed_kernel(
    own_ref, peer_ref, grad_own_ref, grad_peer_ref, inner_weight_ref, outer_weight_ref,
    row_ref, grad_ref, hidden_ref, inner_ref,
    back_own_ref, back_peer_ref, second_own_ref, second_peer_ref,
):
    step = pl.program_id(0)

    @pl.when(step == 0)
    def _():
        row_ref[...] = own_ref[...]
        grad_ref[...] = grad_own_ref[...]

    @pl.when(step == 1)
    def _():
        row_ref[...] = peer_ref[...]
        grad_ref[...] = grad_peer_ref[...]

    weight = whole_weight(inner_weight_ref)
    outer_weight = whole_weight(outer_weight_ref)
    act = product(row_ref[...], weight)
    size = jnp.abs(act)
    bell = jnp.exp(act * act * -0.5)
    near = 1.0 / (1.0 + size * (0.3275911 * 0.5**0.5))
    tail = near * (0.254829592 + near * (-0.284496736 + near * (
        1.421413741 + near * (-1.453152027 + near * 1.061405429))))
    tail = tail * bell * 0.5
    normal = jnp.where(act >= 0.0, 1.0 - tail, tail)
    hidden = (act * normal).astype(bf)
    hidden_ref[...] = hidden
    slope = normal + act * bell * (2.0 * math.pi) ** -0.5
    inner = (through(grad_ref[...], outer_weight) * slope).astype(bf)
    inner_ref[...] = inner
    back = through(inner, weight).astype(bf)
    second = product(hidden, outer_weight).astype(bf)

    @pl.when(step == 0)
    def _():
        back_own_ref[...] = back
        second_own_ref[...] = second

    @pl.when(step == 1)
    def _():
        back_peer_ref[...] = back
        second_peer_ref[...] = second


def feed_forward(own, peer, grad_own, grad_peer, shards):
    count, width = own.shape
    units = shards.shape[3]

    def part(columns):
        return pl.BlockSpec((count, columns), lambda i: (i, 0))

    whole = pl.BlockSpec((count, width), lambda i: (0, 0), pipeline_mode=pl.Buffered(1))
    by_width = jax.ShapeDtypeStruct((2 * count, width), bf)
    by_units = jax.ShapeDtypeStruct((2 * count, units), bf)
    half = jax.ShapeDtypeStruct((count, width), bf)
    return pl.pallas_call(
        feed_kernel,
        grid=(2,),
        out_shape=(by_width, by_width, by_units, by_units, half, half, half, half),
        in_specs=[whole] * 4 + [shard_spec(shards, 0), shard_spec(shards, 1)],
        out_specs=(
            part(width), part(width), part(units), part(units), whole, whole, whole, whole
        ),
        compiler_params=pltpu.CompilerParams(vmem_limit_bytes=VMEM_LIMIT),
        name="feed_forward",
        cost_estimate=takes(9),
    )(own, peer, grad_own, grad_peer, shards, shards)


def mix_kernel(
    parts_ref, weight_ref, first_ref, gain_ref, shift_ref,
    mixed_ref, low_ref, sum_ref, unit_ref, scale_ref, feed_ref,
):
    heads, rows = parts_ref.shape[0], first_ref.shape[0]
    eye = diagonal()
    ones = jnp.ones((2 * TOKB, TOKB), bf)
    for head in range(heads):
        columns = slice(head * HEADD, (head + 1) * HEADD)
        for block in range(rows // TOKB):
            here = slice(block * TOKB, (block + 1) * TOKB)
            sums = parts_ref[head, rows : rows + PAD, :].astype(f32)[block : block + 1]
            mixed = parts_ref[head, here, :].astype(f32) / lanes(sums, eye, ones)
            mixed_ref[here, columns] = mixed
            low_ref[here, columns] = mixed.astype(bf)
    total = first_ref[...].astype(f32) + product(low_ref[...], whole_weight(weight_ref))
    sum_ref[...] = total.astype(bf)
    centre = total - jnp.mean(total, axis=-1, keepdims=True)
    scale = lax.rsqrt(jnp.mean(centre * centre, axis=-1, keepdims=True) + NORM_EPS)
    unit = centre * scale
    unit_ref[...] = unit
    scale_ref[...] = scale
    feed_ref[...] = (unit * gain_ref[...] + shift_ref[...]).astype(bf)


def mix_rows(parts, shards, first_half, gain, shift):
    rows, width = first_half.shape
    vm = pl.BlockSpec(memory_space=pltpu.VMEM)
    wide, low = jax.ShapeDtypeStruct((rows, width), f32), jax.ShapeDtypeStruct((rows, width), bf)
    return pl.pallas_call(
        mix_kernel,
        out_shape=(wide, low, low, wide, jax.ShapeDtypeStruct((rows, 1), f32), low),
        grid=(1,),
        in_specs=[vm, shard_spec(shards, 2), vm, vm, vm],
        out_specs=(vm,) * 6,
        compiler_params=pltpu.CompilerParams(vmem_limit_bytes=VMEM_LIMIT),
        name="mix_rows",
        cost_estimate=takes(5),
    )(parts, shards, first_half, gain, shift)


def carry_kernel(
    near_ref, far_ref, gain_ref, unit_ref, scale_ref, grad_ref, weight_ref, mixed_ref, parts_ref,
    carry_ref, pay_ref, wide_ref,
):
    heads, rows = parts_ref.shape[0], grad_ref.shape[0]
    blocks = rows // TOKB
    back = near_ref[...].astype(f32) + far_ref[...].astype(f32)
    unit = unit_ref[...]
    gain_sum = jnp.sum(back * unit, axis=0, keepdims=True)
    shift_sum = jnp.sum(back, axis=0, keepdims=True)
    grad = back * gain_ref[...]
    along = jnp.mean(grad * unit, axis=-1, keepdims=True)
    grad = scale_ref[...] * (grad - jnp.mean(grad, axis=-1, keepdims=True) - unit * along)
    carry_ref[...] = (grad_ref[...].astype(f32) + grad).astype(bf)
    wide_ref[...] = through(carry_ref[...], whole_weight(weight_ref))
    eye = diagonal()
    pad_rows = lax.broadcasted_iota(jnp.int32, (PAD, TOKB), 0)
    for head in range(heads):
        columns = slice(head * HEADD, (head + 1) * HEADD)
        sums = parts_ref[head, rows : rows + PAD, :].astype(f32)
        tails = jnp.zeros((PAD, TOKB), f32)
        for block in range(blocks):
            here = slice(block * TOKB, (block + 1) * TOKB)
            wide = wide_ref[here, columns]
            pay_ref[head, here, :] = wide.astype(bf)
            dot = jnp.sum(wide * mixed_ref[here, columns], axis=-1, keepdims=True)
            packed = jnp.sum(jnp.where(eye, dot, 0.0), axis=0, keepdims=True)
            tails = jnp.where(pad_rows == block, packed, tails)
            tails = jnp.where(pad_rows == blocks + block, sums[block : block + 1], tails)
        tails = jnp.where(pad_rows == 2 * blocks, gain_sum[:, columns], tails)
        tails = jnp.where(pad_rows == 2 * blocks + 1, shift_sum[:, columns], tails)
        pay_ref[head, rows : rows + PAD, :] = tails.astype(bf)


def carry_rows(near, far, gain, unit, scale, first_grad, shards, mixed, parts):
    rows, width = near.shape
    vm = pl.BlockSpec(memory_space=pltpu.VMEM)
    return pl.pallas_call(
        carry_kernel,
        out_shape=(
            jax.ShapeDtypeStruct((rows, width), bf),
            jax.ShapeDtypeStruct(parts.shape, bf),
        ),
        grid=(1,),
        in_specs=[vm] * 6 + [shard_spec(shards, 2)] + [vm] * 2,
        out_specs=(vm,) * 2,
        scratch_shapes=[pltpu.VMEM((rows, width), f32)],
        compiler_params=pltpu.CompilerParams(vmem_limit_bytes=VMEM_LIMIT),
        name="carry_rows",
        cost_estimate=takes(5),
    )(near, far, gain, unit, scale, first_grad, shards, mixed, parts)


def add_kernel(left_ref, right_ref, out_ref):
    total = left_ref[...].astype(f32) + right_ref[...].astype(f32)
    out_ref[...] = total.astype(out_ref.dtype)


def add_rows(left, right):
    shape = left.shape
    left, right = left.reshape(-1, shape[-1]), right.reshape(-1, shape[-1])
    step = math.gcd(left.shape[0], 1024)
    spec = pl.BlockSpec((step, shape[-1]), lambda i: (i, 0))
    out = pl.pallas_call(
        add_kernel,
        grid=(left.shape[0] // step,),
        out_shape=jax.ShapeDtypeStruct(left.shape, left.dtype),
        in_specs=[spec, spec],
        out_specs=spec,
        name="add_rows",
        cost_estimate=takes(3),
    )(left, right)
    return out.reshape(shape)


def last_kernel(
    back_ref, weight_ref, gain_ref, unit_ref, scale_ref, grad_ref, out_ref, query_ref, value_ref,
):
    for head in range(back_ref.shape[0]):
        columns = slice(head * HEADD, (head + 1) * HEADD)
        query_ref[:, columns] = back_ref[head, :, :HEADD]
        value_ref[:, columns] = back_ref[head, :, HEADD:]
    total = through(query_ref[...], weight_ref[0]) + through(value_ref[...], weight_ref[1])
    grad = total * gain_ref[...]
    unit = unit_ref[...]
    along = jnp.mean(grad * unit, axis=-1, keepdims=True)
    centred = grad - jnp.mean(grad, axis=-1, keepdims=True) - unit * along
    out_ref[...] = (grad_ref[...].astype(f32) + scale_ref[...] * centred).astype(bf)


def last_rows(own_back, weights, gain, unit, scale, second_grad):
    rows, width = unit.shape
    vm = pl.BlockSpec(memory_space=pltpu.VMEM)
    return pl.pallas_call(
        last_kernel,
        out_shape=jax.ShapeDtypeStruct((rows, width), bf),
        in_specs=[vm] * 6,
        out_specs=vm,
        scratch_shapes=[pltpu.VMEM((rows, width), bf)] * 2,
        compiler_params=pltpu.CompilerParams(vmem_limit_bytes=VMEM_LIMIT),
        name="last_rows",
        cost_estimate=takes(6),
    )(own_back, weights, gain, unit, scale, second_grad)


def weight_kernel(order_ref, back_ref, *refs):
    pieces, (part_ref, column_ref) = refs[:-2], refs[-2:]
    half = pieces[-1].shape[0]
    total = None
    for number, piece in enumerate(pieces[:-1]):
        back = back_ref[order_ref[number]]
        if piece.shape[0] == half:
            term = against(piece[...], back[:half]) + against(pieces[-1][...], back[half:])
        else:
            term = against(piece[...], back)
        total = term if total is None else total + term
    part_ref[...] = total
    columns = jnp.sum(back_ref[...].astype(f32), axis=(0, 1), keepdims=True)[0]
    column_ref[...] = jnp.broadcast_to(columns, column_ref.shape)


def weight_part(order, back, pieces):
    width = pieces[0].shape[1]
    vm = pl.BlockSpec(memory_space=pltpu.VMEM)
    return pl.pallas_call(
        weight_kernel,
        out_shape=(
            jax.ShapeDtypeStruct((width, back.shape[2]), f32),
            jax.ShapeDtypeStruct((8, back.shape[2]), f32),
        ),
        in_specs=[pl.BlockSpec(memory_space=pltpu.SMEM)] + [vm] * (1 + len(pieces)),
        out_specs=(vm, vm),
        compiler_params=pltpu.CompilerParams(vmem_limit_bytes=VMEM_LIMIT),
        name="weight_part",
        cost_estimate=takes(5),
    )(order, back, *pieces)


ALL = ("hd", "kk", "ry", "rc")
SEQ = ("hd", "kk")
ROUND = ("ry", "rc")
SWAP = [(0, 1), (1, 0)]
RING = (0, 2, 4, 6, 7, 5, 3, 1)
UP = [(RING[i], RING[(i + 1) % HEADS]) for i in range(HEADS)]
DOWN = [(RING[(i + 1) % HEADS], RING[i]) for i in range(HEADS)]
STEPS = ((0, -1, 1, -2, 2), (-3, 3, 4))
BUCKETS = 32


def normalised(values):
    centre = values - jnp.mean(values, axis=-1, keepdims=True)
    spread = jnp.mean(centre * centre, axis=-1, keepdims=True)
    inverse = lax.rsqrt(spread + NORM_EPS)
    return centre * inverse, inverse


def norm_back(unit, inverse, grad):
    along = jnp.mean(grad * unit, axis=-1, keepdims=True)
    return inverse * (grad - jnp.mean(grad, axis=-1, keepdims=True) - unit * along)


def together(*values):
    return lax.optimization_barrier(values)


def exchange(parts, axes="hd"):
    return lax.all_to_all(parts, axes, split_axis=0, concat_axis=0, tiled=True)


def swapped(value, axis):
    return lax.ppermute(value, axis, SWAP)


def over_groups(mine):
    if lax.axis_size("kk") > 1:
        return lax.all_gather(mine, "kk", axis=0, tiled=False)
    return mine[None]


def sum_groups(parts):
    if lax.axis_size("kk") > 1:
        return lax.psum_scatter(parts, "kk", scatter_dimension=0, tiled=False)
    return parts[0]


def pair_sum(keep, give, axis):
    return (keep.astype(f32) + swapped(give, axis).astype(f32)).astype(bf)


def spread_pair(mine):
    pair = jnp.stack([mine, swapped(mine, "ry")])
    return pair, swapped(pair, "rc")


def chip_pair(mine):
    return jnp.concatenate([mine, swapped(mine, "rc")], axis=0)


def sum_pair(own, peer):
    total = pair_sum(own, peer, "rc")
    return pair_sum(total[0], total[1], "ry")


def ordered(mine, axis, dim):
    return pair_order(mine, swapped(mine, axis), axis, dim)


def pair_order(mine, got, axis, dim):
    is_first = lax.axis_index(axis) == 0
    return jnp.stack([jnp.where(is_first, mine, got), jnp.where(is_first, got, mine)], axis=dim)


def scattered(parts, axis, dim):
    me = lax.axis_index(axis)
    keep = lax.dynamic_index_in_dim(parts, me, dim, keepdims=False)
    give = lax.dynamic_index_in_dim(parts, 1 - me, dim, keepdims=False)
    return pair_sum(keep, give, axis)


def ring_step(up, down):
    return lax.ppermute(up, "hd", UP), lax.ppermute(down, "hd", DOWN)


def ring_order():
    position = jnp.array([RING.index(i) for i in range(HEADS)], jnp.int32)[lax.axis_index("hd")]
    offsets = jnp.array([o for step in STEPS for o in step], jnp.int32)
    return jnp.array(RING, jnp.int32)[(position + offsets) % HEADS]


def wide_scattered(parts, axis, dim):
    me = lax.axis_index(axis)
    keep = lax.dynamic_index_in_dim(parts, me, dim, keepdims=False)
    return keep + swapped(lax.dynamic_index_in_dim(parts, 1 - me, dim, keepdims=False), axis)


def traded(parts, axis, dim):
    me = lax.axis_index(axis)
    got = swapped(lax.dynamic_index_in_dim(parts, 1 - me, dim, keepdims=True), axis)
    return lax.dynamic_update_slice_in_dim(parts, got, 1 - me, dim)


def index_codes(slots, buckets, slot_rows):
    first_bucket = slots // slot_rows * BUCKETS
    return jnp.concatenate([slots // 256, slots % 256, buckets - first_bucket]).astype(bf)


def sorted_layout(codes, slot_rows, own_spans):
    heads = lax.axis_size("hd")
    codes = codes.astype(jnp.int32)
    slot_grid = codes[:, :, 0] * 256 + codes[:, :, 1]
    before = lax.axis_index("kk") * heads - 1
    target = slot_grid // slot_rows
    block = target - before
    local_place = slot_grid - target * slot_rows
    category = (block * (BUCKETS + 1) + codes[:, :, 2]).reshape(1, -1)
    categories = jnp.arange((heads + 1) * (BUCKETS + 1), dtype=jnp.int32)[:, None]
    members = jnp.sum((category == categories).astype(jnp.int32), axis=1)
    members = members.reshape(heads + 1, BUCKETS + 1)
    counts = jnp.sum(members, axis=1)
    last_start = jnp.maximum(counts[:1] - 1, 0) // SPAN * SPAN
    span_counts = -(-counts[1:] // SPAN)
    own_start = (1 + jnp.cumsum(span_counts) - span_counts) * SPAN
    start = jnp.concatenate([-last_start, own_start])
    lowest = jnp.concatenate([last_start, jnp.zeros_like(own_start)])
    dump = (own_spans + 1) * SPAN
    numbers = jnp.arange(heads + 1, dtype=jnp.int32)[:, None]
    local_place, block = local_place.reshape(1, -1), block.reshape(1, -1)
    here = (block == numbers) & (local_place >= lowest[:, None])
    place = jnp.sum(jnp.where(here, local_place + start[:, None] - dump, 0), axis=0) + dump
    ends = (start[:, None] + jnp.cumsum(members, axis=1)).reshape(-1, 1)
    rows = jnp.arange(dump, dtype=jnp.int32)[None, :]
    passed = jnp.sum((ends <= rows).astype(jnp.int32), axis=0)
    row_block = jnp.sum((own_start[:, None] <= rows).astype(jnp.int32), axis=0)
    local_bucket = passed - row_block * (BUCKETS + 1)
    row_bucket = jnp.where(
        local_bucket <= BUCKETS, (before + row_block) * BUCKETS + local_bucket, -1
    )
    span_bucket = row_bucket.astype(f32).reshape(-1, SPAN)
    return place, jnp.concatenate([span_bucket[:-1], span_bucket[1:]], axis=1)


def chunk_tables(groups):
    order = ring_order()
    flip = jnp.stack([lax.axis_index("rc"), lax.axis_index("ry")])

    def number(dc, dy, kk, hd):
        return ((hd * groups + kk) * 2 + (dy ^ flip[1])) * 2 + (dc ^ flip[0])

    def column(values):
        return jnp.array(values, jnp.int32)

    offsets = [list(range(sum(map(len, STEPS[:i])), sum(map(len, STEPS[: i + 1])))) for i in range(len(STEPS))]
    coming = [
        (dc, dy, kk, at)
        for dc in range(2)
        for part in offsets
        for dy in range(2)
        for kk in range(groups)
        for at in part
    ]
    going = [
        (dc, dy, kk, hd)
        for dc in range(2)
        for dy in range(2)
        for kk in range(groups)
        for hd in range(HEADS)
    ]
    dc, dy, kk, at = map(column, zip(*coming))
    in_table = number(dc, dy, kk, order[at])
    return in_table, number(*map(column, zip(*going)))


def per_device(
    first_half,
    second_half,
    qk_weight,
    value_weight,
    output_weight,
    inner_weight,
    outer_weight,
    attn_gain,
    attn_shift,
    ffn_gain,
    ffn_shift,
    buckets,
    slots,
    first_grad,
    second_grad,
):
    heads = lax.axis_size("hd")
    groups = lax.axis_size("kk")
    seq_count = heads * groups
    round_count = lax.axis_size("ry") * lax.axis_size("rc")
    device_count = seq_count * round_count
    own_rows, model_width = first_half.shape
    weight_rows, hidden_width = inner_weight.shape
    group_rows = own_rows * round_count
    slot_rows = 2 * group_rows
    tokens = group_rows * seq_count
    own_spans = min((tokens + (SPAN - 1) * heads) // SPAN, heads * slot_rows // SPAN)
    own_spans = -(-own_spans // UNROLL) * UNROLL
    piece = hidden_width // device_count
    blocks = own_rows // TOKB
    both = 2 * HEADD

    second_in = second_half.astype(f32)
    unit, unit_scale = normalised(second_in)
    unit_low = unit.astype(bf)
    vectors = jnp.stack([attn_gain, attn_shift, ffn_gain, ffn_shift], axis=1)
    vectors = jnp.pad(vectors, ((0, 0), (0, HEADD - 4)))
    wide = both + HEADD
    head_shard = jnp.concatenate(
        [
            qk_weight.reshape(weight_rows, heads, HEADD),
            value_weight.reshape(weight_rows, heads, HEADD),
            jnp.broadcast_to(vectors[:, None], (weight_rows, heads, HEADD)),
        ],
        axis=2,
    )
    code_rows = 3 * group_rows // wide
    codes = index_codes(slots, buckets, slot_rows).reshape(code_rows, wide)
    codes = jnp.pad(codes, ((0, -code_rows % PAD), (0, 0)))
    codes = jnp.broadcast_to(codes[None], (heads,) + codes.shape)
    starter = jnp.concatenate([jnp.transpose(head_shard, (1, 0, 2)), codes], axis=1)

    inner_split = inner_weight.reshape(weight_rows, seq_count, round_count, piece)
    inner_split = jnp.transpose(inner_split, (2, 0, 1, 3)).reshape(2, 2, weight_rows, -1)
    unit_low, starter = together(unit_low, starter)
    ring = [(unit_low,)]
    up, down = ring_step(unit_low, unit_low)
    up, down, starter, inner_split = together(up, down, exchange(starter), inner_split)
    ring.append((up, down))

    up, down = ring_step(up, down)
    starter = jnp.transpose(over_groups(starter), (1, 0, 2, 3))
    codes = starter[:, :, weight_rows : weight_rows + code_rows].reshape(heads, groups, 3, -1)
    head_weight = ordered(ordered(starter[:, :, :weight_rows], "ry", 2), "rc", 3)
    head_weight = head_weight.reshape(model_width, wide)
    vectors_full = head_weight[:, both : both + 4].astype(f32)
    attn_gain_col, attn_shift_col = vectors_full[:, :1], vectors_full[:, 1:2]
    ffn_gain_row, ffn_shift_row = vectors_full[:, 2][None], vectors_full[:, 3][None]
    head_float = head_weight[:, :both].astype(f32)
    head_scaled = (head_float * attn_gain_col).astype(bf)
    head_offset = jnp.sum(head_float * attn_shift_col, axis=0, keepdims=True)
    inner_rows = traded(traded(inner_split, "rc", 1), "ry", 0)
    cut = round_count * weight_rows
    output_rows = ordered(ordered(output_weight, "rc", 0), "ry", 0).reshape(cut, model_width)
    shard = jnp.stack([inner_rows.reshape(cut, -1), outer_weight, output_rows])
    up, down, head_scaled, head_offset, shard, second_later = together(
        up, down, head_scaled, head_offset, shard, second_grad
    )
    ring.append((up, down))

    def head_part(parts):
        rows = [product(part, head_scaled) + head_offset for part in parts]
        return over_groups(jnp.concatenate(rows, axis=0).astype(bf))

    up, down = ring_step(up, down)
    first_heads = head_part([part for step in ring for part in step])
    up, down, first_heads, codes, shard = together(up, down, first_heads, codes, shard)
    ring.append((up, down))

    half = own_rows // 2
    up, down = ring_step(up[:half], down[half:])
    ring.append((up, down))
    last_heads = head_part(ring[3] + ring[4])
    head_own = []
    for rows in (first_heads, last_heads):
        head_own += [rows, swapped(rows, "ry")]
    head_own = jnp.concatenate([part.reshape(-1, both) for part in head_own], axis=0)
    place, key_bucket = sorted_layout(codes, slot_rows, own_spans)
    in_table, out_table = chunk_tables(groups)
    head_own, place, key_bucket, in_table, out_table = together(
        head_own, place, key_bucket, in_table, out_table
    )
    head_peer = swapped(head_own, "rc")

    grad_peer = swapped(second_later, "rc")
    grad_far = swapped(second_later, "ry")
    grad_last = swapped(grad_far, "rc")
    shards = lax.all_gather(shard, SEQ, axis=0, tiled=False)

    payload_own, payload_peer, sorted_q, sorted_k, sorted_v, probs, token_sums = attend_forward(
        in_table,
        out_table,
        place,
        key_bucket,
        head_own,
        head_peer,
        own_rows,
    )
    packed = (2, groups, heads, own_rows + PAD, HEADD)
    head_sums = sum_pair(payload_own.reshape(packed), payload_peer.reshape(packed))
    mixed_parts = exchange(sum_groups(head_sums))
    mixed_parts, shards = together(mixed_parts, shards)
    mixed, mixed_low, first_sum, ffn_unit, ffn_scale, ffn_low = mix_rows(
        mixed_parts, shards, first_half, ffn_gain_row, ffn_shift_row
    )
    ffn_low, qkv_rows = together(ffn_low, jnp.stack([qk_weight, value_weight]))
    qkv_rows = exchange(jnp.broadcast_to(qkv_rows[None], (heads,) + qkv_rows.shape))
    ffn_far = swapped(ffn_low, "ry")
    pair = feed_forward(ffn_low, swapped(ffn_low, "rc"), second_later, grad_peer, shards)
    ffn_far, pair = together(ffn_far, pair)
    far = feed_forward(ffn_far, swapped(ffn_far, "rc"), grad_far, grad_last, shards)
    pair, far = together(pair, far)
    ffn_pair, grad_pair, hidden_pair, inner_pair, *back_pair = pair
    ffn_far, grad_far, hidden_far, inner_far, *back_far = far
    far_sum = swapped(pair_sum(back_far[0], back_far[1], "rc"), "ry")
    near_sum = pair_sum(back_pair[0], back_pair[1], "rc")
    second_far = pair_sum(back_far[2], back_far[3], "rc")
    second_pair = pair_sum(back_pair[2], back_pair[3], "rc")
    outer_part = (against(hidden_pair, grad_pair) + against(hidden_far, grad_far)).astype(bf)
    inner_part = (against(ffn_pair, inner_pair) + against(ffn_far, inner_far)).astype(bf)
    part_sums = jnp.stack(
        [
            inner_part.reshape(seq_count, cut, -1),
            outer_part.reshape(seq_count, -1, model_width),
        ],
        axis=1,
    )
    near_sum, far_sum, part_sums, qkv_rows = together(near_sum, far_sum, part_sums, qkv_rows)
    part_grads = lax.psum_scatter(part_sums, SEQ, scatter_dimension=0, tiled=False)
    carry_low, back_parts = carry_rows(
        near_sum,
        far_sum,
        ffn_gain_row,
        ffn_unit,
        ffn_scale,
        first_grad,
        shards,
        mixed,
        mixed_parts,
    )
    back_parts = exchange(back_parts)
    output_part = against(mixed_low, carry_low).astype(bf)
    output_part = output_part.reshape(heads, groups, 2, 2, weight_rows, model_width)
    output_part = scattered(scattered(output_part, "rc", 3), "ry", 2)
    back_parts, output_part, second_pair, second_far, qkv_rows = together(
        back_parts, output_part, second_pair, second_far, qkv_rows
    )
    qkv_rows = jnp.transpose(over_groups(qkv_rows), (2, 1, 0, 3, 4))
    back_own, back_peer = spread_pair(over_groups(back_parts))
    back_own, second_far, qkv_rows = together(back_own, second_far, qkv_rows)
    second_far = swapped(second_far, "ry")
    qkv_got = swapped(qkv_rows, "ry")
    query_value_own, query_value_peer = attend_backward(
        out_table,
        place,
        back_own.reshape(-1, HEADD),
        back_peer.reshape(-1, HEADD),
        token_sums,
        sorted_q,
        sorted_k,
        sorted_v,
        probs,
        own_rows,
    )
    vector_rows = back_parts[:, own_rows + 2 * blocks : own_rows + 2 * blocks + 2]
    packed = (2, groups, heads, own_rows, both)
    vector_rows = back_parts[:, own_rows + 2 * blocks : own_rows + 2 * blocks + 2]
    packed = (2, groups, heads, own_rows, both)
    query_value_peer, qkv_got, second_far = together(query_value_peer, qkv_got, second_far)
    second_sum = second_in + second_pair.astype(f32) + second_far.astype(f32)
    head_back = pair_sum(query_value_own.reshape(packed), query_value_peer.reshape(packed), "rc")
    head_back, output_part, vector_rows, qkv_rows, qkv_got = together(
        head_back, output_part, vector_rows, qkv_rows, qkv_got
    )
    qkv_rows = pair_order(qkv_rows, qkv_got, "ry", 3)
    qkv_full = ordered(qkv_rows, "rc", 4).reshape(2, model_width, model_width)
    output_rows = exchange(sum_groups(jnp.transpose(output_part, (1, 0, 2, 3))))
    head_got, output_rows, qkv_full = together(
        swapped(head_back[1], "ry"), output_rows, qkv_full
    )
    output_grad = jnp.sum(output_rows.astype(f32), axis=0)
    head_back = sum_groups(add_rows(head_back[0], head_got))
    own_back = exchange(head_back)
    vector_sums = jnp.sum(vector_rows.astype(f32), axis=0)
    if groups > 1:
        vector_sums = lax.psum_scatter(
            vector_sums.reshape(2, groups, -1), "kk", scatter_dimension=1, tiled=False
        )
    vector_sums = jnp.pad(
        vector_sums.reshape(2, 2, 2, weight_rows), ((0, 6), (0, 0), (0, 0), (0, HEADD - weight_rows))
    )
    pieces = [part for step in ring for part in step]
    qkv_part, col_part = weight_part(ring_order(), head_back, pieces)
    qkv_part = qkv_part.reshape(heads, groups, 2, 2, weight_rows, both)
    col_part = jnp.broadcast_to(col_part[0], (heads, groups, 2, 2, PAD, both))
    qkv_part = jnp.concatenate([qkv_part, col_part], axis=4).astype(bf)
    qkv_part = scattered(scattered(qkv_part, "rc", 3), "ry", 2)
    qkv_part = sum_groups(jnp.transpose(qkv_part, (1, 0, 2, 3)))
    outer_grad = part_grads[1].astype(f32)
    turned = part_grads[0].reshape(2, 2, weight_rows, -1)
    turned = traded(traded(turned, "ry", 0), "rc", 1)
    vector_sums = wide_scattered(wide_scattered(vector_sums, "rc", 2), "ry", 1)
    vector_grads = vector_sums[:2, :weight_rows]
    own_back, qkv_part, turned = together(own_back, qkv_part, turned)
    inner_cols = turned.reshape(round_count, weight_rows, seq_count, piece)
    inner_grad = jnp.transpose(inner_cols, (1, 2, 0, 3)).reshape(weight_rows, hidden_width)
    qkv_rows = exchange(qkv_part).astype(f32)
    qkv_rows = qkv_rows.reshape(heads, weight_rows + PAD, 2, HEADD)
    qkv_rows = jnp.transpose(qkv_rows, (2, 1, 0, 3)).reshape(2, weight_rows + PAD, model_width)
    unit_grads, col_sums = qkv_rows[:, :weight_rows], qkv_rows[:, weight_rows]
    own_weights = jnp.stack([qk_weight, value_weight]).astype(f32)
    gain_own = attn_gain.astype(f32)[:, None]
    shift_own = attn_shift.astype(f32)[:, None]
    qkv_grads = unit_grads * gain_own + shift_own * col_sums[:, None]
    attn_gain_grad = jnp.sum(own_weights * unit_grads, axis=(0, 2))
    attn_shift_grad = jnp.sum(own_weights * col_sums[:, None], axis=(0, 2))

    second_carry = last_rows(
        own_back, qkv_full, attn_gain_col.reshape(1, -1), unit, unit_scale, second_grad
    )

    return (
        first_sum,
        second_sum.astype(bf),
        carry_low,
        second_carry,
        qkv_grads[0],
        qkv_grads[1],
        output_grad,
        inner_grad.astype(f32),
        outer_grad,
        attn_gain_grad,
        attn_shift_grad,
        vector_grads[0],
        vector_grads[1],
    )


def solution(mesh):
    seq_count, round_count = mesh.devices.shape
    shape = (HEADS, seq_count // HEADS, round_count // 2, 2)
    split_mesh = Mesh(mesh.devices.reshape(shape), ALL)
    rows = P(ALL, None)
    vector = P(ALL)
    table = P(ROUND, SEQ)
    in_specs = (rows,) * 7 + (vector,) * 4 + (table,) * 2 + (rows,) * 2
    out_specs = (rows,) * 9 + (vector,) * 4
    return jax.shard_map(
        per_device, mesh=split_mesh, in_specs=in_specs, out_specs=out_specs, check_vma=False
    )
```

```python
import functools
import math

import jax
import jax.numpy as jnp
from jax import lax
from jax.experimental import pallas as pl
from jax.experimental.pallas import tpu as pltpu
from jax.sharding import Mesh
from jax.sharding import PartitionSpec as P

HEADS = 8
NORM_EPS = 1e-05
SPAN = 64
HEADD = 128
PAD = 16
UNROLL = 17
TOKB = 128
BUCKETS = 32
CHUNK = 4096
VMEM_LIMIT = 60 * 2**20
KEY_EPS = 1e-06
bf = jnp.bfloat16
f32 = jnp.float32


def product(left_side, right_side):
    return jnp.dot(left_side, right_side, preferred_element_type=f32)


def against(left_side, right_side):
    return lax.dot_general(
        left_side, right_side, (((0,), (0,)), ((), ())), preferred_element_type=f32
    )


def through(left_side, right_side):
    return lax.dot_general(
        left_side, right_side, (((1,), (1,)), ((), ())), preferred_element_type=f32
    )


def takes(microseconds):
    return pl.CostEstimate(
        flops=int(microseconds * 1e8), bytes_accessed=int(microseconds * 3e6), transcendentals=0
    )


def aligned(start, size, step=SPAN):
    return pl.ds(pl.multiple_of(start, step), size)


def fill(ref, value):
    def body(step, carry):
        ref[aligned(step * SPAN, SPAN), :] = jnp.full((SPAN, ref.shape[1]), value, ref.dtype)
        return carry

    lax.fori_loop(0, ref.shape[0] // SPAN, body, 0)


def diagonal():
    rows = lax.broadcasted_iota(jnp.int32, (TOKB, TOKB), 0)
    return rows == lax.broadcasted_iota(jnp.int32, (TOKB, TOKB), 1)


def chunk_start(table_ref, own_rows, position):
    return table_ref[position // own_rows] * own_rows + position % own_rows


def lanes(row, eye, ones):
    high = row.astype(bf).astype(f32)
    parts = [jnp.where(eye, high, 0.0), jnp.where(eye, row - high, 0.0)]
    return product(jnp.concatenate(parts, axis=1).astype(bf), ones)


def forward_kernel(
    own_rows,
    load_steps,
    in_ref,
    out_ref,
    place_ref,
    bucket_ref,
    own_ref,
    peer_ref,
    pay_own_ref,
    pay_peer_ref,
    query_out,
    key_out,
    value_out,
    prob_out,
    sum_ref,
    query_ref,
    key_ref,
    value_ref,
    prob_ref,
    wide_a,
    wide_b,
    stage_a,
    stage_b,
    sems,
):
    step = pl.program_id(0)
    leaving = [
        pltpu.make_async_copy(source, target, sems.at[number])
        for number, (source, target) in enumerate(
            [
                (query_ref, query_out),
                (key_ref, key_out),
                (value_ref, value_out),
                (prob_ref, prob_out),
            ]
        )
    ]
    own_spans = prob_ref.shape[0] // SPAN
    tail = SPAN * (own_spans + 1)

    @pl.when(step == 0)
    def _():
        fill(wide_a, 0.0)
        fill(wide_b, 0.0)

    def scatter_from(token_ref):
        def scatter(block, carry):
            both = token_ref[aligned(block * TOKB, TOKB, TOKB), :].astype(f32)
            stage_a[...] = both[:, :HEADD]
            stage_b[...] = both[:, HEADD:]
            first = chunk_start(in_ref, own_rows, step * CHUNK + block * TOKB)
            for row in range(TOKB):
                place = place_ref[first + row]
                wide_a[pl.ds(place, 1), :] = stage_a[row : row + 1, :]
                wide_b[pl.ds(place, 1), :] = stage_b[row : row + 1, :]
            return carry

        lax.fori_loop(0, CHUNK // TOKB, scatter, 0)

    pl.when(step < load_steps // 2)(lambda: scatter_from(own_ref))
    pl.when((step >= load_steps // 2) & (step < load_steps))(lambda: scatter_from(peer_ref))

    def unit_keys(query):
        square = jnp.sum(query * query, axis=-1, keepdims=True)
        scale = lax.rsqrt(square * (1.0 / HEADD) + KEY_EPS) * HEADD**-0.5
        return (query * scale).astype(bf)

    @pl.when(step == load_steps)
    def _():
        query_ref[:SPAN, :] = wide_a[:SPAN, :].astype(bf)
        key_ref[:SPAN, :] = unit_keys(wide_a[:SPAN, :])
        value_ref[:SPAN, :] = wide_b[:SPAN, :].astype(bf)
        wide_a[:SPAN, :] = jnp.zeros((SPAN, HEADD), f32)
        wide_b[:SPAN, :] = jnp.zeros((SPAN, HEADD), f32)
        for ref in (query_ref, key_ref, value_ref):
            ref[pl.ds(tail, SPAN), :] = jnp.zeros((SPAN, HEADD), bf)
        ones = jnp.ones((2 * SPAN, HEADD), bf)
        row_ids = lax.broadcasted_iota(jnp.int32, (SPAN, 2 * SPAN), 0)
        lane_ids = lax.broadcasted_iota(jnp.int32, (SPAN, 2 * SPAN), 1)
        before, itself = lane_ids == row_ids, lane_ids == row_ids + SPAN

        def spans(group, carry):
            first = group * (UNROLL * SPAN)
            prev = aligned(first, SPAN)
            here = aligned(first + SPAN, UNROLL * SPAN)
            query_wide = wide_a[here, :]
            values = wide_b[here, :].astype(bf)
            keys = jnp.concatenate([key_ref[prev, :], unit_keys(query_wide)], axis=0)
            seen = jnp.concatenate([value_ref[prev, :], values], axis=0)
            query = query_wide.astype(bf)
            key_buckets, columns = [], []
            for span in range(UNROLL):
                row = bucket_ref[pl.ds(group * UNROLL + span, 1), :]
                high = row.astype(bf).astype(f32)
                low = pltpu.roll(row - high, SPAN, 1)
                key_buckets.append(row)
                columns.append(jnp.where(itself, high, jnp.where(before, low, 0.0)).astype(bf))
            columns = product(jnp.concatenate(columns, axis=0), ones)
            raised = []
            for span in range(UNROLL):
                mine = slice(span * SPAN, (span + 1) * SPAN)
                both = slice(span * SPAN, (span + 2) * SPAN)
                same = columns[mine] == key_buckets[span]
                matches = jnp.sum(jnp.where(same, 1.0, 0.0), axis=-1, keepdims=True)
                allowed = same & (jnp.logical_not(itself) | (matches < 1.5))
                scores = through(query[mine], keys[both])
                raised.append(jnp.where(allowed, jnp.exp(scores), 0.0))
            lows = [member.astype(bf) for member in raised]
            totals = product(jnp.concatenate(lows, axis=0), ones)
            results = []
            for span in range(UNROLL):
                mine = slice(span * SPAN, (span + 1) * SPAN)
                both = slice(span * SPAN, (span + 2) * SPAN)
                total = totals[mine]
                inverse = jnp.where(total > 0.0, 1.0 / total, 0.0)
                probs = (raised[span] * inverse).astype(bf)
                results.append((product(lows[span], seen[both]), total, probs))
            query_ref[here, :] = query
            key_ref[here, :] = keys[SPAN:]
            value_ref[here, :] = values
            for span, (weighted, total, probs) in enumerate(results):
                at = aligned(first + (span + 1) * SPAN, SPAN)
                wide_a[at, :] = weighted
                wide_b[at, :] = total
                prob_ref[aligned(first + span * SPAN, SPAN), :] = probs
            return carry

        lax.fori_loop(0, own_spans // UNROLL, spans, 0)
        for copy in leaving:
            copy.start()
        wide_a[pl.ds(tail, SPAN), :] = jnp.zeros((SPAN, HEADD), f32)
        wide_b[pl.ds(tail, SPAN), :] = jnp.zeros((SPAN, HEADD), f32)

    def collect_to(pay_ref):
        blocks = own_rows // TOKB
        per_step = CHUNK // own_rows
        eye = diagonal()
        sum_rows = lax.broadcasted_iota(jnp.int32, (PAD, TOKB), 0)
        offset = (step - load_steps - 1) * CHUNK

        def collect(chunk, carry):
            first = chunk * (own_rows + PAD)
            sums = jnp.zeros((PAD, TOKB), f32)
            for block in range(blocks):
                start = chunk_start(out_ref, own_rows, offset + chunk * own_rows + block * TOKB)
                for row in range(TOKB):
                    place = place_ref[start + row]
                    stage_a[row : row + 1, :] = wide_a[pl.ds(place, 1), :]
                    stage_b[row : row + 1, :] = wide_b[pl.ds(place, 1), :]
                pay_ref[aligned(first + block * TOKB, TOKB, PAD), :] = stage_a[...].astype(bf)
                packed = jnp.sum(jnp.where(eye, stage_b[...], 0.0), axis=0, keepdims=True)
                sum_ref[pl.ds(chunk * blocks + block, 1), :] = packed
                sums = jnp.where(sum_rows == block, packed, sums)
            pay_ref[aligned(first + own_rows, PAD, PAD), :] = sums.astype(bf)
            return carry

        lax.fori_loop(0, per_step, collect, 0)

    half = load_steps + 1 + load_steps // 2
    pl.when((step > load_steps) & (step < half))(lambda: collect_to(pay_own_ref))
    pl.when(step >= half)(lambda: collect_to(pay_peer_ref))

    @pl.when(step == 2 * load_steps)
    def _():
        for copy in leaving:
            copy.wait()


def part_spec(shape, first, count):
    return pl.BlockSpec(shape, lambda step: (jnp.clip(step - first, 0, count - 1), 0))


def attend_forward(in_table, out_table, place, key_bucket, own, peer, own_rows):
    tokens = place.shape[0]
    steps = tokens // CHUNK
    half = steps // 2
    own_spans = key_bucket.shape[0]
    rows = SPAN * (own_spans + 2)
    pay_rows = CHUNK // own_rows * (own_rows + PAD)
    once = pl.Buffered(1)

    def whole(shape):
        return pl.BlockSpec(shape, lambda step: (0, 0), pipeline_mode=once)

    sorted_rows = jax.ShapeDtypeStruct((rows, HEADD), bf)
    return pl.pallas_call(
        functools.partial(forward_kernel, own_rows, steps),
        grid=(2 * steps + 1,),
        out_shape=(
            jax.ShapeDtypeStruct((half * pay_rows, HEADD), bf),
            jax.ShapeDtypeStruct((half * pay_rows, HEADD), bf),
            sorted_rows,
            sorted_rows,
            sorted_rows,
            jax.ShapeDtypeStruct((own_spans * SPAN, 2 * SPAN), bf),
            jax.ShapeDtypeStruct((tokens // TOKB, TOKB), f32),
        ),
        in_specs=[
            pl.BlockSpec(memory_space=pltpu.SMEM),
            pl.BlockSpec(memory_space=pltpu.SMEM),
            pl.BlockSpec(memory_space=pltpu.SMEM),
            whole(key_bucket.shape),
            part_spec((CHUNK, 2 * HEADD), 0, half),
            part_spec((CHUNK, 2 * HEADD), half, half),
        ],
        out_specs=(
            part_spec((pay_rows, HEADD), steps + 1, half),
            part_spec((pay_rows, HEADD), steps + 1 + half, half),
            pl.BlockSpec(memory_space=pl.ANY),
            pl.BlockSpec(memory_space=pl.ANY),
            pl.BlockSpec(memory_space=pl.ANY),
            pl.BlockSpec(memory_space=pl.ANY),
            part_spec((CHUNK // TOKB, TOKB), steps + 1, steps),
        ),
        scratch_shapes=[pltpu.VMEM((rows, HEADD), bf)] * 3
        + [pltpu.VMEM((own_spans * SPAN, 2 * SPAN), bf)]
        + [pltpu.VMEM((rows, HEADD), f32)] * 2
        + [pltpu.VMEM((TOKB, HEADD), f32)] * 2
        + [pltpu.SemaphoreType.DMA((4,))],
        compiler_params=pltpu.CompilerParams(vmem_limit_bytes=VMEM_LIMIT),
        name="attend_forward",
        cost_estimate=takes(35),
    )(in_table, out_table, place, key_bucket, own, peer)


def backward_kernel(
    own_rows,
    load_steps,
    table_ref,
    place_ref,
    pay_own_ref,
    pay_peer_ref,
    sum_ref,
    query_in,
    key_in,
    value_in,
    prob_in,
    out_own_ref,
    out_peer_ref,
    query_ref,
    key_ref,
    value_ref,
    prob_ref,
    wide_a,
    wide_b,
    wide_c,
    stage_a,
    stage_b,
    sems,
):
    step = pl.program_id(0)
    coming = [
        pltpu.make_async_copy(source, target, sems.at[number])
        for number, (source, target) in enumerate(
            [(query_in, query_ref), (key_in, key_ref), (value_in, value_ref), (prob_in, prob_ref)]
        )
    ]
    own_spans = prob_ref.shape[0] // SPAN
    tail = SPAN * (own_spans + 1)

    @pl.when(step == 0)
    def _():
        for copy in coming:
            copy.start()
        fill(wide_a, 0.0)
        fill(wide_b, 0.0)

    def scatter_from(pay_ref):
        blocks = own_rows // TOKB
        eye = diagonal()
        ones = jnp.ones((2 * TOKB, TOKB), bf)

        def scatter(chunk, carry):
            first = chunk * (own_rows + PAD)
            extra = pay_ref[aligned(first + own_rows, PAD, PAD), :].astype(f32)
            for block in range(blocks):
                share = sum_ref[pl.ds(chunk * blocks + block, 1), :]
                share = share / extra[blocks + block : blocks + block + 1, :]
                rows = pay_ref[aligned(first + block * TOKB, TOKB, PAD), :].astype(f32)
                stage_a[...] = rows * lanes(share, eye, ones)
                stage_b[...] = lanes(share * extra[block : block + 1, :], eye, ones)
                start = step * CHUNK + chunk * own_rows + block * TOKB
                start = chunk_start(table_ref, own_rows, start)
                for row in range(TOKB):
                    place = place_ref[start + row]
                    wide_a[pl.ds(place, 1), :] = stage_a[row : row + 1, :]
                    wide_b[pl.ds(place, 1), :] = stage_b[row : row + 1, :]
            return carry

        lax.fori_loop(0, CHUNK // own_rows, scatter, 0)

    pl.when(step < load_steps // 2)(lambda: scatter_from(pay_own_ref))
    pl.when((step >= load_steps // 2) & (step < load_steps))(lambda: scatter_from(pay_peer_ref))

    def pulled(query_low, d_query, d_keys):
        query = query_low.astype(f32)
        inverse = lax.rsqrt(
            jnp.sum(query * query, axis=-1, keepdims=True) * (1.0 / HEADD) + KEY_EPS
        )
        along = jnp.sum(query * d_keys, axis=-1, keepdims=True)
        scale = inverse * HEADD**-0.5
        return d_query + scale * d_keys - (scale * inverse * inverse * along * (1.0 / HEADD)) * query

    @pl.when(step == load_steps)
    def _():
        for copy in coming:
            copy.wait()
        for ref in (wide_a, wide_b, wide_c):
            ref[:SPAN, :] = jnp.zeros((SPAN, HEADD), f32)
        zero = jnp.zeros((SPAN, HEADD), bf)

        def spans(group, carry):
            first = group * (UNROLL * SPAN)
            prev = aligned(first, SPAN)
            own = aligned(first, UNROLL * SPAN)
            here = aligned(first + SPAN, UNROLL * SPAN)
            around = aligned(first, (UNROLL + 1) * SPAN)
            query = query_ref[around, :]
            keys = key_ref[around, :]
            values = value_ref[around, :]
            probs = prob_ref[own, :]
            d_out = wide_a[here, :].astype(bf)
            delta = wide_b[here, :]
            d_query = [wide_a[prev, :]]
            d_keys = [wide_b[prev, :]]
            d_values = [wide_c[prev, :]]
            for span in range(UNROLL):
                mine = slice(span * SPAN, (span + 1) * SPAN)
                after = slice((span + 1) * SPAN, (span + 2) * SPAN)
                both = slice(span * SPAN, (span + 2) * SPAN)
                d_probs = through(d_out[mine], values[both])
                prob = probs[mine]
                d_scores = (prob.astype(f32) * (d_probs - delta[mine])).astype(bf)
                d_query.append(product(d_scores, keys[both]))
                right = jnp.concatenate(
                    [
                        jnp.concatenate([query[after], zero], axis=1),
                        jnp.concatenate([zero, d_out[mine]], axis=1),
                    ],
                    axis=0,
                )
                pair = against(jnp.concatenate([d_scores, prob], axis=0), right)
                d_keys[-1] = d_keys[-1] + pair[:SPAN, :HEADD]
                d_values[-1] = d_values[-1] + pair[:SPAN, HEADD:]
                d_keys.append(pair[SPAN:, :HEADD])
                d_values.append(pair[SPAN:, HEADD:])
            for span in range(UNROLL + 1):
                at = aligned(first + span * SPAN, SPAN)
                wide_c[at, :] = d_values[span]
                if span < UNROLL:
                    rows = slice(span * SPAN, (span + 1) * SPAN)
                    wide_a[at, :] = pulled(query[rows], d_query[span], d_keys[span])
                else:
                    wide_a[at, :] = d_query[span]
                    wide_b[at, :] = d_keys[span]
            return carry

        lax.fori_loop(0, own_spans // UNROLL, spans, 0)
        last = pl.ds(tail - SPAN, SPAN)
        wide_a[last, :] = pulled(query_ref[last, :], wide_a[last, :], wide_b[last, :])
        wide_a[pl.ds(tail, SPAN), :] = jnp.zeros((SPAN, HEADD), f32)
        wide_c[pl.ds(tail, SPAN), :] = jnp.zeros((SPAN, HEADD), f32)

    def collect_to(out_ref):
        offset = (step - load_steps - 1) * CHUNK

        def collect(block, carry):
            start = chunk_start(table_ref, own_rows, offset + block * TOKB)
            for row in range(TOKB):
                place = place_ref[start + row]
                stage_a[row : row + 1, :] = wide_a[pl.ds(place, 1), :]
                stage_b[row : row + 1, :] = wide_c[pl.ds(place, 1), :]
            here = aligned(block * TOKB, TOKB, TOKB)
            out_ref[here, :HEADD] = stage_a[...].astype(bf)
            out_ref[here, HEADD:] = stage_b[...].astype(bf)
            return carry

        lax.fori_loop(0, CHUNK // TOKB, collect, 0)

    half = load_steps + 1 + load_steps // 2
    pl.when((step > load_steps) & (step < half))(lambda: collect_to(out_own_ref))
    pl.when(step >= half)(lambda: collect_to(out_peer_ref))


def attend_backward(out_table, place, pay_own, pay_peer, sums, query, keys, values, probs, own_rows):
    tokens = place.shape[0]
    steps = tokens // CHUNK
    half = steps // 2
    rows = query.shape[0]
    pay_rows = CHUNK // own_rows * (own_rows + PAD)
    out_half = jax.ShapeDtypeStruct((tokens // 2, 2 * HEADD), bf)
    return pl.pallas_call(
        functools.partial(backward_kernel, own_rows, steps),
        grid=(2 * steps + 1,),
        out_shape=(out_half, out_half),
        in_specs=[
            pl.BlockSpec(memory_space=pltpu.SMEM),
            pl.BlockSpec(memory_space=pltpu.SMEM),
            part_spec((pay_rows, HEADD), 0, half),
            part_spec((pay_rows, HEADD), half, half),
            part_spec((CHUNK // TOKB, TOKB), 0, steps),
            pl.BlockSpec(memory_space=pl.ANY),
            pl.BlockSpec(memory_space=pl.ANY),
            pl.BlockSpec(memory_space=pl.ANY),
            pl.BlockSpec(memory_space=pl.ANY),
        ],
        out_specs=(
            part_spec((CHUNK, 2 * HEADD), steps + 1, half),
            part_spec((CHUNK, 2 * HEADD), steps + 1 + half, half),
        ),
        scratch_shapes=[pltpu.VMEM((rows, HEADD), bf)] * 3
        + [pltpu.VMEM(probs.shape, bf)]
        + [pltpu.VMEM((rows, HEADD), f32)] * 3
        + [pltpu.VMEM((TOKB, HEADD), f32)] * 2
        + [pltpu.SemaphoreType.DMA((4,))],
        compiler_params=pltpu.CompilerParams(vmem_limit_bytes=VMEM_LIMIT),
        name="attend_backward",
        cost_estimate=takes(44),
    )(out_table, place, pay_own, pay_peer, sums, query, keys, values, probs)


def shard_spec(shards, number):
    block = (shards.shape[0], 1) + shards.shape[2:]
    return pl.BlockSpec(block, lambda *_: (0, number, 0, 0), pipeline_mode=pl.Buffered(1))


def whole_weight(ref):
    value = ref[...]
    return value.reshape(-1, value.shape[-1])


def feed_kernel(
    own_ref, peer_ref, grad_own_ref, grad_peer_ref, inner_weight_ref, outer_weight_ref,
    row_ref, grad_ref, hidden_ref, inner_ref,
    back_own_ref, back_peer_ref, second_own_ref, second_peer_ref,
):
    step = pl.program_id(0)

    @pl.when(step == 0)
    def _():
        row_ref[...] = own_ref[...]
        grad_ref[...] = grad_own_ref[...]

    @pl.when(step == 1)
    def _():
        row_ref[...] = peer_ref[...]
        grad_ref[...] = grad_peer_ref[...]

    weight = whole_weight(inner_weight_ref)
    outer_weight = whole_weight(outer_weight_ref)
    act = product(row_ref[...], weight)
    size = jnp.abs(act)
    bell = jnp.exp(act * act * -0.5)
    near = 1.0 / (1.0 + size * (0.3275911 * 0.5**0.5))
    tail = near * (0.254829592 + near * (-0.284496736 + near * (
        1.421413741 + near * (-1.453152027 + near * 1.061405429))))
    tail = tail * bell * 0.5
    normal = jnp.where(act >= 0.0, 1.0 - tail, tail)
    hidden = (act * normal).astype(bf)
    hidden_ref[...] = hidden
    slope = normal + act * bell * (2.0 * math.pi) ** -0.5
    inner = (through(grad_ref[...], outer_weight) * slope).astype(bf)
    inner_ref[...] = inner
    back = through(inner, weight).astype(bf)
    second = product(hidden, outer_weight).astype(bf)

    @pl.when(step == 0)
    def _():
        back_own_ref[...] = back
        second_own_ref[...] = second

    @pl.when(step == 1)
    def _():
        back_peer_ref[...] = back
        second_peer_ref[...] = second


def feed_forward(own, peer, grad_own, grad_peer, shards):
    count, width = own.shape
    units = shards.shape[3]

    def part(columns):
        return pl.BlockSpec((count, columns), lambda i: (i, 0))

    whole = pl.BlockSpec((count, width), lambda i: (0, 0), pipeline_mode=pl.Buffered(1))
    by_width = jax.ShapeDtypeStruct((2 * count, width), bf)
    by_units = jax.ShapeDtypeStruct((2 * count, units), bf)
    half = jax.ShapeDtypeStruct((count, width), bf)
    return pl.pallas_call(
        feed_kernel,
        grid=(2,),
        out_shape=(by_width, by_width, by_units, by_units, half, half, half, half),
        in_specs=[whole] * 4 + [shard_spec(shards, 0), shard_spec(shards, 1)],
        out_specs=(
            part(width), part(width), part(units), part(units), whole, whole, whole, whole
        ),
        compiler_params=pltpu.CompilerParams(vmem_limit_bytes=VMEM_LIMIT),
        name="feed_forward",
        cost_estimate=takes(9),
    )(own, peer, grad_own, grad_peer, shards, shards)


def mix_kernel(
    parts_ref, weight_ref, first_ref, gain_ref, shift_ref,
    mixed_ref, low_ref, sum_ref, unit_ref, scale_ref, feed_ref,
):
    heads, rows = parts_ref.shape[0], first_ref.shape[0]
    eye = diagonal()
    ones = jnp.ones((2 * TOKB, TOKB), bf)
    for head in range(heads):
        columns = slice(head * HEADD, (head + 1) * HEADD)
        for block in range(rows // TOKB):
            here = slice(block * TOKB, (block + 1) * TOKB)
            sums = parts_ref[head, rows : rows + PAD, :].astype(f32)[block : block + 1]
            mixed = parts_ref[head, here, :].astype(f32) / lanes(sums, eye, ones)
            mixed_ref[here, columns] = mixed
            low_ref[here, columns] = mixed.astype(bf)
    total = first_ref[...].astype(f32) + product(low_ref[...], whole_weight(weight_ref))
    sum_ref[...] = total.astype(bf)
    centre = total - jnp.mean(total, axis=-1, keepdims=True)
    scale = lax.rsqrt(jnp.mean(centre * centre, axis=-1, keepdims=True) + NORM_EPS)
    unit = centre * scale
    unit_ref[...] = unit
    scale_ref[...] = scale
    feed_ref[...] = (unit * gain_ref[...] + shift_ref[...]).astype(bf)


def mix_rows(parts, shards, first_half, gain, shift):
    rows, width = first_half.shape
    vm = pl.BlockSpec(memory_space=pltpu.VMEM)
    wide, low = jax.ShapeDtypeStruct((rows, width), f32), jax.ShapeDtypeStruct((rows, width), bf)
    return pl.pallas_call(
        mix_kernel,
        out_shape=(wide, low, low, wide, jax.ShapeDtypeStruct((rows, 1), f32), low),
        grid=(1,),
        in_specs=[vm, shard_spec(shards, 2), vm, vm, vm],
        out_specs=(vm,) * 6,
        compiler_params=pltpu.CompilerParams(vmem_limit_bytes=VMEM_LIMIT),
        name="mix_rows",
        cost_estimate=takes(5),
    )(parts, shards, first_half, gain, shift)


def carry_kernel(
    near_ref, far_ref, gain_ref, unit_ref, scale_ref, grad_ref, weight_ref, mixed_ref, parts_ref,
    carry_ref, pay_ref, wide_ref,
):
    heads, rows = parts_ref.shape[0], grad_ref.shape[0]
    blocks = rows // TOKB
    back = near_ref[...].astype(f32) + far_ref[...].astype(f32)
    unit = unit_ref[...]
    gain_sum = jnp.sum(back * unit, axis=0, keepdims=True)
    shift_sum = jnp.sum(back, axis=0, keepdims=True)
    grad = back * gain_ref[...]
    along = jnp.mean(grad * unit, axis=-1, keepdims=True)
    grad = scale_ref[...] * (grad - jnp.mean(grad, axis=-1, keepdims=True) - unit * along)
    carry_ref[...] = (grad_ref[...].astype(f32) + grad).astype(bf)
    wide_ref[...] = through(carry_ref[...], whole_weight(weight_ref))
    eye = diagonal()
    pad_rows = lax.broadcasted_iota(jnp.int32, (PAD, TOKB), 0)
    for head in range(heads):
        columns = slice(head * HEADD, (head + 1) * HEADD)
        sums = parts_ref[head, rows : rows + PAD, :].astype(f32)
        tails = jnp.zeros((PAD, TOKB), f32)
        for block in range(blocks):
            here = slice(block * TOKB, (block + 1) * TOKB)
            wide = wide_ref[here, columns]
            pay_ref[head, here, :] = wide.astype(bf)
            dot = jnp.sum(wide * mixed_ref[here, columns], axis=-1, keepdims=True)
            packed = jnp.sum(jnp.where(eye, dot, 0.0), axis=0, keepdims=True)
            tails = jnp.where(pad_rows == block, packed, tails)
            tails = jnp.where(pad_rows == blocks + block, sums[block : block + 1], tails)
        tails = jnp.where(pad_rows == 2 * blocks, gain_sum[:, columns], tails)
        tails = jnp.where(pad_rows == 2 * blocks + 1, shift_sum[:, columns], tails)
        pay_ref[head, rows : rows + PAD, :] = tails.astype(bf)


def carry_rows(near, far, gain, unit, scale, first_grad, shards, mixed, parts):
    rows, width = near.shape
    vm = pl.BlockSpec(memory_space=pltpu.VMEM)
    return pl.pallas_call(
        carry_kernel,
        out_shape=(
            jax.ShapeDtypeStruct((rows, width), bf),
            jax.ShapeDtypeStruct(parts.shape, bf),
        ),
        grid=(1,),
        in_specs=[vm] * 6 + [shard_spec(shards, 2)] + [vm] * 2,
        out_specs=(vm,) * 2,
        scratch_shapes=[pltpu.VMEM((rows, width), f32)],
        compiler_params=pltpu.CompilerParams(vmem_limit_bytes=VMEM_LIMIT),
        name="carry_rows",
        cost_estimate=takes(5),
    )(near, far, gain, unit, scale, first_grad, shards, mixed, parts)


def add_kernel(left_ref, right_ref, out_ref):
    total = left_ref[...].astype(f32) + right_ref[...].astype(f32)
    out_ref[...] = total.astype(out_ref.dtype)


def add_rows(left, right):
    shape = left.shape
    left, right = left.reshape(-1, shape[-1]), right.reshape(-1, shape[-1])
    step = math.gcd(left.shape[0], 1024)
    spec = pl.BlockSpec((step, shape[-1]), lambda i: (i, 0))
    out = pl.pallas_call(
        add_kernel,
        grid=(left.shape[0] // step,),
        out_shape=jax.ShapeDtypeStruct(left.shape, left.dtype),
        in_specs=[spec, spec],
        out_specs=spec,
        name="add_rows",
        cost_estimate=takes(3),
    )(left, right)
    return out.reshape(shape)


def last_kernel(
    back_ref, weight_ref, gain_ref, unit_ref, scale_ref, grad_ref, out_ref, query_ref, value_ref,
):
    for head in range(back_ref.shape[0]):
        columns = slice(head * HEADD, (head + 1) * HEADD)
        query_ref[:, columns] = back_ref[head, :, :HEADD]
        value_ref[:, columns] = back_ref[head, :, HEADD:]
    total = through(query_ref[...], weight_ref[0]) + through(value_ref[...], weight_ref[1])
    grad = total * gain_ref[...]
    unit = unit_ref[...]
    along = jnp.mean(grad * unit, axis=-1, keepdims=True)
    centred = grad - jnp.mean(grad, axis=-1, keepdims=True) - unit * along
    out_ref[...] = (grad_ref[...].astype(f32) + scale_ref[...] * centred).astype(bf)


def last_rows(own_back, weights, gain, unit, scale, second_grad):
    rows, width = unit.shape
    vm = pl.BlockSpec(memory_space=pltpu.VMEM)
    return pl.pallas_call(
        last_kernel,
        out_shape=jax.ShapeDtypeStruct((rows, width), bf),
        in_specs=[vm] * 6,
        out_specs=vm,
        scratch_shapes=[pltpu.VMEM((rows, width), bf)] * 2,
        compiler_params=pltpu.CompilerParams(vmem_limit_bytes=VMEM_LIMIT),
        name="last_rows",
        cost_estimate=takes(6),
    )(own_back, weights, gain, unit, scale, second_grad)


def weight_kernel(order_ref, back_ref, *refs):
    pieces, (part_ref, column_ref) = refs[:-2], refs[-2:]
    half = pieces[-1].shape[0]
    total = None
    for number, piece in enumerate(pieces[:-1]):
        back = back_ref[order_ref[number]]
        if piece.shape[0] == half:
            term = against(piece[...], back[:half]) + against(pieces[-1][...], back[half:])
        else:
            term = against(piece[...], back)
        total = term if total is None else total + term
    part_ref[...] = total
    columns = jnp.sum(back_ref[...].astype(f32), axis=(0, 1), keepdims=True)[0]
    column_ref[...] = jnp.broadcast_to(columns, column_ref.shape)


def weight_part(order, back, pieces):
    width = pieces[0].shape[1]
    vm = pl.BlockSpec(memory_space=pltpu.VMEM)
    return pl.pallas_call(
        weight_kernel,
        out_shape=(
            jax.ShapeDtypeStruct((width, back.shape[2]), f32),
            jax.ShapeDtypeStruct((8, back.shape[2]), f32),
        ),
        in_specs=[pl.BlockSpec(memory_space=pltpu.SMEM)] + [vm] * (1 + len(pieces)),
        out_specs=(vm, vm),
        compiler_params=pltpu.CompilerParams(vmem_limit_bytes=VMEM_LIMIT),
        name="weight_part",
        cost_estimate=takes(5),
    )(order, back, *pieces)


def layout_kernel(
    heads, slot_rows, first_ref, code_ref, place_ref, bucket_ref, start_ref, low_ref, end_ref
):
    sources = code_ref.shape[0]
    rows = place_ref.shape[0] // sources
    own_spans = bucket_ref.shape[0]
    categories = BUCKETS + 1
    before = first_ref[0].astype(f32)
    codes = code_ref[...].astype(f32)[:, :rows].reshape(sources * rows, 3 * TOKB)
    slots = codes[:, :TOKB] * 256.0 + codes[:, TOKB : 2 * TOKB]
    buckets = codes[:, 2 * TOKB :]
    target = jnp.floor(slots * (1.0 / slot_rows))
    block = target - before
    local = slots - target * slot_rows
    block_ids = lax.broadcasted_iota(jnp.int32, (16, TOKB), 0).astype(f32)
    bucket_ids = lax.broadcasted_iota(jnp.int32, (TOKB, TOKB), 0).astype(f32)
    counts = jnp.zeros((16, TOKB), f32)
    for row in range(sources * rows):
        left = jnp.where(block_ids == block[row : row + 1], 1.0, 0.0).astype(bf)
        right = jnp.where(bucket_ids == buckets[row : row + 1], 1.0, 0.0).astype(bf)
        counts += through(left, right)
    lane_ids = lax.broadcasted_iota(jnp.int32, (16, TOKB), 1)
    row_ids = lax.broadcasted_iota(jnp.int32, (16, TOKB), 0)
    total = jnp.broadcast_to(jnp.sum(counts, axis=1, keepdims=True), counts.shape)
    step = 1
    while step < categories:
        counts += jnp.where(lane_ids >= step, pltpu.roll(counts, step, 1), 0.0)
        step *= 2
    spans = jnp.where(row_ids == 0, 0.0, jnp.floor((total + (SPAN - 1)) * (1.0 / SPAN)))
    start = spans
    step = 1
    while step < 16:
        start += jnp.where(row_ids >= step, pltpu.roll(start, step, 0), 0.0)
        step *= 2
    start = (start - spans + 1.0) * SPAN
    last_start = jnp.floor(jnp.maximum(total - 1.0, 0.0) * (1.0 / SPAN)) * SPAN
    start = jnp.where(row_ids == 0, -last_start, start)
    start_ref[...] = start
    low_ref[...] = jnp.where(row_ids == 0, last_start, 0.0)
    unused = (row_ids > heads) | (lane_ids >= categories)
    ends = jnp.where(unused, 1e9, start + counts)
    for bucket in range(categories):
        wide = jnp.sum(jnp.where(lane_ids == bucket, ends, 0.0), axis=1, keepdims=True)
        end_ref[bucket] = jnp.broadcast_to(wide, ends.shape)
    place = jnp.full(local.shape, (own_spans + 1.0) * SPAN, f32)
    for number in range(heads + 1):
        here = (block == float(number)) & (local >= low_ref[number : number + 1, :])
        place = jnp.where(here, local + start_ref[number : number + 1, :], place)
    place_ref[...] = place.astype(jnp.int32)
    shape = (own_spans, TOKB)
    at = lax.broadcasted_iota(jnp.int32, shape, 0) * SPAN + lax.broadcasted_iota(jnp.int32, shape, 1)
    at = at.astype(f32)
    block_number = jnp.zeros(shape, f32)
    for number in range(1, heads + 1):
        block_number += jnp.where(at >= start_ref[number : number + 1, :], 1.0, 0.0)
    passed = -block_number * categories

    def count(bucket, passed):
        for number in range(heads + 1):
            passed += jnp.where(at >= end_ref[bucket, number : number + 1, :], 1.0, 0.0)
        return passed

    passed = lax.fori_loop(0, categories, count, passed)
    bucket_ref[...] = jnp.where(
        passed <= BUCKETS, (before + block_number) * BUCKETS + passed, -1.0
    )


def sorted_layout(first, codes, heads, slot_rows, own_spans, rows):
    sources = codes.shape[0]
    vm = pl.BlockSpec(memory_space=pltpu.VMEM)
    return pl.pallas_call(
        functools.partial(layout_kernel, heads, slot_rows),
        out_shape=(
            jax.ShapeDtypeStruct((sources * rows, TOKB), jnp.int32),
            jax.ShapeDtypeStruct((own_spans, 2 * SPAN), f32),
        ),
        in_specs=[pl.BlockSpec(memory_space=pltpu.SMEM), vm],
        out_specs=(vm, vm),
        scratch_shapes=[
            pltpu.VMEM((16, TOKB), f32),
            pltpu.VMEM((16, TOKB), f32),
            pltpu.VMEM((BUCKETS + 1, 16, TOKB), f32),
        ],
        compiler_params=pltpu.CompilerParams(vmem_limit_bytes=VMEM_LIMIT),
        name="sorted_layout",
        cost_estimate=takes(5),
    )(first, codes)


ALL = ("hd", "kk", "ry", "rc")
SEQ = ("hd", "kk")
ROUND = ("ry", "rc")
SWAP = [(0, 1), (1, 0)]
RING = (0, 2, 4, 6, 7, 5, 3, 1)
UP = [(RING[i], RING[(i + 1) % HEADS]) for i in range(HEADS)]
DOWN = [(RING[(i + 1) % HEADS], RING[i]) for i in range(HEADS)]
STEPS = ((0, -1, 1, -2, 2), (-3, 3, 4))
BUCKETS = 32


def normalised(values):
    centre = values - jnp.mean(values, axis=-1, keepdims=True)
    spread = jnp.mean(centre * centre, axis=-1, keepdims=True)
    inverse = lax.rsqrt(spread + NORM_EPS)
    return centre * inverse, inverse


def norm_back(unit, inverse, grad):
    along = jnp.mean(grad * unit, axis=-1, keepdims=True)
    return inverse * (grad - jnp.mean(grad, axis=-1, keepdims=True) - unit * along)


def together(*values):
    return lax.optimization_barrier(values)


def exchange(parts, axes="hd"):
    return lax.all_to_all(parts, axes, split_axis=0, concat_axis=0, tiled=True)


def swapped(value, axis):
    return lax.ppermute(value, axis, SWAP)


def over_groups(mine):
    if lax.axis_size("kk") > 1:
        return lax.all_gather(mine, "kk", axis=0, tiled=False)
    return mine[None]


def sum_groups(parts):
    if lax.axis_size("kk") > 1:
        return lax.psum_scatter(parts, "kk", scatter_dimension=0, tiled=False)
    return parts[0]


def pair_sum(keep, give, axis):
    return (keep.astype(f32) + swapped(give, axis).astype(f32)).astype(bf)


def spread_pair(mine):
    pair = jnp.stack([mine, swapped(mine, "ry")])
    return pair, swapped(pair, "rc")


def chip_pair(mine):
    return jnp.concatenate([mine, swapped(mine, "rc")], axis=0)


def sum_pair(own, peer):
    total = pair_sum(own, peer, "rc")
    return pair_sum(total[0], total[1], "ry")


def ordered(mine, axis, dim):
    return pair_order(mine, swapped(mine, axis), axis, dim)


def pair_order(mine, got, axis, dim):
    is_first = lax.axis_index(axis) == 0
    return jnp.stack([jnp.where(is_first, mine, got), jnp.where(is_first, got, mine)], axis=dim)


def scattered(parts, axis, dim):
    me = lax.axis_index(axis)
    keep = lax.dynamic_index_in_dim(parts, me, dim, keepdims=False)
    give = lax.dynamic_index_in_dim(parts, 1 - me, dim, keepdims=False)
    return pair_sum(keep, give, axis)


def ring_step(up, down):
    return lax.ppermute(up, "hd", UP), lax.ppermute(down, "hd", DOWN)


def ring_order():
    position = jnp.array([RING.index(i) for i in range(HEADS)], jnp.int32)[lax.axis_index("hd")]
    offsets = jnp.array([o for step in STEPS for o in step], jnp.int32)
    return jnp.array(RING, jnp.int32)[(position + offsets) % HEADS]


def wide_scattered(parts, axis, dim):
    me = lax.axis_index(axis)
    keep = lax.dynamic_index_in_dim(parts, me, dim, keepdims=False)
    return keep + swapped(lax.dynamic_index_in_dim(parts, 1 - me, dim, keepdims=False), axis)


def traded(parts, axis, dim):
    me = lax.axis_index(axis)
    got = swapped(lax.dynamic_index_in_dim(parts, 1 - me, dim, keepdims=True), axis)
    return lax.dynamic_update_slice_in_dim(parts, got, 1 - me, dim)


def index_codes(slots, buckets, slot_rows):
    first_bucket = slots // slot_rows * BUCKETS
    return jnp.concatenate([slots // 256, slots % 256, buckets - first_bucket]).astype(bf)


def sorted_layout(codes, slot_rows, own_spans):
    heads = lax.axis_size("hd")
    codes = codes.astype(jnp.int32)
    slot_grid = codes[:, :, 0] * 256 + codes[:, :, 1]
    before = lax.axis_index("kk") * heads - 1
    target = slot_grid // slot_rows
    block = target - before
    local_place = slot_grid - target * slot_rows
    category = (block * (BUCKETS + 1) + codes[:, :, 2]).reshape(1, -1)
    categories = jnp.arange((heads + 1) * (BUCKETS + 1), dtype=jnp.int32)[:, None]
    members = jnp.sum((category == categories).astype(jnp.int32), axis=1)
    members = members.reshape(heads + 1, BUCKETS + 1)
    counts = jnp.sum(members, axis=1)
    last_start = jnp.maximum(counts[:1] - 1, 0) // SPAN * SPAN
    span_counts = -(-counts[1:] // SPAN)
    own_start = (1 + jnp.cumsum(span_counts) - span_counts) * SPAN
    start = jnp.concatenate([-last_start, own_start])
    lowest = jnp.concatenate([last_start, jnp.zeros_like(own_start)])
    dump = (own_spans + 1) * SPAN
    numbers = jnp.arange(heads + 1, dtype=jnp.int32)[:, None]
    local_place, block = local_place.reshape(1, -1), block.reshape(1, -1)
    here = (block == numbers) & (local_place >= lowest[:, None])
    place = jnp.sum(jnp.where(here, local_place + start[:, None] - dump, 0), axis=0) + dump
    ends = (start[:, None] + jnp.cumsum(members, axis=1)).reshape(-1, 1)
    rows = jnp.arange(dump, dtype=jnp.int32)[None, :]
    passed = jnp.sum((ends <= rows).astype(jnp.int32), axis=0)
    row_block = jnp.sum((own_start[:, None] <= rows).astype(jnp.int32), axis=0)
    local_bucket = passed - row_block * (BUCKETS + 1)
    row_bucket = jnp.where(
        local_bucket <= BUCKETS, (before + row_block) * BUCKETS + local_bucket, -1
    )
    span_bucket = row_bucket.astype(f32).reshape(-1, SPAN)
    return place, jnp.concatenate([span_bucket[:-1], span_bucket[1:]], axis=1)


def chunk_tables(groups):
    order = ring_order()
    flip = jnp.stack([lax.axis_index("rc"), lax.axis_index("ry")])

    def number(dc, dy, kk, hd):
        return ((hd * groups + kk) * 2 + (dy ^ flip[1])) * 2 + (dc ^ flip[0])

    def column(values):
        return jnp.array(values, jnp.int32)

    offsets = [list(range(sum(map(len, STEPS[:i])), sum(map(len, STEPS[: i + 1])))) for i in range(len(STEPS))]
    coming = [
        (dc, dy, kk, at)
        for dc in range(2)
        for part in offsets
        for dy in range(2)
        for kk in range(groups)
        for at in part
    ]
    going = [
        (dc, dy, kk, hd)
        for dc in range(2)
        for dy in range(2)
        for kk in range(groups)
        for hd in range(HEADS)
    ]
    dc, dy, kk, at = map(column, zip(*coming))
    in_table = number(dc, dy, kk, order[at])
    return in_table, number(*map(column, zip(*going)))


def per_device(
    first_half,
    second_half,
    qk_weight,
    value_weight,
    output_weight,
    inner_weight,
    outer_weight,
    attn_gain,
    attn_shift,
    ffn_gain,
    ffn_shift,
    buckets,
    slots,
    first_grad,
    second_grad,
):
    heads = lax.axis_size("hd")
    groups = lax.axis_size("kk")
    seq_count = heads * groups
    round_count = lax.axis_size("ry") * lax.axis_size("rc")
    device_count = seq_count * round_count
    own_rows, model_width = first_half.shape
    weight_rows, hidden_width = inner_weight.shape
    group_rows = own_rows * round_count
    slot_rows = 2 * group_rows
    tokens = group_rows * seq_count
    own_spans = min((tokens + (SPAN - 1) * heads) // SPAN, heads * slot_rows // SPAN)
    own_spans = -(-own_spans // UNROLL) * UNROLL
    piece = hidden_width // device_count
    blocks = own_rows // TOKB
    both = 2 * HEADD

    vectors = jnp.stack([attn_gain, attn_shift, ffn_gain, ffn_shift], axis=1)
    vectors = jnp.pad(vectors, ((0, 0), (0, HEADD - 4)))
    wide = both + HEADD
    head_shard = jnp.concatenate(
        [
            qk_weight.reshape(weight_rows, heads, HEADD),
            value_weight.reshape(weight_rows, heads, HEADD),
            jnp.broadcast_to(vectors[:, None], (weight_rows, heads, HEADD)),
        ],
        axis=2,
    )
    code_rows = 3 * group_rows // wide
    codes = index_codes(slots, buckets, slot_rows).reshape(code_rows, wide)
    codes = jnp.pad(codes, ((0, -code_rows % PAD), (0, 0)))
    codes = jnp.broadcast_to(codes[None], (heads,) + codes.shape)
    starter = jnp.concatenate([jnp.transpose(head_shard, (1, 0, 2)), codes], axis=1)

    second_later, starter = together(second_half, starter)
    second_in = second_later.astype(f32)
    unit, unit_scale = normalised(second_in)
    unit_low = unit.astype(bf)
    inner_split = inner_weight.reshape(weight_rows, seq_count, round_count, piece)
    inner_split = jnp.transpose(inner_split, (2, 0, 1, 3)).reshape(2, 2, weight_rows, -1)
    ring = [(unit_low,)]
    up, down = ring_step(unit_low, unit_low)
    inner_rows = traded(traded(inner_split, "rc", 1), "ry", 0)
    cut = round_count * weight_rows
    output_rows = ordered(ordered(output_weight, "rc", 0), "ry", 0).reshape(cut, model_width)
    shard = jnp.stack([inner_rows.reshape(cut, -1), outer_weight, output_rows])
    up, down, starter, shard = together(up, down, exchange(starter), shard)
    ring.append((up, down))

    up, down = ring_step(up, down)
    starter = jnp.transpose(over_groups(starter), (1, 0, 2, 3))
    codes = starter[:, :, weight_rows : weight_rows + code_rows].reshape(heads, groups, 3, -1)
    head_weight = ordered(ordered(starter[:, :, :weight_rows], "ry", 2), "rc", 3)
    head_weight = head_weight.reshape(model_width, wide)
    vectors_full = head_weight[:, both : both + 4].astype(f32)
    attn_gain_col, attn_shift_col = vectors_full[:, :1], vectors_full[:, 1:2]
    ffn_gain_row, ffn_shift_row = vectors_full[:, 2][None], vectors_full[:, 3][None]
    head_float = head_weight[:, :both].astype(f32)
    head_scaled = (head_float * attn_gain_col).astype(bf)
    head_offset = jnp.sum(head_float * attn_shift_col, axis=0, keepdims=True)
    up, down, head_scaled, head_offset, shard, second_later = together(
        up, down, head_scaled, head_offset, shard, second_grad
    )
    ring.append((up, down))

    def head_part(parts):
        rows = [product(part, head_scaled) + head_offset for part in parts]
        return over_groups(jnp.concatenate(rows, axis=0).astype(bf))

    up, down = ring_step(up, down)
    first_heads = head_part([part for step in ring for part in step])
    up, down, codes, shard = together(up, down, codes, shard)
    ring.append((up, down))

    half = own_rows // 2
    up, down = ring_step(up[:half], down[half:])
    up, down, first_swapped = together(up, down, swapped(first_heads, "ry"))
    ring.append((up, down))
    last_heads = head_part(ring[3] + ring[4])
    head_own = [first_heads, first_swapped, last_heads, swapped(last_heads, "ry")]
    head_own = jnp.concatenate([part.reshape(-1, both) for part in head_own], axis=0)
    place, key_bucket = sorted_layout(codes, slot_rows, own_spans)
    in_table, out_table = chunk_tables(groups)
    head_own, place, key_bucket, in_table, out_table = together(
        head_own, place, key_bucket, in_table, out_table
    )
    head_peer = swapped(head_own, "rc")

    grad_peer = swapped(second_later, "rc")
    grad_far = swapped(second_later, "ry")
    grad_last = swapped(grad_far, "rc")
    shards = lax.all_gather(shard, SEQ, axis=0, tiled=False)

    payload_own, payload_peer, sorted_q, sorted_k, sorted_v, probs, token_sums = attend_forward(
        in_table,
        out_table,
        place,
        key_bucket,
        head_own,
        head_peer,
        own_rows,
    )
    packed = (2, groups, heads, own_rows + PAD, HEADD)
    head_sums = sum_pair(payload_own.reshape(packed), payload_peer.reshape(packed))
    mixed_parts = exchange(sum_groups(head_sums))
    mixed_parts, shards = together(mixed_parts, shards)
    mixed, mixed_low, first_sum, ffn_unit, ffn_scale, ffn_low = mix_rows(
        mixed_parts, shards, first_half, ffn_gain_row, ffn_shift_row
    )
    ffn_low, qkv_rows = together(ffn_low, jnp.stack([qk_weight, value_weight]))
    qkv_rows = exchange(jnp.broadcast_to(qkv_rows[None], (heads,) + qkv_rows.shape))
    ffn_far = swapped(ffn_low, "ry")
    pair = feed_forward(ffn_low, swapped(ffn_low, "rc"), second_later, grad_peer, shards)
    ffn_far, pair = together(ffn_far, pair)
    far = feed_forward(ffn_far, swapped(ffn_far, "rc"), grad_far, grad_last, shards)
    pair, far = together(pair, far)
    ffn_pair, grad_pair, hidden_pair, inner_pair, *back_pair = pair
    ffn_far, grad_far, hidden_far, inner_far, *back_far = far
    far_sum = swapped(pair_sum(back_far[0], back_far[1], "rc"), "ry")
    near_sum = pair_sum(back_pair[0], back_pair[1], "rc")
    second_far = pair_sum(back_far[2], back_far[3], "rc")
    second_pair = pair_sum(back_pair[2], back_pair[3], "rc")
    outer_part = (against(hidden_pair, grad_pair) + against(hidden_far, grad_far)).astype(bf)
    inner_part = (against(ffn_pair, inner_pair) + against(ffn_far, inner_far)).astype(bf)
    part_sums = jnp.stack(
        [
            inner_part.reshape(seq_count, cut, -1),
            outer_part.reshape(seq_count, -1, model_width),
        ],
        axis=1,
    )
    near_sum, far_sum, part_sums, qkv_rows = together(near_sum, far_sum, part_sums, qkv_rows)
    part_grads = lax.psum_scatter(part_sums, SEQ, scatter_dimension=0, tiled=False)
    carry_low, back_parts = carry_rows(
        near_sum,
        far_sum,
        ffn_gain_row,
        ffn_unit,
        ffn_scale,
        first_grad,
        shards,
        mixed,
        mixed_parts,
    )
    back_parts = exchange(back_parts)
    output_part = against(mixed_low, carry_low).astype(bf)
    output_part = output_part.reshape(heads, groups, 2, 2, weight_rows, model_width)
    output_part = scattered(scattered(output_part, "rc", 3), "ry", 2)
    back_parts, output_part, second_pair, second_far, qkv_rows = together(
        back_parts, output_part, second_pair, second_far, qkv_rows
    )
    qkv_rows = jnp.transpose(over_groups(qkv_rows), (2, 1, 0, 3, 4))
    back_own, back_peer = spread_pair(over_groups(back_parts))
    back_own, second_far, qkv_rows, output_part = together(
        back_own, second_far, qkv_rows, output_part
    )
    output_rows = exchange(sum_groups(jnp.transpose(output_part, (1, 0, 2, 3))))
    second_far = swapped(second_far, "ry")
    qkv_got = swapped(qkv_rows, "ry")
    query_value_own, query_value_peer = attend_backward(
        out_table,
        place,
        back_own.reshape(-1, HEADD),
        back_peer.reshape(-1, HEADD),
        token_sums,
        sorted_q,
        sorted_k,
        sorted_v,
        probs,
        own_rows,
    )
    vector_rows = back_parts[:, own_rows + 2 * blocks : own_rows + 2 * blocks + 2]
    packed = (2, groups, heads, own_rows, both)
    vector_rows = back_parts[:, own_rows + 2 * blocks : own_rows + 2 * blocks + 2]
    packed = (2, groups, heads, own_rows, both)
    query_value_peer, qkv_got, second_far, output_rows = together(
        query_value_peer, qkv_got, second_far, output_rows
    )
    second_sum = second_in + second_pair.astype(f32) + second_far.astype(f32)
    query_value_own = query_value_own.reshape(packed)
    query_value_peer = swapped(query_value_peer.reshape(packed), "rc")

    def summed(part):
        return (query_value_own[part].astype(f32) + query_value_peer[part].astype(f32)).astype(bf)

    head_send = summed(1)
    head_send, output_rows, vector_rows, qkv_rows, qkv_got = together(
        head_send, output_rows, vector_rows, qkv_rows, qkv_got
    )
    qkv_rows = pair_order(qkv_rows, qkv_got, "ry", 3)
    qkv_full = ordered(qkv_rows, "rc", 4).reshape(2, model_width, model_width)
    head_got, qkv_full, head_keep = together(swapped(head_send, "ry"), qkv_full, summed(0))
    output_grad = jnp.sum(output_rows.astype(f32), axis=0)
    head_back = sum_groups(add_rows(head_keep, head_got))
    own_back = exchange(head_back)
    vector_sums = jnp.sum(vector_rows.astype(f32), axis=0)
    if groups > 1:
        vector_sums = lax.psum_scatter(
            vector_sums.reshape(2, groups, -1), "kk", scatter_dimension=1, tiled=False
        )
    vector_sums = jnp.pad(
        vector_sums.reshape(2, 2, 2, weight_rows), ((0, 6), (0, 0), (0, 0), (0, HEADD - weight_rows))
    )
    pieces = [part for step in ring for part in step]
    qkv_part, col_part = weight_part(ring_order(), head_back, pieces)
    qkv_part = qkv_part.reshape(heads, groups, 2, 2, weight_rows, both)
    col_part = jnp.broadcast_to(col_part[0], (heads, groups, 2, 2, PAD, both))
    qkv_part = jnp.concatenate([qkv_part, col_part], axis=4).astype(bf)
    qkv_part = scattered(scattered(qkv_part, "rc", 3), "ry", 2)
    qkv_part = sum_groups(jnp.transpose(qkv_part, (1, 0, 2, 3)))
    outer_grad = part_grads[1].astype(f32)
    turned = part_grads[0].reshape(2, 2, weight_rows, -1)
    turned = traded(traded(turned, "ry", 0), "rc", 1)
    vector_sums = wide_scattered(wide_scattered(vector_sums, "rc", 2), "ry", 1)
    vector_grads = vector_sums[:2, :weight_rows]
    own_back, qkv_part, turned = together(own_back, qkv_part, turned)
    inner_cols = turned.reshape(round_count, weight_rows, seq_count, piece)
    inner_grad = jnp.transpose(inner_cols, (1, 2, 0, 3)).reshape(weight_rows, hidden_width)
    qkv_rows = exchange(qkv_part).astype(f32)
    qkv_rows = qkv_rows.reshape(heads, weight_rows + PAD, 2, HEADD)
    qkv_rows = jnp.transpose(qkv_rows, (2, 1, 0, 3)).reshape(2, weight_rows + PAD, model_width)
    unit_grads, col_sums = qkv_rows[:, :weight_rows], qkv_rows[:, weight_rows]
    own_weights = jnp.stack([qk_weight, value_weight]).astype(f32)
    gain_own = attn_gain.astype(f32)[:, None]
    shift_own = attn_shift.astype(f32)[:, None]
    qkv_grads = unit_grads * gain_own + shift_own * col_sums[:, None]
    attn_gain_grad = jnp.sum(own_weights * unit_grads, axis=(0, 2))
    attn_shift_grad = jnp.sum(own_weights * col_sums[:, None], axis=(0, 2))

    second_carry = last_rows(
        own_back, qkv_full, attn_gain_col.reshape(1, -1), unit, unit_scale, second_grad
    )

    return (
        first_sum,
        second_sum.astype(bf),
        carry_low,
        second_carry,
        qkv_grads[0],
        qkv_grads[1],
        output_grad,
        inner_grad.astype(f32),
        outer_grad,
        attn_gain_grad,
        attn_shift_grad,
        vector_grads[0],
        vector_grads[1],
    )


def solution(mesh):
    seq_count, round_count = mesh.devices.shape
    shape = (HEADS, seq_count // HEADS, round_count // 2, 2)
    split_mesh = Mesh(mesh.devices.reshape(shape), ALL)
    rows = P(ALL, None)
    vector = P(ALL)
    table = P(ROUND, SEQ)
    in_specs = (rows,) * 7 + (vector,) * 4 + (table,) * 2 + (rows,) * 2
    out_specs = (rows,) * 9 + (vector,) * 4
    return jax.shard_map(
        per_device, mesh=split_mesh, in_specs=in_specs, out_specs=out_specs, check_vma=False
    )
```

```python
import functools
import math

import jax
import jax.numpy as jnp
from jax import lax
from jax.experimental import pallas as pl
from jax.experimental.pallas import tpu as pltpu
from jax.sharding import Mesh
from jax.sharding import PartitionSpec as P

HEADS = 8
NORM_EPS = 1e-05
SPAN = 64
HEADD = 128
PAD = 16
UNROLL = 34
TOKB = 128
BUCKETS = 32
CHUNK = 4096
VMEM_LIMIT = 60 * 2**20
KEY_EPS = 1e-06
bf = jnp.bfloat16
f32 = jnp.float32


def product(left_side, right_side):
    return jnp.dot(left_side, right_side, preferred_element_type=f32)


def against(left_side, right_side):
    return lax.dot_general(
        left_side, right_side, (((0,), (0,)), ((), ())), preferred_element_type=f32
    )


def through(left_side, right_side):
    return lax.dot_general(
        left_side, right_side, (((1,), (1,)), ((), ())), preferred_element_type=f32
    )


def takes(microseconds):
    return pl.CostEstimate(
        flops=int(microseconds * 1e8), bytes_accessed=int(microseconds * 3e6), transcendentals=0
    )


def aligned(start, size, step=SPAN):
    return pl.ds(pl.multiple_of(start, step), size)


def fill(ref, value):
    def body(step, carry):
        ref[aligned(step * SPAN, SPAN), :] = jnp.full((SPAN, ref.shape[1]), value, ref.dtype)
        return carry

    lax.fori_loop(0, ref.shape[0] // SPAN, body, 0)


def diagonal():
    rows = lax.broadcasted_iota(jnp.int32, (TOKB, TOKB), 0)
    return rows == lax.broadcasted_iota(jnp.int32, (TOKB, TOKB), 1)


def lanes(row, eye, ones):
    high = row.astype(bf).astype(f32)
    parts = [jnp.where(eye, high, 0.0), jnp.where(eye, row - high, 0.0)]
    return product(jnp.concatenate(parts, axis=1).astype(bf), ones)


def forward_kernel(
    own_rows,
    load_steps,
    in_ref,
    out_ref,
    place_ref,
    bucket_ref,
    own_ref,
    peer_ref,
    pay_own_ref,
    pay_peer_ref,
    query_out,
    key_out,
    value_out,
    prob_out,
    sum_ref,
    query_ref,
    key_ref,
    value_ref,
    prob_ref,
    wide_a,
    wide_b,
    stage_a,
    stage_b,
    sems,
):
    step = pl.program_id(0)
    leaving = [
        pltpu.make_async_copy(source, target, sems.at[number])
        for number, (source, target) in enumerate(
            [
                (query_ref, query_out),
                (key_ref, key_out),
                (value_ref, value_out),
                (prob_ref, prob_out),
            ]
        )
    ]
    own_spans = prob_ref.shape[0] // SPAN
    tail = SPAN * (own_spans + 1)

    @pl.when(step == 0)
    def _():
        fill(wide_a, 0.0)
        fill(wide_b, 0.0)

    def scatter_from(token_ref):
        def scatter(chunk, carry):
            both = token_ref[aligned(chunk * own_rows, own_rows, TOKB), :].astype(f32)
            stage_a[...] = both[:, :HEADD]
            stage_b[...] = both[:, HEADD:]
            first = in_ref[step * (CHUNK // own_rows) + chunk] * own_rows
            for row in range(own_rows):
                place = place_ref[first + row]
                wide_a[pl.ds(place, 1), :] = stage_a[row : row + 1, :]
                wide_b[pl.ds(place, 1), :] = stage_b[row : row + 1, :]
            return carry

        lax.fori_loop(0, CHUNK // own_rows, scatter, 0)

    pl.when(step < load_steps // 2)(lambda: scatter_from(own_ref))
    pl.when((step >= load_steps // 2) & (step < load_steps))(lambda: scatter_from(peer_ref))

    def unit_keys(query):
        square = jnp.sum(query * query, axis=-1, keepdims=True)
        scale = lax.rsqrt(square * (1.0 / HEADD) + KEY_EPS) * HEADD**-0.5
        return (query * scale).astype(bf)

    @pl.when(step == load_steps)
    def _():
        query_ref[:SPAN, :] = wide_a[:SPAN, :].astype(bf)
        key_ref[:SPAN, :] = unit_keys(wide_a[:SPAN, :])
        value_ref[:SPAN, :] = wide_b[:SPAN, :].astype(bf)
        wide_a[:SPAN, :] = jnp.zeros((SPAN, HEADD), f32)
        wide_b[:SPAN, :] = jnp.zeros((SPAN, HEADD), f32)
        for ref in (query_ref, key_ref, value_ref):
            ref[pl.ds(tail, SPAN), :] = jnp.zeros((SPAN, HEADD), bf)
        ones = jnp.ones((2 * SPAN, HEADD), bf)
        row_ids = lax.broadcasted_iota(jnp.int32, (SPAN, 2 * SPAN), 0)
        lane_ids = lax.broadcasted_iota(jnp.int32, (SPAN, 2 * SPAN), 1)
        before, itself = lane_ids == row_ids, lane_ids == row_ids + SPAN

        def spans(group, carry):
            first = group * (UNROLL * SPAN)
            prev = aligned(first, SPAN)
            here = aligned(first + SPAN, UNROLL * SPAN)
            query_wide = wide_a[here, :]
            values = wide_b[here, :].astype(bf)
            keys = jnp.concatenate([key_ref[prev, :], unit_keys(query_wide)], axis=0)
            seen = jnp.concatenate([value_ref[prev, :], values], axis=0)
            query = query_wide.astype(bf)
            key_buckets, columns = [], []
            for span in range(UNROLL):
                row = bucket_ref[pl.ds(group * UNROLL + span, 1), :]
                high = row.astype(bf).astype(f32)
                low = pltpu.roll(row - high, SPAN, 1)
                key_buckets.append(row)
                columns.append(jnp.where(itself, high, jnp.where(before, low, 0.0)).astype(bf))
            columns = product(jnp.concatenate(columns, axis=0), ones)
            raised = []
            for span in range(UNROLL):
                mine = slice(span * SPAN, (span + 1) * SPAN)
                both = slice(span * SPAN, (span + 2) * SPAN)
                same = columns[mine] == key_buckets[span]
                matches = jnp.sum(jnp.where(same, 1.0, 0.0), axis=-1, keepdims=True)
                allowed = same & (jnp.logical_not(itself) | (matches < 1.5))
                scores = through(query[mine], keys[both])
                raised.append(jnp.where(allowed, jnp.exp(scores), 0.0))
            lows = [member.astype(bf) for member in raised]
            totals = product(jnp.concatenate(lows, axis=0), ones)
            results = []
            for span in range(UNROLL):
                mine = slice(span * SPAN, (span + 1) * SPAN)
                both = slice(span * SPAN, (span + 2) * SPAN)
                total = totals[mine]
                inverse = jnp.where(total > 0.0, 1.0 / total, 0.0)
                probs = (raised[span] * inverse).astype(bf)
                results.append((product(lows[span], seen[both]), total, probs))
            query_ref[here, :] = query
            key_ref[here, :] = keys[SPAN:]
            value_ref[here, :] = values
            for span, (weighted, total, probs) in enumerate(results):
                at = aligned(first + (span + 1) * SPAN, SPAN)
                wide_a[at, :] = weighted
                wide_b[at, :] = total
                prob_ref[aligned(first + span * SPAN, SPAN), :] = probs
            return carry

        lax.fori_loop(0, own_spans // UNROLL, spans, 0)
        for copy in leaving:
            copy.start()
        wide_a[pl.ds(tail, SPAN), :] = jnp.zeros((SPAN, HEADD), f32)
        wide_b[pl.ds(tail, SPAN), :] = jnp.zeros((SPAN, HEADD), f32)

    def collect_to(pay_ref):
        blocks = own_rows // TOKB
        per_step = CHUNK // own_rows
        eye = diagonal()
        sum_rows = lax.broadcasted_iota(jnp.int32, (PAD, TOKB), 0)
        offset = (step - load_steps - 1) * per_step

        def collect(chunk, carry):
            first = chunk * (own_rows + PAD)
            sums = jnp.zeros((PAD, TOKB), f32)
            start = out_ref[offset + chunk] * own_rows
            for row in range(own_rows):
                place = place_ref[start + row]
                stage_a[row : row + 1, :] = wide_a[pl.ds(place, 1), :]
                stage_b[row : row + 1, :] = wide_b[pl.ds(place, 1), :]
            pay_ref[aligned(first, own_rows, PAD), :] = stage_a[...].astype(bf)
            for block in range(blocks):
                wide_sums = stage_b[block * TOKB : (block + 1) * TOKB, :]
                packed = jnp.sum(jnp.where(eye, wide_sums, 0.0), axis=0, keepdims=True)
                sum_ref[pl.ds(chunk * blocks + block, 1), :] = packed
                sums = jnp.where(sum_rows == block, packed, sums)
            pay_ref[aligned(first + own_rows, PAD, PAD), :] = sums.astype(bf)
            return carry

        lax.fori_loop(0, per_step, collect, 0)

    half = load_steps + 1 + load_steps // 2
    pl.when((step > load_steps) & (step < half))(lambda: collect_to(pay_own_ref))
    pl.when(step >= half)(lambda: collect_to(pay_peer_ref))

    @pl.when(step == 2 * load_steps)
    def _():
        for copy in leaving:
            copy.wait()


def part_spec(shape, first, count):
    return pl.BlockSpec(shape, lambda step: (jnp.clip(step - first, 0, count - 1), 0))


def attend_forward(in_table, out_table, place, key_bucket, own, peer, own_rows):
    tokens = place.shape[0]
    steps = tokens // CHUNK
    half = steps // 2
    own_spans = key_bucket.shape[0]
    rows = SPAN * (own_spans + 2)
    pay_rows = CHUNK // own_rows * (own_rows + PAD)
    once = pl.Buffered(1)

    def whole(shape):
        return pl.BlockSpec(shape, lambda step: (0, 0), pipeline_mode=once)

    sorted_rows = jax.ShapeDtypeStruct((rows, HEADD), bf)
    return pl.pallas_call(
        functools.partial(forward_kernel, own_rows, steps),
        grid=(2 * steps + 1,),
        out_shape=(
            jax.ShapeDtypeStruct((half * pay_rows, HEADD), bf),
            jax.ShapeDtypeStruct((half * pay_rows, HEADD), bf),
            sorted_rows,
            sorted_rows,
            sorted_rows,
            jax.ShapeDtypeStruct((own_spans * SPAN, 2 * SPAN), bf),
            jax.ShapeDtypeStruct((tokens // TOKB, TOKB), f32),
        ),
        in_specs=[
            pl.BlockSpec(memory_space=pltpu.SMEM),
            pl.BlockSpec(memory_space=pltpu.SMEM),
            pl.BlockSpec(memory_space=pltpu.SMEM),
            whole(key_bucket.shape),
            part_spec((CHUNK, 2 * HEADD), 0, half),
            part_spec((CHUNK, 2 * HEADD), half, half),
        ],
        out_specs=(
            part_spec((pay_rows, HEADD), steps + 1, half),
            part_spec((pay_rows, HEADD), steps + 1 + half, half),
            pl.BlockSpec(memory_space=pl.ANY),
            pl.BlockSpec(memory_space=pl.ANY),
            pl.BlockSpec(memory_space=pl.ANY),
            pl.BlockSpec(memory_space=pl.ANY),
            part_spec((CHUNK // TOKB, TOKB), steps + 1, steps),
        ),
        scratch_shapes=[pltpu.VMEM((rows, HEADD), bf)] * 3
        + [pltpu.VMEM((own_spans * SPAN, 2 * SPAN), bf)]
        + [pltpu.VMEM((rows, HEADD), f32)] * 2
        + [pltpu.VMEM((own_rows, HEADD), f32)] * 2
        + [pltpu.SemaphoreType.DMA((4,))],
        compiler_params=pltpu.CompilerParams(vmem_limit_bytes=VMEM_LIMIT),
        name="attend_forward",
        cost_estimate=takes(35),
    )(in_table, out_table, place, key_bucket, own, peer)


def backward_kernel(
    own_rows,
    load_steps,
    table_ref,
    place_ref,
    pay_own_ref,
    pay_peer_ref,
    sum_ref,
    query_in,
    key_in,
    value_in,
    prob_in,
    out_own_ref,
    out_peer_ref,
    query_ref,
    key_ref,
    value_ref,
    prob_ref,
    wide_a,
    wide_b,
    wide_c,
    stage_a,
    stage_b,
    sems,
):
    step = pl.program_id(0)
    coming = [
        pltpu.make_async_copy(source, target, sems.at[number])
        for number, (source, target) in enumerate(
            [(query_in, query_ref), (key_in, key_ref), (value_in, value_ref), (prob_in, prob_ref)]
        )
    ]
    own_spans = prob_ref.shape[0] // SPAN
    tail = SPAN * (own_spans + 1)

    @pl.when(step == 0)
    def _():
        for copy in coming:
            copy.start()
        fill(wide_a, 0.0)
        fill(wide_b, 0.0)

    def scatter_from(pay_ref):
        blocks = own_rows // TOKB
        eye = diagonal()
        ones = jnp.ones((2 * TOKB, TOKB), bf)

        def scatter(chunk, carry):
            first = chunk * (own_rows + PAD)
            extra = pay_ref[aligned(first + own_rows, PAD, PAD), :].astype(f32)
            for block in range(blocks):
                share = sum_ref[pl.ds(chunk * blocks + block, 1), :]
                share = share / extra[blocks + block : blocks + block + 1, :]
                rows = pay_ref[aligned(first + block * TOKB, TOKB, PAD), :].astype(f32)
                here = slice(block * TOKB, (block + 1) * TOKB)
                stage_a[here, :] = rows * lanes(share, eye, ones)
                stage_b[here, :] = lanes(share * extra[block : block + 1, :], eye, ones)
            start = table_ref[step * (CHUNK // own_rows) + chunk] * own_rows
            for row in range(own_rows):
                place = place_ref[start + row]
                wide_a[pl.ds(place, 1), :] = stage_a[row : row + 1, :]
                wide_b[pl.ds(place, 1), :] = stage_b[row : row + 1, :]
            return carry

        lax.fori_loop(0, CHUNK // own_rows, scatter, 0)

    pl.when(step < load_steps // 2)(lambda: scatter_from(pay_own_ref))
    pl.when((step >= load_steps // 2) & (step < load_steps))(lambda: scatter_from(pay_peer_ref))

    def pulled(query_low, d_query, d_keys):
        query = query_low.astype(f32)
        inverse = lax.rsqrt(
            jnp.sum(query * query, axis=-1, keepdims=True) * (1.0 / HEADD) + KEY_EPS
        )
        along = jnp.sum(query * d_keys, axis=-1, keepdims=True)
        scale = inverse * HEADD**-0.5
        return d_query + scale * d_keys - (scale * inverse * inverse * along * (1.0 / HEADD)) * query

    @pl.when(step == load_steps)
    def _():
        for copy in coming:
            copy.wait()
        for ref in (wide_a, wide_b, wide_c):
            ref[:SPAN, :] = jnp.zeros((SPAN, HEADD), f32)
        zero = jnp.zeros((SPAN, HEADD), bf)

        def spans(group, carry):
            first = group * (UNROLL * SPAN)
            prev = aligned(first, SPAN)
            own = aligned(first, UNROLL * SPAN)
            here = aligned(first + SPAN, UNROLL * SPAN)
            around = aligned(first, (UNROLL + 1) * SPAN)
            query = query_ref[around, :]
            keys = key_ref[around, :]
            values = value_ref[around, :]
            probs = prob_ref[own, :]
            d_out = wide_a[here, :].astype(bf)
            delta = wide_b[here, :]
            d_query = [wide_a[prev, :]]
            d_keys = [wide_b[prev, :]]
            d_values = [wide_c[prev, :]]
            for span in range(UNROLL):
                mine = slice(span * SPAN, (span + 1) * SPAN)
                after = slice((span + 1) * SPAN, (span + 2) * SPAN)
                both = slice(span * SPAN, (span + 2) * SPAN)
                d_probs = through(d_out[mine], values[both])
                prob = probs[mine]
                d_scores = (prob.astype(f32) * (d_probs - delta[mine])).astype(bf)
                d_query.append(product(d_scores, keys[both]))
                right = jnp.concatenate(
                    [
                        jnp.concatenate([query[after], zero], axis=1),
                        jnp.concatenate([zero, d_out[mine]], axis=1),
                    ],
                    axis=0,
                )
                pair = against(jnp.concatenate([d_scores, prob], axis=0), right)
                d_keys[-1] = d_keys[-1] + pair[:SPAN, :HEADD]
                d_values[-1] = d_values[-1] + pair[:SPAN, HEADD:]
                d_keys.append(pair[SPAN:, :HEADD])
                d_values.append(pair[SPAN:, HEADD:])
            for span in range(UNROLL + 1):
                at = aligned(first + span * SPAN, SPAN)
                wide_c[at, :] = d_values[span]
                if span < UNROLL:
                    rows = slice(span * SPAN, (span + 1) * SPAN)
                    wide_a[at, :] = pulled(query[rows], d_query[span], d_keys[span])
                else:
                    wide_a[at, :] = d_query[span]
                    wide_b[at, :] = d_keys[span]
            return carry

        lax.fori_loop(0, own_spans // UNROLL, spans, 0)
        last = pl.ds(tail - SPAN, SPAN)
        wide_a[last, :] = pulled(query_ref[last, :], wide_a[last, :], wide_b[last, :])
        wide_a[pl.ds(tail, SPAN), :] = jnp.zeros((SPAN, HEADD), f32)
        wide_c[pl.ds(tail, SPAN), :] = jnp.zeros((SPAN, HEADD), f32)

    def collect_to(out_ref):
        offset = (step - load_steps - 1) * (CHUNK // own_rows)

        def collect(chunk, carry):
            start = table_ref[offset + chunk] * own_rows
            for row in range(own_rows):
                place = place_ref[start + row]
                stage_a[row : row + 1, :] = wide_a[pl.ds(place, 1), :]
                stage_b[row : row + 1, :] = wide_c[pl.ds(place, 1), :]
            here = aligned(chunk * own_rows, own_rows, TOKB)
            out_ref[here, :HEADD] = stage_a[...].astype(bf)
            out_ref[here, HEADD:] = stage_b[...].astype(bf)
            return carry

        lax.fori_loop(0, CHUNK // own_rows, collect, 0)

    half = load_steps + 1 + load_steps // 2
    pl.when((step > load_steps) & (step < half))(lambda: collect_to(out_own_ref))
    pl.when(step >= half)(lambda: collect_to(out_peer_ref))


def attend_backward(out_table, place, pay_own, pay_peer, sums, query, keys, values, probs, own_rows):
    tokens = place.shape[0]
    steps = tokens // CHUNK
    half = steps // 2
    rows = query.shape[0]
    pay_rows = CHUNK // own_rows * (own_rows + PAD)
    out_half = jax.ShapeDtypeStruct((tokens // 2, 2 * HEADD), bf)
    return pl.pallas_call(
        functools.partial(backward_kernel, own_rows, steps),
        grid=(2 * steps + 1,),
        out_shape=(out_half, out_half),
        in_specs=[
            pl.BlockSpec(memory_space=pltpu.SMEM),
            pl.BlockSpec(memory_space=pltpu.SMEM),
            part_spec((pay_rows, HEADD), 0, half),
            part_spec((pay_rows, HEADD), half, half),
            part_spec((CHUNK // TOKB, TOKB), 0, steps),
            pl.BlockSpec(memory_space=pl.ANY),
            pl.BlockSpec(memory_space=pl.ANY),
            pl.BlockSpec(memory_space=pl.ANY),
            pl.BlockSpec(memory_space=pl.ANY),
        ],
        out_specs=(
            part_spec((CHUNK, 2 * HEADD), steps + 1, half),
            part_spec((CHUNK, 2 * HEADD), steps + 1 + half, half),
        ),
        scratch_shapes=[pltpu.VMEM((rows, HEADD), bf)] * 3
        + [pltpu.VMEM(probs.shape, bf)]
        + [pltpu.VMEM((rows, HEADD), f32)] * 3
        + [pltpu.VMEM((own_rows, HEADD), f32)] * 2
        + [pltpu.SemaphoreType.DMA((4,))],
        compiler_params=pltpu.CompilerParams(vmem_limit_bytes=VMEM_LIMIT),
        name="attend_backward",
        cost_estimate=takes(44),
    )(out_table, place, pay_own, pay_peer, sums, query, keys, values, probs)


def shard_spec(shards, number):
    block = (shards.shape[0], 1) + shards.shape[2:]
    return pl.BlockSpec(block, lambda *_: (0, number, 0, 0), pipeline_mode=pl.Buffered(1))


def whole_weight(ref):
    value = ref[...]
    return value.reshape(-1, value.shape[-1])


def feed_kernel(
    own_ref, peer_ref, grad_own_ref, grad_peer_ref, inner_weight_ref, outer_weight_ref,
    row_ref, grad_ref, hidden_ref, inner_ref,
    back_own_ref, back_peer_ref, second_own_ref, second_peer_ref,
):
    step = pl.program_id(0)

    @pl.when(step == 0)
    def _():
        row_ref[...] = own_ref[...]
        grad_ref[...] = grad_own_ref[...]

    @pl.when(step == 1)
    def _():
        row_ref[...] = peer_ref[...]
        grad_ref[...] = grad_peer_ref[...]

    weight = whole_weight(inner_weight_ref)
    outer_weight = whole_weight(outer_weight_ref)
    act = product(row_ref[...], weight)
    size = jnp.abs(act)
    bell = jnp.exp(act * act * -0.5)
    near = 1.0 / (1.0 + size * (0.3275911 * 0.5**0.5))
    tail = near * (0.254829592 + near * (-0.284496736 + near * (
        1.421413741 + near * (-1.453152027 + near * 1.061405429))))
    tail = tail * bell * 0.5
    normal = jnp.where(act >= 0.0, 1.0 - tail, tail)
    hidden = (act * normal).astype(bf)
    hidden_ref[...] = hidden
    slope = normal + act * bell * (2.0 * math.pi) ** -0.5
    inner = (through(grad_ref[...], outer_weight) * slope).astype(bf)
    inner_ref[...] = inner
    back = through(inner, weight).astype(bf)
    second = product(hidden, outer_weight).astype(bf)

    @pl.when(step == 0)
    def _():
        back_own_ref[...] = back
        second_own_ref[...] = second

    @pl.when(step == 1)
    def _():
        back_peer_ref[...] = back
        second_peer_ref[...] = second


def feed_forward(own, peer, grad_own, grad_peer, shards):
    count, width = own.shape
    units = shards.shape[3]

    def part(columns):
        return pl.BlockSpec((count, columns), lambda i: (i, 0))

    whole = pl.BlockSpec((count, width), lambda i: (0, 0), pipeline_mode=pl.Buffered(1))
    by_width = jax.ShapeDtypeStruct((2 * count, width), bf)
    by_units = jax.ShapeDtypeStruct((2 * count, units), bf)
    half = jax.ShapeDtypeStruct((count, width), bf)
    return pl.pallas_call(
        feed_kernel,
        grid=(2,),
        out_shape=(by_width, by_width, by_units, by_units, half, half, half, half),
        in_specs=[whole] * 4 + [shard_spec(shards, 0), shard_spec(shards, 1)],
        out_specs=(
            part(width), part(width), part(units), part(units), whole, whole, whole, whole
        ),
        compiler_params=pltpu.CompilerParams(vmem_limit_bytes=VMEM_LIMIT),
        name="feed_forward",
        cost_estimate=takes(9),
    )(own, peer, grad_own, grad_peer, shards, shards)


def mix_kernel(
    parts_ref, weight_ref, first_ref, gain_ref, shift_ref,
    low_ref, sum_ref, unit_ref, scale_ref, feed_ref,
):
    heads, rows = parts_ref.shape[0], first_ref.shape[0]
    eye = diagonal()
    ones = jnp.ones((2 * TOKB, TOKB), bf)
    for head in range(heads):
        columns = slice(head * HEADD, (head + 1) * HEADD)
        for block in range(rows // TOKB):
            here = slice(block * TOKB, (block + 1) * TOKB)
            sums = parts_ref[head, rows : rows + PAD, :].astype(f32)[block : block + 1]
            mixed = parts_ref[head, here, :].astype(f32) / lanes(sums, eye, ones)
            low_ref[here, columns] = mixed.astype(bf)
    total = first_ref[...].astype(f32) + product(low_ref[...], whole_weight(weight_ref))
    sum_ref[...] = total.astype(bf)
    centre = total - jnp.mean(total, axis=-1, keepdims=True)
    scale = lax.rsqrt(jnp.mean(centre * centre, axis=-1, keepdims=True) + NORM_EPS)
    unit = centre * scale
    unit_ref[...] = unit
    scale_ref[...] = scale
    feed_ref[...] = (unit * gain_ref[...] + shift_ref[...]).astype(bf)


def mix_rows(parts, shards, first_half, gain, shift):
    rows, width = first_half.shape
    vm = pl.BlockSpec(memory_space=pltpu.VMEM)
    wide, low = jax.ShapeDtypeStruct((rows, width), f32), jax.ShapeDtypeStruct((rows, width), bf)
    return pl.pallas_call(
        mix_kernel,
        out_shape=(low, low, wide, jax.ShapeDtypeStruct((rows, 1), f32), low),
        grid=(1,),
        in_specs=[vm, shard_spec(shards, 2), vm, vm, vm],
        out_specs=(vm,) * 5,
        compiler_params=pltpu.CompilerParams(vmem_limit_bytes=VMEM_LIMIT),
        name="mix_rows",
        cost_estimate=takes(5),
    )(parts, shards, first_half, gain, shift)


def carry_kernel(
    near_ref, far_ref, gain_ref, unit_ref, scale_ref, grad_ref, weight_ref, mixed_ref, parts_ref,
    carry_ref, pay_ref, wide_ref,
):
    heads, rows = parts_ref.shape[0], grad_ref.shape[0]
    blocks = rows // TOKB
    back = near_ref[...].astype(f32) + far_ref[...].astype(f32)
    unit = unit_ref[...]
    gain_sum = jnp.sum(back * unit, axis=0, keepdims=True)
    shift_sum = jnp.sum(back, axis=0, keepdims=True)
    grad = back * gain_ref[...]
    along = jnp.mean(grad * unit, axis=-1, keepdims=True)
    grad = scale_ref[...] * (grad - jnp.mean(grad, axis=-1, keepdims=True) - unit * along)
    carry_ref[...] = (grad_ref[...].astype(f32) + grad).astype(bf)
    wide_ref[...] = through(carry_ref[...], whole_weight(weight_ref))
    eye = diagonal()
    pad_rows = lax.broadcasted_iota(jnp.int32, (PAD, TOKB), 0)
    for head in range(heads):
        columns = slice(head * HEADD, (head + 1) * HEADD)
        sums = parts_ref[head, rows : rows + PAD, :].astype(f32)
        tails = jnp.zeros((PAD, TOKB), f32)
        for block in range(blocks):
            here = slice(block * TOKB, (block + 1) * TOKB)
            wide = wide_ref[here, columns]
            pay_ref[head, here, :] = wide.astype(bf)
            mixed = mixed_ref[here, columns].astype(f32)
            dot = jnp.sum(wide * mixed, axis=-1, keepdims=True)
            packed = jnp.sum(jnp.where(eye, dot, 0.0), axis=0, keepdims=True)
            tails = jnp.where(pad_rows == block, packed, tails)
            tails = jnp.where(pad_rows == blocks + block, sums[block : block + 1], tails)
        tails = jnp.where(pad_rows == 2 * blocks, gain_sum[:, columns], tails)
        tails = jnp.where(pad_rows == 2 * blocks + 1, shift_sum[:, columns], tails)
        pay_ref[head, rows : rows + PAD, :] = tails.astype(bf)


def carry_rows(near, far, gain, unit, scale, first_grad, shards, mixed, parts):
    rows, width = near.shape
    vm = pl.BlockSpec(memory_space=pltpu.VMEM)
    return pl.pallas_call(
        carry_kernel,
        out_shape=(
            jax.ShapeDtypeStruct((rows, width), bf),
            jax.ShapeDtypeStruct(parts.shape, bf),
        ),
        grid=(1,),
        in_specs=[vm] * 6 + [shard_spec(shards, 2)] + [vm] * 2,
        out_specs=(vm,) * 2,
        scratch_shapes=[pltpu.VMEM((rows, width), f32)],
        compiler_params=pltpu.CompilerParams(vmem_limit_bytes=VMEM_LIMIT),
        name="carry_rows",
        cost_estimate=takes(5),
    )(near, far, gain, unit, scale, first_grad, shards, mixed, parts)


def add_kernel(left_ref, right_ref, out_ref):
    total = left_ref[...].astype(f32) + right_ref[...].astype(f32)
    out_ref[...] = total.astype(out_ref.dtype)


def add_rows(left, right):
    shape = left.shape
    left, right = left.reshape(-1, shape[-1]), right.reshape(-1, shape[-1])
    step = math.gcd(left.shape[0], 1024)
    spec = pl.BlockSpec((step, shape[-1]), lambda i: (i, 0))
    out = pl.pallas_call(
        add_kernel,
        grid=(left.shape[0] // step,),
        out_shape=jax.ShapeDtypeStruct(left.shape, left.dtype),
        in_specs=[spec, spec],
        out_specs=spec,
        name="add_rows",
        cost_estimate=takes(3),
    )(left, right)
    return out.reshape(shape)


def last_kernel(
    back_ref, weight_ref, gain_ref, unit_ref, scale_ref, grad_ref, out_ref, query_ref, value_ref,
):
    for head in range(back_ref.shape[0]):
        columns = slice(head * HEADD, (head + 1) * HEADD)
        query_ref[:, columns] = back_ref[head, :, :HEADD]
        value_ref[:, columns] = back_ref[head, :, HEADD:]
    total = through(query_ref[...], weight_ref[0]) + through(value_ref[...], weight_ref[1])
    grad = total * gain_ref[...]
    unit = unit_ref[...]
    along = jnp.mean(grad * unit, axis=-1, keepdims=True)
    centred = grad - jnp.mean(grad, axis=-1, keepdims=True) - unit * along
    out_ref[...] = (grad_ref[...].astype(f32) + scale_ref[...] * centred).astype(bf)


def last_rows(own_back, weights, gain, unit, scale, second_grad):
    rows, width = unit.shape
    vm = pl.BlockSpec(memory_space=pltpu.VMEM)
    return pl.pallas_call(
        last_kernel,
        out_shape=jax.ShapeDtypeStruct((rows, width), bf),
        in_specs=[vm] * 6,
        out_specs=vm,
        scratch_shapes=[pltpu.VMEM((rows, width), bf)] * 2,
        compiler_params=pltpu.CompilerParams(vmem_limit_bytes=VMEM_LIMIT),
        name="last_rows",
        cost_estimate=takes(6),
    )(own_back, weights, gain, unit, scale, second_grad)


def weight_kernel(order_ref, back_ref, *refs):
    pieces, (part_ref, column_ref) = refs[:-2], refs[-2:]
    half = pieces[-1].shape[0]
    total = None
    for number, piece in enumerate(pieces[:-1]):
        back = back_ref[order_ref[number]]
        if piece.shape[0] == half:
            term = against(piece[...], back[:half]) + against(pieces[-1][...], back[half:])
        else:
            term = against(piece[...], back)
        total = term if total is None else total + term
    part_ref[...] = total
    columns = jnp.sum(back_ref[...].astype(f32), axis=(0, 1), keepdims=True)[0]
    column_ref[...] = jnp.broadcast_to(columns, column_ref.shape)


def weight_part(order, back, pieces):
    width = pieces[0].shape[1]
    vm = pl.BlockSpec(memory_space=pltpu.VMEM)
    return pl.pallas_call(
        weight_kernel,
        out_shape=(
            jax.ShapeDtypeStruct((width, back.shape[2]), f32),
            jax.ShapeDtypeStruct((8, back.shape[2]), f32),
        ),
        in_specs=[pl.BlockSpec(memory_space=pltpu.SMEM)] + [vm] * (1 + len(pieces)),
        out_specs=(vm, vm),
        compiler_params=pltpu.CompilerParams(vmem_limit_bytes=VMEM_LIMIT),
        name="weight_part",
        cost_estimate=takes(5),
    )(order, back, *pieces)


def layout_kernel(
    heads, slot_rows, first_ref, code_ref, place_ref, bucket_ref, start_ref, low_ref, end_ref
):
    sources = code_ref.shape[0]
    rows = place_ref.shape[0] // sources
    own_spans = bucket_ref.shape[0]
    categories = BUCKETS + 1
    before = first_ref[0].astype(f32)
    codes = code_ref[...].astype(f32)[:, :rows].reshape(sources * rows, 3 * TOKB)
    slots = codes[:, :TOKB] * 256.0 + codes[:, TOKB : 2 * TOKB]
    buckets = codes[:, 2 * TOKB :]
    target = jnp.floor(slots * (1.0 / slot_rows))
    block = target - before
    local = slots - target * slot_rows
    block_ids = lax.broadcasted_iota(jnp.int32, (16, TOKB), 0).astype(f32)
    bucket_ids = lax.broadcasted_iota(jnp.int32, (TOKB, TOKB), 0).astype(f32)
    counts = jnp.zeros((16, TOKB), f32)
    for row in range(sources * rows):
        left = jnp.where(block_ids == block[row : row + 1], 1.0, 0.0).astype(bf)
        right = jnp.where(bucket_ids == buckets[row : row + 1], 1.0, 0.0).astype(bf)
        counts += through(left, right)
    lane_ids = lax.broadcasted_iota(jnp.int32, (16, TOKB), 1)
    row_ids = lax.broadcasted_iota(jnp.int32, (16, TOKB), 0)
    total = jnp.broadcast_to(jnp.sum(counts, axis=1, keepdims=True), counts.shape)
    step = 1
    while step < categories:
        counts += jnp.where(lane_ids >= step, pltpu.roll(counts, step, 1), 0.0)
        step *= 2
    spans = jnp.where(row_ids == 0, 0.0, jnp.floor((total + (SPAN - 1)) * (1.0 / SPAN)))
    start = spans
    step = 1
    while step < 16:
        start += jnp.where(row_ids >= step, pltpu.roll(start, step, 0), 0.0)
        step *= 2
    start = (start - spans + 1.0) * SPAN
    last_start = jnp.floor(jnp.maximum(total - 1.0, 0.0) * (1.0 / SPAN)) * SPAN
    start = jnp.where(row_ids == 0, -last_start, start)
    start_ref[...] = start
    low_ref[...] = jnp.where(row_ids == 0, last_start, 0.0)
    unused = (row_ids > heads) | (lane_ids >= categories)
    ends = jnp.where(unused, 1e9, start + counts)
    for bucket in range(categories):
        wide = jnp.sum(jnp.where(lane_ids == bucket, ends, 0.0), axis=1, keepdims=True)
        end_ref[bucket] = jnp.broadcast_to(wide, ends.shape)
    place = jnp.full(local.shape, (own_spans + 1.0) * SPAN, f32)
    for number in range(heads + 1):
        here = (block == float(number)) & (local >= low_ref[number : number + 1, :])
        place = jnp.where(here, local + start_ref[number : number + 1, :], place)
    place_ref[...] = place.astype(jnp.int32)
    shape = (own_spans, TOKB)
    at = lax.broadcasted_iota(jnp.int32, shape, 0) * SPAN + lax.broadcasted_iota(jnp.int32, shape, 1)
    at = at.astype(f32)
    block_number = jnp.zeros(shape, f32)
    for number in range(1, heads + 1):
        block_number += jnp.where(at >= start_ref[number : number + 1, :], 1.0, 0.0)
    passed = -block_number * categories

    def count(bucket, passed):
        for number in range(heads + 1):
            passed += jnp.where(at >= end_ref[bucket, number : number + 1, :], 1.0, 0.0)
        return passed

    passed = lax.fori_loop(0, categories, count, passed)
    bucket_ref[...] = jnp.where(
        passed <= BUCKETS, (before + block_number) * BUCKETS + passed, -1.0
    )


def sorted_layout(first, codes, heads, slot_rows, own_spans, rows):
    sources = codes.shape[0]
    vm = pl.BlockSpec(memory_space=pltpu.VMEM)
    return pl.pallas_call(
        functools.partial(layout_kernel, heads, slot_rows),
        out_shape=(
            jax.ShapeDtypeStruct((sources * rows, TOKB), jnp.int32),
            jax.ShapeDtypeStruct((own_spans, 2 * SPAN), f32),
        ),
        in_specs=[pl.BlockSpec(memory_space=pltpu.SMEM), vm],
        out_specs=(vm, vm),
        scratch_shapes=[
            pltpu.VMEM((16, TOKB), f32),
            pltpu.VMEM((16, TOKB), f32),
            pltpu.VMEM((BUCKETS + 1, 16, TOKB), f32),
        ],
        compiler_params=pltpu.CompilerParams(vmem_limit_bytes=VMEM_LIMIT),
        name="sorted_layout",
        cost_estimate=takes(5),
    )(first, codes)


def parts_kernel(
    row_pair_ref, row_far_ref, inner_pair_ref, inner_far_ref,
    hidden_pair_ref, hidden_far_ref, grad_pair_ref, grad_far_ref, out_ref,
):
    inner = against(row_pair_ref[...], inner_pair_ref[...])
    inner += against(row_far_ref[...], inner_far_ref[...])
    out_ref[0, 0] = inner.astype(bf)
    outer = against(hidden_pair_ref[...], grad_pair_ref[...])
    outer += against(hidden_far_ref[...], grad_far_ref[...])
    out_ref[0, 1] = outer.astype(bf)


def parts_product(row_pair, row_far, inner_pair, inner_far, hidden_pair, hidden_far, grads):
    rows, width = row_pair.shape
    units = hidden_pair.shape[1]
    block = pl.BlockSpec((rows, TOKB), lambda i: (0, i))

    def whole(columns):
        return pl.BlockSpec((rows, columns), lambda i: (0, 0), pipeline_mode=pl.Buffered(1))

    return pl.pallas_call(
        parts_kernel,
        grid=(width // TOKB,),
        out_shape=jax.ShapeDtypeStruct((width // TOKB, 2, TOKB, width), bf),
        in_specs=[block, block, whole(units), whole(units), block, block]
        + [whole(width), whole(width)],
        out_specs=pl.BlockSpec((1, 2, TOKB, width), lambda i: (i, 0, 0, 0)),
        compiler_params=pltpu.CompilerParams(vmem_limit_bytes=VMEM_LIMIT),
        name="parts_product",
        cost_estimate=takes(0),
    )(row_pair, row_far, inner_pair, inner_far, hidden_pair, hidden_far, *grads)


ALL = ("hd", "kk", "ry", "rc")
SEQ = ("hd", "kk")
ROUND = ("ry", "rc")
SWAP = [(0, 1), (1, 0)]
RING = (0, 2, 4, 6, 7, 5, 3, 1)
UP = [(RING[i], RING[(i + 1) % HEADS]) for i in range(HEADS)]
DOWN = [(RING[(i + 1) % HEADS], RING[i]) for i in range(HEADS)]
STEPS = ((0, -1, 1, -2, 2), (-3, 3, 4))
BUCKETS = 32


def normalised(values):
    centre = values - jnp.mean(values, axis=-1, keepdims=True)
    spread = jnp.mean(centre * centre, axis=-1, keepdims=True)
    inverse = lax.rsqrt(spread + NORM_EPS)
    return centre * inverse, inverse


def norm_back(unit, inverse, grad):
    along = jnp.mean(grad * unit, axis=-1, keepdims=True)
    return inverse * (grad - jnp.mean(grad, axis=-1, keepdims=True) - unit * along)


def together(*values):
    return lax.optimization_barrier(values)


def exchange(parts, axes="hd"):
    return lax.all_to_all(parts, axes, split_axis=0, concat_axis=0, tiled=True)


def swapped(value, axis):
    return lax.ppermute(value, axis, SWAP)


def over_groups(mine):
    if lax.axis_size("kk") > 1:
        return lax.all_gather(mine, "kk", axis=0, tiled=False)
    return mine[None]


def sum_groups(parts):
    if lax.axis_size("kk") > 1:
        return lax.psum_scatter(parts, "kk", scatter_dimension=0, tiled=False)
    return parts[0]


def pair_sum(keep, give, axis):
    return (keep.astype(f32) + swapped(give, axis).astype(f32)).astype(bf)


def spread_pair(mine):
    pair = jnp.stack([mine, swapped(mine, "ry")])
    return pair, swapped(pair, "rc")


def chip_pair(mine):
    return jnp.concatenate([mine, swapped(mine, "rc")], axis=0)


def sum_pair(own, peer):
    total = pair_sum(own, peer, "rc")
    return pair_sum(total[0], total[1], "ry")


def ordered(mine, axis, dim):
    return pair_order(mine, swapped(mine, axis), axis, dim)


def pair_order(mine, got, axis, dim):
    is_first = lax.axis_index(axis) == 0
    return jnp.stack([jnp.where(is_first, mine, got), jnp.where(is_first, got, mine)], axis=dim)


def scattered(parts, axis, dim):
    me = lax.axis_index(axis)
    keep = lax.dynamic_index_in_dim(parts, me, dim, keepdims=False)
    give = lax.dynamic_index_in_dim(parts, 1 - me, dim, keepdims=False)
    return pair_sum(keep, give, axis)


def ring_step(up, down):
    return lax.ppermute(up, "hd", UP), lax.ppermute(down, "hd", DOWN)


def ring_order():
    position = jnp.array([RING.index(i) for i in range(HEADS)], jnp.int32)[lax.axis_index("hd")]
    offsets = jnp.array([o for step in STEPS for o in step], jnp.int32)
    return jnp.array(RING, jnp.int32)[(position + offsets) % HEADS]


def wide_scattered(parts, axis, dim):
    me = lax.axis_index(axis)
    keep = lax.dynamic_index_in_dim(parts, me, dim, keepdims=False)
    return keep + swapped(lax.dynamic_index_in_dim(parts, 1 - me, dim, keepdims=False), axis)


def traded(parts, axis, dim):
    me = lax.axis_index(axis)
    got = swapped(lax.dynamic_index_in_dim(parts, 1 - me, dim, keepdims=True), axis)
    return lax.dynamic_update_slice_in_dim(parts, got, 1 - me, dim)


def index_codes(slots, buckets, slot_rows):
    first_bucket = slots // slot_rows * BUCKETS
    return jnp.concatenate([slots // 256, slots % 256, buckets - first_bucket]).astype(bf)


def sorted_layout(codes, slot_rows, own_spans):
    heads = lax.axis_size("hd")
    codes = codes.astype(jnp.int32)
    slot_grid = codes[:, :, 0] * 256 + codes[:, :, 1]
    before = lax.axis_index("kk") * heads - 1
    target = slot_grid // slot_rows
    block = target - before
    local_place = slot_grid - target * slot_rows
    category = (block * (BUCKETS + 1) + codes[:, :, 2]).reshape(1, -1)
    categories = jnp.arange((heads + 1) * (BUCKETS + 1), dtype=jnp.int32)[:, None]
    members = jnp.sum((category == categories).astype(jnp.int32), axis=1)
    members = members.reshape(heads + 1, BUCKETS + 1)
    counts = jnp.sum(members, axis=1)
    last_start = jnp.maximum(counts[:1] - 1, 0) // SPAN * SPAN
    span_counts = -(-counts[1:] // SPAN)
    own_start = (1 + jnp.cumsum(span_counts) - span_counts) * SPAN
    start = jnp.concatenate([-last_start, own_start])
    lowest = jnp.concatenate([last_start, jnp.zeros_like(own_start)])
    dump = (own_spans + 1) * SPAN
    numbers = jnp.arange(heads + 1, dtype=jnp.int32)[:, None]
    local_place, block = local_place.reshape(1, -1), block.reshape(1, -1)
    here = (block == numbers) & (local_place >= lowest[:, None])
    place = jnp.sum(jnp.where(here, local_place + start[:, None] - dump, 0), axis=0) + dump
    ends = (start[:, None] + jnp.cumsum(members, axis=1)).reshape(-1, 1)
    rows = jnp.arange(dump, dtype=jnp.int32)[None, :]
    passed = jnp.sum((ends <= rows).astype(jnp.int32), axis=0)
    row_block = jnp.sum((own_start[:, None] <= rows).astype(jnp.int32), axis=0)
    local_bucket = passed - row_block * (BUCKETS + 1)
    row_bucket = jnp.where(
        local_bucket <= BUCKETS, (before + row_block) * BUCKETS + local_bucket, -1
    )
    span_bucket = row_bucket.astype(f32).reshape(-1, SPAN)
    return place, jnp.concatenate([span_bucket[:-1], span_bucket[1:]], axis=1)


def chunk_tables(groups):
    order = ring_order()
    flip = jnp.stack([lax.axis_index("rc"), lax.axis_index("ry")])

    def number(dc, dy, kk, hd):
        return ((hd * groups + kk) * 2 + (dy ^ flip[1])) * 2 + (dc ^ flip[0])

    def column(values):
        return jnp.array(values, jnp.int32)

    offsets = [list(range(sum(map(len, STEPS[:i])), sum(map(len, STEPS[: i + 1])))) for i in range(len(STEPS))]
    coming = [
        (dc, dy, kk, at)
        for dc in range(2)
        for part in offsets
        for dy in range(2)
        for kk in range(groups)
        for at in part
    ]
    going = [
        (dc, dy, kk, hd)
        for dc in range(2)
        for dy in range(2)
        for kk in range(groups)
        for hd in range(HEADS)
    ]
    dc, dy, kk, at = map(column, zip(*coming))
    in_table = number(dc, dy, kk, order[at])
    return in_table, number(*map(column, zip(*going)))


def per_device(
    first_half,
    second_half,
    qk_weight,
    value_weight,
    output_weight,
    inner_weight,
    outer_weight,
    attn_gain,
    attn_shift,
    ffn_gain,
    ffn_shift,
    buckets,
    slots,
    first_grad,
    second_grad,
):
    heads = lax.axis_size("hd")
    groups = lax.axis_size("kk")
    seq_count = heads * groups
    round_count = lax.axis_size("ry") * lax.axis_size("rc")
    device_count = seq_count * round_count
    own_rows, model_width = first_half.shape
    weight_rows, hidden_width = inner_weight.shape
    group_rows = own_rows * round_count
    slot_rows = 2 * group_rows
    tokens = group_rows * seq_count
    own_spans = min((tokens + (SPAN - 1) * heads) // SPAN, heads * slot_rows // SPAN)
    own_spans = -(-own_spans // UNROLL) * UNROLL
    piece = hidden_width // device_count
    blocks = own_rows // TOKB
    both = 2 * HEADD

    vectors = jnp.stack([attn_gain, attn_shift, ffn_gain, ffn_shift], axis=1)
    vectors = jnp.pad(vectors, ((0, 0), (0, HEADD - 4)))
    wide = both + HEADD
    head_shard = jnp.concatenate(
        [
            qk_weight.reshape(weight_rows, heads, HEADD),
            value_weight.reshape(weight_rows, heads, HEADD),
            jnp.broadcast_to(vectors[:, None], (weight_rows, heads, HEADD)),
        ],
        axis=2,
    )
    code_rows = 3 * group_rows // wide
    codes = index_codes(slots, buckets, slot_rows).reshape(code_rows, wide)
    codes = jnp.pad(codes, ((0, -code_rows % PAD), (0, 0)))
    codes = jnp.broadcast_to(codes[None], (heads,) + codes.shape)
    starter = jnp.concatenate([jnp.transpose(head_shard, (1, 0, 2)), codes], axis=1)

    second_later, starter = together(second_half, starter)
    second_in = second_later.astype(f32)
    unit, unit_scale = normalised(second_in)
    unit_low = unit.astype(bf)
    inner_split = inner_weight.reshape(weight_rows, seq_count, round_count, piece)
    inner_split = jnp.transpose(inner_split, (2, 0, 1, 3)).reshape(2, 2, weight_rows, -1)
    ring = [(unit_low,)]
    up, down = ring_step(unit_low, unit_low)
    inner_rows = traded(traded(inner_split, "rc", 1), "ry", 0)
    cut = round_count * weight_rows
    output_rows = ordered(ordered(output_weight, "rc", 0), "ry", 0).reshape(cut, model_width)
    shard = jnp.stack([inner_rows.reshape(cut, -1), outer_weight, output_rows])
    up, down, starter, shard = together(up, down, exchange(starter), shard)
    ring.append((up, down))

    up, down = ring_step(up, down)
    starter = jnp.transpose(over_groups(starter), (1, 0, 2, 3))
    codes = starter[:, :, weight_rows : weight_rows + code_rows].reshape(heads, groups, 3, -1)
    head_weight = ordered(ordered(starter[:, :, :weight_rows], "ry", 2), "rc", 3)
    head_weight = head_weight.reshape(model_width, wide)
    vectors_full = head_weight[:, both : both + 4].astype(f32)
    attn_gain_col, attn_shift_col = vectors_full[:, :1], vectors_full[:, 1:2]
    ffn_gain_row, ffn_shift_row = vectors_full[:, 2][None], vectors_full[:, 3][None]
    head_float = head_weight[:, :both].astype(f32)
    head_scaled = (head_float * attn_gain_col).astype(bf)
    head_offset = jnp.sum(head_float * attn_shift_col, axis=0, keepdims=True)
    up, down, head_scaled, head_offset, shard, second_later = together(
        up, down, head_scaled, head_offset, shard, second_grad
    )
    ring.append((up, down))

    def head_part(parts):
        rows = [product(part, head_scaled) + head_offset for part in parts]
        return over_groups(jnp.concatenate(rows, axis=0).astype(bf))

    up, down = ring_step(up, down)
    first_heads = head_part([part for step in ring for part in step])
    up, down, codes, shard = together(up, down, codes, shard)
    ring.append((up, down))

    half = own_rows // 2
    up, down = ring_step(up[:half], down[half:])
    up, down, first_swapped = together(up, down, swapped(first_heads, "ry"))
    ring.append((up, down))
    last_heads = head_part(ring[3] + ring[4])
    head_own = [first_heads, first_swapped, last_heads, swapped(last_heads, "ry")]
    head_own = jnp.concatenate([part.reshape(-1, both) for part in head_own], axis=0)
    place, key_bucket = sorted_layout(codes, slot_rows, own_spans)
    in_table, out_table = chunk_tables(groups)
    head_own, place, key_bucket, in_table, out_table = together(
        head_own, place, key_bucket, in_table, out_table
    )
    head_peer = swapped(head_own, "rc")

    grad_peer = swapped(second_later, "rc")
    grad_far = swapped(second_later, "ry")
    grad_last = swapped(grad_far, "rc")
    shards = lax.all_gather(shard, SEQ, axis=0, tiled=False)

    payload_own, payload_peer, sorted_q, sorted_k, sorted_v, probs, token_sums = attend_forward(
        in_table,
        out_table,
        place,
        key_bucket,
        head_own,
        head_peer,
        own_rows,
    )
    packed = (2, groups, heads, own_rows + PAD, HEADD)
    head_sums = sum_pair(payload_own.reshape(packed), payload_peer.reshape(packed))
    mixed_parts = exchange(sum_groups(head_sums))
    mixed_parts, shards = together(mixed_parts, shards)
    mixed_low, first_sum, ffn_unit, ffn_scale, ffn_low = mix_rows(
        mixed_parts, shards, first_half, ffn_gain_row, ffn_shift_row
    )
    ffn_low, qkv_rows = together(ffn_low, jnp.stack([qk_weight, value_weight]))
    qkv_rows = exchange(jnp.broadcast_to(qkv_rows[None], (heads,) + qkv_rows.shape))
    ffn_far = swapped(ffn_low, "ry")
    pair = feed_forward(ffn_low, swapped(ffn_low, "rc"), second_later, grad_peer, shards)
    ffn_far, pair = together(ffn_far, pair)
    far = feed_forward(ffn_far, swapped(ffn_far, "rc"), grad_far, grad_last, shards)
    pair, far = together(pair, far)
    ffn_pair, grad_pair, hidden_pair, inner_pair, *back_pair = pair
    ffn_far, grad_far, hidden_far, inner_far, *back_far = far
    far_sum = swapped(pair_sum(back_far[0], back_far[1], "rc"), "ry")
    near_sum = pair_sum(back_pair[0], back_pair[1], "rc")
    second_far = pair_sum(back_far[2], back_far[3], "rc")
    second_pair = pair_sum(back_pair[2], back_pair[3], "rc")
    part_sums = parts_product(
        ffn_pair,
        ffn_far,
        inner_pair,
        inner_far,
        hidden_pair,
        hidden_far,
        (grad_pair, grad_far),
    )
    part_sums = part_sums.reshape(-1, 2, TOKB // cut, cut, model_width)
    part_sums = jnp.transpose(part_sums, (0, 2, 1, 3, 4)).reshape(seq_count, 2, cut, model_width)
    near_sum, far_sum, part_sums, qkv_rows = together(near_sum, far_sum, part_sums, qkv_rows)
    part_grads = lax.psum_scatter(part_sums, SEQ, scatter_dimension=0, tiled=False)
    carry_low, back_parts = carry_rows(
        near_sum,
        far_sum,
        ffn_gain_row,
        ffn_unit,
        ffn_scale,
        first_grad,
        shards,
        mixed_low,
        mixed_parts,
    )
    back_parts = exchange(back_parts)
    output_part = against(mixed_low, carry_low).astype(bf)
    output_part = output_part.reshape(heads, groups, 2, 2, weight_rows, model_width)
    output_part = scattered(scattered(output_part, "rc", 3), "ry", 2)
    back_parts, output_part, second_pair, second_far, qkv_rows = together(
        back_parts, output_part, second_pair, second_far, qkv_rows
    )
    qkv_rows = jnp.transpose(over_groups(qkv_rows), (2, 1, 0, 3, 4))
    back_own, back_peer = spread_pair(over_groups(back_parts))
    back_own, second_far, qkv_rows, output_part = together(
        back_own, second_far, qkv_rows, output_part
    )
    output_rows = exchange(sum_groups(jnp.transpose(output_part, (1, 0, 2, 3))))
    second_far = swapped(second_far, "ry")
    qkv_got = swapped(qkv_rows, "ry")
    query_value_own, query_value_peer = attend_backward(
        out_table,
        place,
        back_own.reshape(-1, HEADD),
        back_peer.reshape(-1, HEADD),
        token_sums,
        sorted_q,
        sorted_k,
        sorted_v,
        probs,
        own_rows,
    )
    vector_rows = back_parts[:, own_rows + 2 * blocks : own_rows + 2 * blocks + 2]
    packed = (2, groups, heads, own_rows, both)
    vector_rows = back_parts[:, own_rows + 2 * blocks : own_rows + 2 * blocks + 2]
    packed = (2, groups, heads, own_rows, both)
    query_value_peer, qkv_got, second_far, output_rows = together(
        query_value_peer, qkv_got, second_far, output_rows
    )
    second_sum = second_in + second_pair.astype(f32) + second_far.astype(f32)
    query_value_own = query_value_own.reshape(packed)
    query_value_peer = swapped(query_value_peer.reshape(packed), "rc")

    def summed(part):
        return (query_value_own[part].astype(f32) + query_value_peer[part].astype(f32)).astype(bf)

    head_send = summed(1)
    head_send, output_rows, vector_rows, qkv_rows, qkv_got = together(
        head_send, output_rows, vector_rows, qkv_rows, qkv_got
    )
    qkv_rows = pair_order(qkv_rows, qkv_got, "ry", 3)
    qkv_full = ordered(qkv_rows, "rc", 4).reshape(2, model_width, model_width)
    head_got, qkv_full, head_keep = together(swapped(head_send, "ry"), qkv_full, summed(0))
    output_grad = jnp.sum(output_rows.astype(f32), axis=0)
    head_back = sum_groups(add_rows(head_keep, head_got))
    own_back = exchange(head_back)
    vector_sums = jnp.sum(vector_rows.astype(f32), axis=0)
    if groups > 1:
        vector_sums = lax.psum_scatter(
            vector_sums.reshape(2, groups, -1), "kk", scatter_dimension=1, tiled=False
        )
    vector_sums = jnp.pad(
        vector_sums.reshape(2, 2, 2, weight_rows), ((0, 6), (0, 0), (0, 0), (0, HEADD - weight_rows))
    )
    pieces = [part for step in ring for part in step]
    qkv_part, col_part = weight_part(ring_order(), head_back, pieces)
    qkv_part = qkv_part.reshape(heads, groups, 2, 2, weight_rows, both)
    col_part = jnp.broadcast_to(col_part[0], (heads, groups, 2, 2, PAD, both))
    qkv_part = jnp.concatenate([qkv_part, col_part], axis=4).astype(bf)
    qkv_part = scattered(scattered(qkv_part, "rc", 3), "ry", 2)
    qkv_part = sum_groups(jnp.transpose(qkv_part, (1, 0, 2, 3)))
    outer_grad = part_grads[1].astype(f32)
    turned = part_grads[0].reshape(2, 2, weight_rows, -1)
    turned = traded(traded(turned, "ry", 0), "rc", 1)
    vector_sums = wide_scattered(wide_scattered(vector_sums, "rc", 2), "ry", 1)
    vector_grads = vector_sums[:2, :weight_rows]
    own_back, qkv_part, turned = together(own_back, qkv_part, turned)
    inner_cols = turned.reshape(round_count, weight_rows, seq_count, piece)
    inner_grad = jnp.transpose(inner_cols, (1, 2, 0, 3)).reshape(weight_rows, hidden_width)
    qkv_rows = exchange(qkv_part).astype(f32)
    qkv_rows = qkv_rows.reshape(heads, weight_rows + PAD, 2, HEADD)
    qkv_rows = jnp.transpose(qkv_rows, (2, 1, 0, 3)).reshape(2, weight_rows + PAD, model_width)
    unit_grads, col_sums = qkv_rows[:, :weight_rows], qkv_rows[:, weight_rows]
    own_weights = jnp.stack([qk_weight, value_weight]).astype(f32)
    gain_own = attn_gain.astype(f32)[:, None]
    shift_own = attn_shift.astype(f32)[:, None]
    qkv_grads = unit_grads * gain_own + shift_own * col_sums[:, None]
    attn_gain_grad = jnp.sum(own_weights * unit_grads, axis=(0, 2))
    attn_shift_grad = jnp.sum(own_weights * col_sums[:, None], axis=(0, 2))

    second_carry = last_rows(
        own_back, qkv_full, attn_gain_col.reshape(1, -1), unit, unit_scale, second_grad
    )

    return (
        first_sum,
        second_sum.astype(bf),
        carry_low,
        second_carry,
        qkv_grads[0],
        qkv_grads[1],
        output_grad,
        inner_grad.astype(f32),
        outer_grad,
        attn_gain_grad,
        attn_shift_grad,
        vector_grads[0],
        vector_grads[1],
    )


def solution(mesh):
    seq_count, round_count = mesh.devices.shape
    shape = (HEADS, seq_count // HEADS, round_count // 2, 2)
    split_mesh = Mesh(mesh.devices.reshape(shape), ALL)
    rows = P(ALL, None)
    vector = P(ALL)
    table = P(ROUND, SEQ)
    in_specs = (rows,) * 7 + (vector,) * 4 + (table,) * 2 + (rows,) * 2
    out_specs = (rows,) * 9 + (vector,) * 4
    return jax.shard_map(
        per_device, mesh=split_mesh, in_specs=in_specs, out_specs=out_specs, check_vma=False
    )
```

```python
import functools
import math

import jax
import jax.numpy as jnp
from jax import lax
from jax.experimental import pallas as pl
from jax.experimental.pallas import tpu as pltpu
from jax.sharding import Mesh
from jax.sharding import PartitionSpec as P

HEADS = 8
NORM_EPS = 1e-05
SPAN = 64
HEADD = 128
PAD = 16
UNROLL = 34
TOKB = 128
BUCKETS = 32
CHUNK = 4096
VMEM_LIMIT = 60 * 2**20
KEY_EPS = 1e-06
bf = jnp.bfloat16
f32 = jnp.float32


def product(left_side, right_side):
    return jnp.dot(left_side, right_side, preferred_element_type=f32)


def against(left_side, right_side):
    return lax.dot_general(
        left_side, right_side, (((0,), (0,)), ((), ())), preferred_element_type=f32
    )


def through(left_side, right_side):
    return lax.dot_general(
        left_side, right_side, (((1,), (1,)), ((), ())), preferred_element_type=f32
    )


def takes(microseconds):
    return pl.CostEstimate(
        flops=int(microseconds * 1e8), bytes_accessed=int(microseconds * 3e6), transcendentals=0
    )


def aligned(start, size, step=SPAN):
    return pl.ds(pl.multiple_of(start, step), size)


def fill(ref, value):
    def body(step, carry):
        ref[aligned(step * SPAN, SPAN), :] = jnp.full((SPAN, ref.shape[1]), value, ref.dtype)
        return carry

    lax.fori_loop(0, ref.shape[0] // SPAN, body, 0)


def diagonal():
    rows = lax.broadcasted_iota(jnp.int32, (TOKB, TOKB), 0)
    return rows == lax.broadcasted_iota(jnp.int32, (TOKB, TOKB), 1)


def lanes(row, eye, ones):
    high = row.astype(bf).astype(f32)
    parts = [jnp.where(eye, high, 0.0), jnp.where(eye, row - high, 0.0)]
    return product(jnp.concatenate(parts, axis=1).astype(bf), ones)


def forward_kernel(
    own_rows,
    load_steps,
    in_ref,
    out_ref,
    place_ref,
    bucket_ref,
    own_ref,
    peer_ref,
    pay_own_ref,
    pay_peer_ref,
    query_out,
    key_out,
    value_out,
    prob_out,
    sum_ref,
    query_ref,
    key_ref,
    value_ref,
    prob_ref,
    wide_a,
    wide_b,
    stage_a,
    stage_b,
    sems,
):
    step = pl.program_id(0)
    leaving = [
        pltpu.make_async_copy(source, target, sems.at[number])
        for number, (source, target) in enumerate(
            [
                (query_ref, query_out),
                (key_ref, key_out),
                (value_ref, value_out),
                (prob_ref, prob_out),
            ]
        )
    ]
    own_spans = prob_ref.shape[0] // SPAN
    unroll = 2 * UNROLL if own_spans == 4 * UNROLL else UNROLL
    tail = SPAN * (own_spans + 1)

    @pl.when(step == 0)
    def _():
        fill(wide_a, 0.0)
        fill(wide_b, 0.0)

    def scatter_from(token_ref):
        def scatter(chunk, carry):
            both = token_ref[aligned(chunk * own_rows, own_rows, TOKB), :].astype(f32)
            stage_a[...] = both[:, :HEADD]
            stage_b[...] = both[:, HEADD:]
            first = in_ref[step * (CHUNK // own_rows) + chunk] * own_rows
            for row in range(own_rows):
                place = place_ref[first + row]
                wide_a[pl.ds(place, 1), :] = stage_a[row : row + 1, :]
                wide_b[pl.ds(place, 1), :] = stage_b[row : row + 1, :]
            return carry

        lax.fori_loop(0, CHUNK // own_rows, scatter, 0)

    pl.when(step < load_steps // 2)(lambda: scatter_from(own_ref))
    pl.when((step >= load_steps // 2) & (step < load_steps))(lambda: scatter_from(peer_ref))

    def unit_keys(query):
        square = jnp.sum(query * query, axis=-1, keepdims=True)
        scale = lax.rsqrt(square * (1.0 / HEADD) + KEY_EPS) * HEADD**-0.5
        return (query * scale).astype(bf)

    @pl.when(step == load_steps)
    def _():
        query_ref[:SPAN, :] = wide_a[:SPAN, :].astype(bf)
        key_ref[:SPAN, :] = unit_keys(wide_a[:SPAN, :])
        value_ref[:SPAN, :] = wide_b[:SPAN, :].astype(bf)
        wide_a[:SPAN, :] = jnp.zeros((SPAN, HEADD), f32)
        wide_b[:SPAN, :] = jnp.zeros((SPAN, HEADD), f32)
        for ref in (query_ref, key_ref, value_ref):
            ref[pl.ds(tail, SPAN), :] = jnp.zeros((SPAN, HEADD), bf)
        ones = jnp.ones((2 * SPAN, HEADD), bf)
        row_ids = lax.broadcasted_iota(jnp.int32, (SPAN, 2 * SPAN), 0)
        lane_ids = lax.broadcasted_iota(jnp.int32, (SPAN, 2 * SPAN), 1)
        before, itself = lane_ids == row_ids, lane_ids == row_ids + SPAN

        def spans(group, carry):
            first = group * (unroll * SPAN)
            prev = aligned(first, SPAN)
            here = aligned(first + SPAN, unroll * SPAN)
            query_wide = wide_a[here, :]
            values = wide_b[here, :].astype(bf)
            keys = jnp.concatenate([key_ref[prev, :], unit_keys(query_wide)], axis=0)
            seen = jnp.concatenate([value_ref[prev, :], values], axis=0)
            query = query_wide.astype(bf)
            key_buckets, columns = [], []
            for span in range(unroll):
                row = bucket_ref[pl.ds(group * unroll + span, 1), :]
                high = row.astype(bf).astype(f32)
                low = pltpu.roll(row - high, SPAN, 1)
                key_buckets.append(row)
                columns.append(jnp.where(itself, high, jnp.where(before, low, 0.0)).astype(bf))
            columns = product(jnp.concatenate(columns, axis=0), ones)
            raised = []
            for span in range(unroll):
                mine = slice(span * SPAN, (span + 1) * SPAN)
                both = slice(span * SPAN, (span + 2) * SPAN)
                same = columns[mine] == key_buckets[span]
                matches = jnp.sum(jnp.where(same, 1.0, 0.0), axis=-1, keepdims=True)
                allowed = same & (jnp.logical_not(itself) | (matches < 1.5))
                scores = through(query[mine], keys[both])
                raised.append(jnp.where(allowed, jnp.exp(scores), 0.0))
            lows = [member.astype(bf) for member in raised]
            totals = product(jnp.concatenate(lows, axis=0), ones)
            results = []
            for span in range(unroll):
                mine = slice(span * SPAN, (span + 1) * SPAN)
                both = slice(span * SPAN, (span + 2) * SPAN)
                total = totals[mine]
                inverse = jnp.where(total > 0.0, 1.0 / total, 0.0)
                probs = (raised[span] * inverse).astype(bf)
                results.append((product(lows[span], seen[both]), total, probs))
            query_ref[here, :] = query
            key_ref[here, :] = keys[SPAN:]
            value_ref[here, :] = values
            for span, (weighted, total, probs) in enumerate(results):
                at = aligned(first + (span + 1) * SPAN, SPAN)
                wide_a[at, :] = weighted
                wide_b[at, :] = total
                prob_ref[aligned(first + span * SPAN, SPAN), :] = probs
            return carry

        lax.fori_loop(0, own_spans // unroll, spans, 0)
        for copy in leaving:
            copy.start()
        wide_a[pl.ds(tail, SPAN), :] = jnp.zeros((SPAN, HEADD), f32)
        wide_b[pl.ds(tail, SPAN), :] = jnp.zeros((SPAN, HEADD), f32)

    def collect_to(pay_ref):
        blocks = own_rows // TOKB
        per_step = CHUNK // own_rows
        eye = diagonal()
        sum_rows = lax.broadcasted_iota(jnp.int32, (PAD, TOKB), 0)
        offset = (step - load_steps - 1) * per_step

        def collect(chunk, carry):
            first = chunk * (own_rows + PAD)
            sums = jnp.zeros((PAD, TOKB), f32)
            start = out_ref[offset + chunk] * own_rows
            for row in range(own_rows):
                place = place_ref[start + row]
                stage_a[row : row + 1, :] = wide_a[pl.ds(place, 1), :]
                stage_b[row : row + 1, :] = wide_b[pl.ds(place, 1), :]
            pay_ref[aligned(first, own_rows, PAD), :] = stage_a[...].astype(bf)
            for block in range(blocks):
                wide_sums = stage_b[block * TOKB : (block + 1) * TOKB, :]
                packed = jnp.sum(jnp.where(eye, wide_sums, 0.0), axis=0, keepdims=True)
                sum_ref[pl.ds(chunk * blocks + block, 1), :] = packed
                sums = jnp.where(sum_rows == block, packed, sums)
            pay_ref[aligned(first + own_rows, PAD, PAD), :] = sums.astype(bf)
            return carry

        lax.fori_loop(0, per_step, collect, 0)

    half = load_steps + 1 + load_steps // 2
    pl.when((step > load_steps) & (step < half))(lambda: collect_to(pay_own_ref))
    pl.when(step >= half)(lambda: collect_to(pay_peer_ref))

    @pl.when(step == 2 * load_steps)
    def _():
        for copy in leaving:
            copy.wait()


def part_spec(shape, first, count):
    return pl.BlockSpec(shape, lambda step: (jnp.clip(step - first, 0, count - 1), 0))


def attend_forward(in_table, out_table, place, key_bucket, own, peer, own_rows):
    tokens = place.shape[0]
    steps = tokens // CHUNK
    half = steps // 2
    own_spans = key_bucket.shape[0]
    rows = SPAN * (own_spans + 2)
    pay_rows = CHUNK // own_rows * (own_rows + PAD)
    once = pl.Buffered(1)

    def whole(shape):
        return pl.BlockSpec(shape, lambda step: (0, 0), pipeline_mode=once)

    sorted_rows = jax.ShapeDtypeStruct((rows, HEADD), bf)
    return pl.pallas_call(
        functools.partial(forward_kernel, own_rows, steps),
        grid=(2 * steps + 1,),
        out_shape=(
            jax.ShapeDtypeStruct((half * pay_rows, HEADD), bf),
            jax.ShapeDtypeStruct((half * pay_rows, HEADD), bf),
            sorted_rows,
            sorted_rows,
            sorted_rows,
            jax.ShapeDtypeStruct((own_spans * SPAN, 2 * SPAN), bf),
            jax.ShapeDtypeStruct((tokens // TOKB, TOKB), f32),
        ),
        in_specs=[
            pl.BlockSpec(memory_space=pltpu.SMEM),
            pl.BlockSpec(memory_space=pltpu.SMEM),
            pl.BlockSpec(memory_space=pltpu.SMEM),
            whole(key_bucket.shape),
            part_spec((CHUNK, 2 * HEADD), 0, half),
            part_spec((CHUNK, 2 * HEADD), half, half),
        ],
        out_specs=(
            part_spec((pay_rows, HEADD), steps + 1, half),
            part_spec((pay_rows, HEADD), steps + 1 + half, half),
            pl.BlockSpec(memory_space=pl.ANY),
            pl.BlockSpec(memory_space=pl.ANY),
            pl.BlockSpec(memory_space=pl.ANY),
            pl.BlockSpec(memory_space=pl.ANY),
            part_spec((CHUNK // TOKB, TOKB), steps + 1, steps),
        ),
        scratch_shapes=[pltpu.VMEM((rows, HEADD), bf)] * 3
        + [pltpu.VMEM((own_spans * SPAN, 2 * SPAN), bf)]
        + [pltpu.VMEM((rows, HEADD), f32)] * 2
        + [pltpu.VMEM((own_rows, HEADD), f32)] * 2
        + [pltpu.SemaphoreType.DMA((4,))],
        compiler_params=pltpu.CompilerParams(vmem_limit_bytes=VMEM_LIMIT),
        name="attend_forward",
        cost_estimate=takes(35),
    )(in_table, out_table, place, key_bucket, own, peer)


def backward_kernel(
    own_rows,
    load_steps,
    table_ref,
    place_ref,
    pay_own_ref,
    pay_peer_ref,
    sum_ref,
    query_in,
    key_in,
    value_in,
    prob_in,
    out_own_ref,
    out_peer_ref,
    query_ref,
    key_ref,
    value_ref,
    prob_ref,
    wide_a,
    wide_b,
    wide_c,
    stage_a,
    stage_b,
    sems,
):
    step = pl.program_id(0)
    coming = [
        pltpu.make_async_copy(source, target, sems.at[number])
        for number, (source, target) in enumerate(
            [(query_in, query_ref), (key_in, key_ref), (value_in, value_ref), (prob_in, prob_ref)]
        )
    ]
    own_spans = prob_ref.shape[0] // SPAN
    unroll = 2 * UNROLL if own_spans == 4 * UNROLL else UNROLL
    tail = SPAN * (own_spans + 1)

    @pl.when(step == 0)
    def _():
        for copy in coming:
            copy.start()
        fill(wide_a, 0.0)
        fill(wide_b, 0.0)

    def scatter_from(pay_ref):
        blocks = own_rows // TOKB
        eye = diagonal()
        ones = jnp.ones((2 * TOKB, TOKB), bf)

        def scatter(chunk, carry):
            first = chunk * (own_rows + PAD)
            extra = pay_ref[aligned(first + own_rows, PAD, PAD), :].astype(f32)
            for block in range(blocks):
                share = sum_ref[pl.ds(chunk * blocks + block, 1), :]
                share = share / extra[blocks + block : blocks + block + 1, :]
                rows = pay_ref[aligned(first + block * TOKB, TOKB, PAD), :].astype(f32)
                here = slice(block * TOKB, (block + 1) * TOKB)
                stage_a[here, :] = rows * lanes(share, eye, ones)
                stage_b[here, :] = lanes(share * extra[block : block + 1, :], eye, ones)
            start = table_ref[step * (CHUNK // own_rows) + chunk] * own_rows
            for row in range(own_rows):
                place = place_ref[start + row]
                wide_a[pl.ds(place, 1), :] = stage_a[row : row + 1, :]
                wide_b[pl.ds(place, 1), :] = stage_b[row : row + 1, :]
            return carry

        lax.fori_loop(0, CHUNK // own_rows, scatter, 0)

    pl.when(step < load_steps // 2)(lambda: scatter_from(pay_own_ref))
    pl.when((step >= load_steps // 2) & (step < load_steps))(lambda: scatter_from(pay_peer_ref))

    def pulled(query_low, d_query, d_keys):
        query = query_low.astype(f32)
        inverse = lax.rsqrt(
            jnp.sum(query * query, axis=-1, keepdims=True) * (1.0 / HEADD) + KEY_EPS
        )
        along = jnp.sum(query * d_keys, axis=-1, keepdims=True)
        scale = inverse * HEADD**-0.5
        return d_query + scale * d_keys - (scale * inverse * inverse * along * (1.0 / HEADD)) * query

    @pl.when(step == load_steps)
    def _():
        for copy in coming:
            copy.wait()
        for ref in (wide_a, wide_b, wide_c):
            ref[:SPAN, :] = jnp.zeros((SPAN, HEADD), f32)
        zero = jnp.zeros((SPAN, HEADD), bf)

        def spans(group, carry):
            first = group * (unroll * SPAN)
            prev = aligned(first, SPAN)
            own = aligned(first, unroll * SPAN)
            here = aligned(first + SPAN, unroll * SPAN)
            around = aligned(first, (unroll + 1) * SPAN)
            query = query_ref[around, :]
            keys = key_ref[around, :]
            values = value_ref[around, :]
            probs = prob_ref[own, :]
            d_out = wide_a[here, :].astype(bf)
            delta = wide_b[here, :]
            d_query = [wide_a[prev, :]]
            d_keys = [wide_b[prev, :]]
            d_values = [wide_c[prev, :]]
            for span in range(unroll):
                mine = slice(span * SPAN, (span + 1) * SPAN)
                after = slice((span + 1) * SPAN, (span + 2) * SPAN)
                both = slice(span * SPAN, (span + 2) * SPAN)
                d_probs = through(d_out[mine], values[both])
                prob = probs[mine]
                d_scores = (prob.astype(f32) * (d_probs - delta[mine])).astype(bf)
                d_query.append(product(d_scores, keys[both]))
                right = jnp.concatenate(
                    [
                        jnp.concatenate([query[after], zero], axis=1),
                        jnp.concatenate([zero, d_out[mine]], axis=1),
                    ],
                    axis=0,
                )
                pair = against(jnp.concatenate([d_scores, prob], axis=0), right)
                d_keys[-1] = d_keys[-1] + pair[:SPAN, :HEADD]
                d_values[-1] = d_values[-1] + pair[:SPAN, HEADD:]
                d_keys.append(pair[SPAN:, :HEADD])
                d_values.append(pair[SPAN:, HEADD:])
            for span in range(unroll + 1):
                at = aligned(first + span * SPAN, SPAN)
                wide_c[at, :] = d_values[span]
                if span < unroll:
                    rows = slice(span * SPAN, (span + 1) * SPAN)
                    wide_a[at, :] = pulled(query[rows], d_query[span], d_keys[span])
                else:
                    wide_a[at, :] = d_query[span]
                    wide_b[at, :] = d_keys[span]
            return carry

        lax.fori_loop(0, own_spans // unroll, spans, 0)
        last = pl.ds(tail - SPAN, SPAN)
        wide_a[last, :] = pulled(query_ref[last, :], wide_a[last, :], wide_b[last, :])
        wide_a[pl.ds(tail, SPAN), :] = jnp.zeros((SPAN, HEADD), f32)
        wide_c[pl.ds(tail, SPAN), :] = jnp.zeros((SPAN, HEADD), f32)

    def collect_to(out_ref):
        offset = (step - load_steps - 1) * (CHUNK // own_rows)

        def collect(chunk, carry):
            start = table_ref[offset + chunk] * own_rows
            for row in range(own_rows):
                place = place_ref[start + row]
                stage_a[row : row + 1, :] = wide_a[pl.ds(place, 1), :]
                stage_b[row : row + 1, :] = wide_c[pl.ds(place, 1), :]
            here = aligned(chunk * own_rows, own_rows, TOKB)
            out_ref[here, :HEADD] = stage_a[...].astype(bf)
            out_ref[here, HEADD:] = stage_b[...].astype(bf)
            return carry

        lax.fori_loop(0, CHUNK // own_rows, collect, 0)

    half = load_steps + 1 + load_steps // 2
    pl.when((step > load_steps) & (step < half))(lambda: collect_to(out_own_ref))
    pl.when(step >= half)(lambda: collect_to(out_peer_ref))


def attend_backward(out_table, place, pay_own, pay_peer, sums, query, keys, values, probs, own_rows):
    tokens = place.shape[0]
    steps = tokens // CHUNK
    half = steps // 2
    rows = query.shape[0]
    pay_rows = CHUNK // own_rows * (own_rows + PAD)
    out_half = jax.ShapeDtypeStruct((tokens // 2, 2 * HEADD), bf)
    return pl.pallas_call(
        functools.partial(backward_kernel, own_rows, steps),
        grid=(2 * steps + 1,),
        out_shape=(out_half, out_half),
        in_specs=[
            pl.BlockSpec(memory_space=pltpu.SMEM),
            pl.BlockSpec(memory_space=pltpu.SMEM),
            part_spec((pay_rows, HEADD), 0, half),
            part_spec((pay_rows, HEADD), half, half),
            part_spec((CHUNK // TOKB, TOKB), 0, steps),
            pl.BlockSpec(memory_space=pl.ANY),
            pl.BlockSpec(memory_space=pl.ANY),
            pl.BlockSpec(memory_space=pl.ANY),
            pl.BlockSpec(memory_space=pl.ANY),
        ],
        out_specs=(
            part_spec((CHUNK, 2 * HEADD), steps + 1, half),
            part_spec((CHUNK, 2 * HEADD), steps + 1 + half, half),
        ),
        scratch_shapes=[pltpu.VMEM((rows, HEADD), bf)] * 3
        + [pltpu.VMEM(probs.shape, bf)]
        + [pltpu.VMEM((rows, HEADD), f32)] * 3
        + [pltpu.VMEM((own_rows, HEADD), f32)] * 2
        + [pltpu.SemaphoreType.DMA((4,))],
        compiler_params=pltpu.CompilerParams(vmem_limit_bytes=VMEM_LIMIT),
        name="attend_backward",
        cost_estimate=takes(44),
    )(out_table, place, pay_own, pay_peer, sums, query, keys, values, probs)


def shard_spec(shards, number):
    block = (shards.shape[0], 1) + shards.shape[2:]
    return pl.BlockSpec(block, lambda *_: (0, number, 0, 0), pipeline_mode=pl.Buffered(1))


def whole_weight(ref):
    value = ref[...]
    return value.reshape(-1, value.shape[-1])


def feed_kernel(
    own_ref, peer_ref, grad_own_ref, grad_peer_ref, inner_weight_ref, outer_weight_ref,
    row_ref, grad_ref, hidden_ref, inner_ref,
    back_own_ref, back_peer_ref, second_own_ref, second_peer_ref,
):
    step = pl.program_id(0)

    @pl.when(step == 0)
    def _():
        row_ref[...] = own_ref[...]
        grad_ref[...] = grad_own_ref[...]

    @pl.when(step == 1)
    def _():
        row_ref[...] = peer_ref[...]
        grad_ref[...] = grad_peer_ref[...]

    weight = whole_weight(inner_weight_ref)
    outer_weight = whole_weight(outer_weight_ref)
    act = product(row_ref[...], weight)
    size = jnp.abs(act)
    bell = jnp.exp(act * act * -0.5)
    near = 1.0 / (1.0 + size * (0.3275911 * 0.5**0.5))
    tail = near * (0.254829592 + near * (-0.284496736 + near * (
        1.421413741 + near * (-1.453152027 + near * 1.061405429))))
    tail = tail * bell * 0.5
    normal = jnp.where(act >= 0.0, 1.0 - tail, tail)
    hidden = (act * normal).astype(bf)
    hidden_ref[...] = hidden
    slope = normal + act * bell * (2.0 * math.pi) ** -0.5
    inner = (through(grad_ref[...], outer_weight) * slope).astype(bf)
    inner_ref[...] = inner
    back = through(inner, weight).astype(bf)
    second = product(hidden, outer_weight).astype(bf)

    @pl.when(step == 0)
    def _():
        back_own_ref[...] = back
        second_own_ref[...] = second

    @pl.when(step == 1)
    def _():
        back_peer_ref[...] = back
        second_peer_ref[...] = second


def feed_forward(own, peer, grad_own, grad_peer, shards):
    count, width = own.shape
    units = shards.shape[3]

    def part(columns):
        return pl.BlockSpec((count, columns), lambda i: (i, 0))

    whole = pl.BlockSpec((count, width), lambda i: (0, 0), pipeline_mode=pl.Buffered(1))
    by_width = jax.ShapeDtypeStruct((2 * count, width), bf)
    by_units = jax.ShapeDtypeStruct((2 * count, units), bf)
    half = jax.ShapeDtypeStruct((count, width), bf)
    return pl.pallas_call(
        feed_kernel,
        grid=(2,),
        out_shape=(by_width, by_width, by_units, by_units, half, half, half, half),
        in_specs=[whole] * 4 + [shard_spec(shards, 0), shard_spec(shards, 1)],
        out_specs=(
            part(width), part(width), part(units), part(units), whole, whole, whole, whole
        ),
        compiler_params=pltpu.CompilerParams(vmem_limit_bytes=VMEM_LIMIT),
        name="feed_forward",
        cost_estimate=takes(9),
    )(own, peer, grad_own, grad_peer, shards, shards)


def mix_kernel(
    parts_ref, weight_ref, first_ref, gain_ref, shift_ref,
    low_ref, sum_ref, unit_ref, scale_ref, feed_ref,
):
    heads, rows = parts_ref.shape[0], first_ref.shape[0]
    eye = diagonal()
    ones = jnp.ones((2 * TOKB, TOKB), bf)
    for head in range(heads):
        columns = slice(head * HEADD, (head + 1) * HEADD)
        for block in range(rows // TOKB):
            here = slice(block * TOKB, (block + 1) * TOKB)
            sums = parts_ref[head, rows : rows + PAD, :].astype(f32)[block : block + 1]
            mixed = parts_ref[head, here, :].astype(f32) / lanes(sums, eye, ones)
            low_ref[here, columns] = mixed.astype(bf)
    total = first_ref[...].astype(f32) + product(low_ref[...], whole_weight(weight_ref))
    sum_ref[...] = total.astype(bf)
    centre = total - jnp.mean(total, axis=-1, keepdims=True)
    scale = lax.rsqrt(jnp.mean(centre * centre, axis=-1, keepdims=True) + NORM_EPS)
    unit = centre * scale
    unit_ref[...] = unit
    scale_ref[...] = scale
    feed_ref[...] = (unit * gain_ref[...] + shift_ref[...]).astype(bf)


def mix_rows(parts, shards, first_half, gain, shift):
    rows, width = first_half.shape
    vm = pl.BlockSpec(memory_space=pltpu.VMEM)
    wide, low = jax.ShapeDtypeStruct((rows, width), f32), jax.ShapeDtypeStruct((rows, width), bf)
    return pl.pallas_call(
        mix_kernel,
        out_shape=(low, low, wide, jax.ShapeDtypeStruct((rows, 1), f32), low),
        grid=(1,),
        in_specs=[vm, shard_spec(shards, 2), vm, vm, vm],
        out_specs=(vm,) * 5,
        compiler_params=pltpu.CompilerParams(vmem_limit_bytes=VMEM_LIMIT),
        name="mix_rows",
        cost_estimate=takes(5),
    )(parts, shards, first_half, gain, shift)


def carry_kernel(
    near_ref, far_ref, gain_ref, unit_ref, scale_ref, grad_ref, weight_ref, mixed_ref, parts_ref,
    carry_ref, pay_ref, wide_ref,
):
    heads, rows = parts_ref.shape[0], grad_ref.shape[0]
    blocks = rows // TOKB
    back = near_ref[...].astype(f32) + far_ref[...].astype(f32)
    unit = unit_ref[...]
    gain_sum = jnp.sum(back * unit, axis=0, keepdims=True)
    shift_sum = jnp.sum(back, axis=0, keepdims=True)
    grad = back * gain_ref[...]
    along = jnp.mean(grad * unit, axis=-1, keepdims=True)
    grad = scale_ref[...] * (grad - jnp.mean(grad, axis=-1, keepdims=True) - unit * along)
    carry_ref[...] = (grad_ref[...].astype(f32) + grad).astype(bf)
    wide_ref[...] = through(carry_ref[...], whole_weight(weight_ref))
    eye = diagonal()
    pad_rows = lax.broadcasted_iota(jnp.int32, (PAD, TOKB), 0)
    for head in range(heads):
        columns = slice(head * HEADD, (head + 1) * HEADD)
        sums = parts_ref[head, rows : rows + PAD, :].astype(f32)
        tails = jnp.zeros((PAD, TOKB), f32)
        for block in range(blocks):
            here = slice(block * TOKB, (block + 1) * TOKB)
            wide = wide_ref[here, columns]
            pay_ref[head, here, :] = wide.astype(bf)
            mixed = mixed_ref[here, columns].astype(f32)
            dot = jnp.sum(wide * mixed, axis=-1, keepdims=True)
            packed = jnp.sum(jnp.where(eye, dot, 0.0), axis=0, keepdims=True)
            tails = jnp.where(pad_rows == block, packed, tails)
            tails = jnp.where(pad_rows == blocks + block, sums[block : block + 1], tails)
        tails = jnp.where(pad_rows == 2 * blocks, gain_sum[:, columns], tails)
        tails = jnp.where(pad_rows == 2 * blocks + 1, shift_sum[:, columns], tails)
        pay_ref[head, rows : rows + PAD, :] = tails.astype(bf)


def carry_rows(near, far, gain, unit, scale, first_grad, shards, mixed, parts):
    rows, width = near.shape
    vm = pl.BlockSpec(memory_space=pltpu.VMEM)
    return pl.pallas_call(
        carry_kernel,
        out_shape=(
            jax.ShapeDtypeStruct((rows, width), bf),
            jax.ShapeDtypeStruct(parts.shape, bf),
        ),
        grid=(1,),
        in_specs=[vm] * 6 + [shard_spec(shards, 2)] + [vm] * 2,
        out_specs=(vm,) * 2,
        scratch_shapes=[pltpu.VMEM((rows, width), f32)],
        compiler_params=pltpu.CompilerParams(vmem_limit_bytes=VMEM_LIMIT),
        name="carry_rows",
        cost_estimate=takes(5),
    )(near, far, gain, unit, scale, first_grad, shards, mixed, parts)


def add_kernel(left_ref, right_ref, out_ref):
    total = left_ref[...].astype(f32) + right_ref[...].astype(f32)
    out_ref[...] = total.astype(out_ref.dtype)


def add_rows(left, right):
    shape = left.shape
    left, right = left.reshape(-1, shape[-1]), right.reshape(-1, shape[-1])
    step = math.gcd(left.shape[0], 1024)
    spec = pl.BlockSpec((step, shape[-1]), lambda i: (i, 0))
    out = pl.pallas_call(
        add_kernel,
        grid=(left.shape[0] // step,),
        out_shape=jax.ShapeDtypeStruct(left.shape, left.dtype),
        in_specs=[spec, spec],
        out_specs=spec,
        name="add_rows",
        cost_estimate=takes(3),
    )(left, right)
    return out.reshape(shape)


def last_kernel(
    back_ref, weight_ref, gain_ref, unit_ref, scale_ref, grad_ref, out_ref, query_ref, value_ref,
):
    for head in range(back_ref.shape[0]):
        columns = slice(head * HEADD, (head + 1) * HEADD)
        query_ref[:, columns] = back_ref[head, :, :HEADD]
        value_ref[:, columns] = back_ref[head, :, HEADD:]
    total = through(query_ref[...], weight_ref[0]) + through(value_ref[...], weight_ref[1])
    grad = total * gain_ref[...]
    unit = unit_ref[...]
    along = jnp.mean(grad * unit, axis=-1, keepdims=True)
    centred = grad - jnp.mean(grad, axis=-1, keepdims=True) - unit * along
    out_ref[...] = (grad_ref[...].astype(f32) + scale_ref[...] * centred).astype(bf)


def last_rows(own_back, weights, gain, unit, scale, second_grad):
    rows, width = unit.shape
    vm = pl.BlockSpec(memory_space=pltpu.VMEM)
    return pl.pallas_call(
        last_kernel,
        out_shape=jax.ShapeDtypeStruct((rows, width), bf),
        in_specs=[vm] * 6,
        out_specs=vm,
        scratch_shapes=[pltpu.VMEM((rows, width), bf)] * 2,
        compiler_params=pltpu.CompilerParams(vmem_limit_bytes=VMEM_LIMIT),
        name="last_rows",
        cost_estimate=takes(6),
    )(own_back, weights, gain, unit, scale, second_grad)


def weight_kernel(order_ref, back_ref, *refs):
    pieces, (part_ref, column_ref) = refs[:-2], refs[-2:]
    half = pieces[-1].shape[0]
    total = None
    for number, piece in enumerate(pieces[:-1]):
        back = back_ref[order_ref[number]]
        if piece.shape[0] == half:
            term = against(piece[...], back[:half]) + against(pieces[-1][...], back[half:])
        else:
            term = against(piece[...], back)
        total = term if total is None else total + term
    part_ref[...] = total
    columns = jnp.sum(back_ref[...].astype(f32), axis=(0, 1), keepdims=True)[0]
    column_ref[...] = jnp.broadcast_to(columns, column_ref.shape)


def weight_part(order, back, pieces):
    width = pieces[0].shape[1]
    vm = pl.BlockSpec(memory_space=pltpu.VMEM)
    return pl.pallas_call(
        weight_kernel,
        out_shape=(
            jax.ShapeDtypeStruct((width, back.shape[2]), f32),
            jax.ShapeDtypeStruct((8, back.shape[2]), f32),
        ),
        in_specs=[pl.BlockSpec(memory_space=pltpu.SMEM)] + [vm] * (1 + len(pieces)),
        out_specs=(vm, vm),
        compiler_params=pltpu.CompilerParams(vmem_limit_bytes=VMEM_LIMIT),
        name="weight_part",
        cost_estimate=takes(5),
    )(order, back, *pieces)


def layout_kernel(
    heads, slot_rows, first_ref, code_ref, place_ref, bucket_ref, start_ref, low_ref, end_ref
):
    sources = code_ref.shape[0]
    rows = place_ref.shape[0] // sources
    own_spans = bucket_ref.shape[0]
    categories = BUCKETS + 1
    before = first_ref[0].astype(f32)
    codes = code_ref[...].astype(f32)[:, :rows].reshape(sources * rows, 3 * TOKB)
    slots = codes[:, :TOKB] * 256.0 + codes[:, TOKB : 2 * TOKB]
    buckets = codes[:, 2 * TOKB :]
    target = jnp.floor(slots * (1.0 / slot_rows))
    block = target - before
    local = slots - target * slot_rows
    block_ids = lax.broadcasted_iota(jnp.int32, (16, TOKB), 0).astype(f32)
    bucket_ids = lax.broadcasted_iota(jnp.int32, (TOKB, TOKB), 0).astype(f32)
    counts = jnp.zeros((16, TOKB), f32)
    for row in range(sources * rows):
        left = jnp.where(block_ids == block[row : row + 1], 1.0, 0.0).astype(bf)
        right = jnp.where(bucket_ids == buckets[row : row + 1], 1.0, 0.0).astype(bf)
        counts += through(left, right)
    lane_ids = lax.broadcasted_iota(jnp.int32, (16, TOKB), 1)
    row_ids = lax.broadcasted_iota(jnp.int32, (16, TOKB), 0)
    total = jnp.broadcast_to(jnp.sum(counts, axis=1, keepdims=True), counts.shape)
    step = 1
    while step < categories:
        counts += jnp.where(lane_ids >= step, pltpu.roll(counts, step, 1), 0.0)
        step *= 2
    spans = jnp.where(row_ids == 0, 0.0, jnp.floor((total + (SPAN - 1)) * (1.0 / SPAN)))
    start = spans
    step = 1
    while step < 16:
        start += jnp.where(row_ids >= step, pltpu.roll(start, step, 0), 0.0)
        step *= 2
    start = (start - spans + 1.0) * SPAN
    last_start = jnp.floor(jnp.maximum(total - 1.0, 0.0) * (1.0 / SPAN)) * SPAN
    start = jnp.where(row_ids == 0, -last_start, start)
    start_ref[...] = start
    low_ref[...] = jnp.where(row_ids == 0, last_start, 0.0)
    unused = (row_ids > heads) | (lane_ids >= categories)
    ends = jnp.where(unused, 1e9, start + counts)
    for bucket in range(categories):
        wide = jnp.sum(jnp.where(lane_ids == bucket, ends, 0.0), axis=1, keepdims=True)
        end_ref[bucket] = jnp.broadcast_to(wide, ends.shape)
    place = jnp.full(local.shape, (own_spans + 1.0) * SPAN, f32)
    for number in range(heads + 1):
        here = (block == float(number)) & (local >= low_ref[number : number + 1, :])
        place = jnp.where(here, local + start_ref[number : number + 1, :], place)
    place_ref[...] = place.astype(jnp.int32)
    shape = (own_spans, TOKB)
    at = lax.broadcasted_iota(jnp.int32, shape, 0) * SPAN + lax.broadcasted_iota(jnp.int32, shape, 1)
    at = at.astype(f32)
    block_number = jnp.zeros(shape, f32)
    for number in range(1, heads + 1):
        block_number += jnp.where(at >= start_ref[number : number + 1, :], 1.0, 0.0)
    passed = -block_number * categories

    def count(bucket, passed):
        for number in range(heads + 1):
            passed += jnp.where(at >= end_ref[bucket, number : number + 1, :], 1.0, 0.0)
        return passed

    passed = lax.fori_loop(0, categories, count, passed)
    bucket_ref[...] = jnp.where(
        passed <= BUCKETS, (before + block_number) * BUCKETS + passed, -1.0
    )


def sorted_layout(first, codes, heads, slot_rows, own_spans, rows):
    sources = codes.shape[0]
    vm = pl.BlockSpec(memory_space=pltpu.VMEM)
    return pl.pallas_call(
        functools.partial(layout_kernel, heads, slot_rows),
        out_shape=(
            jax.ShapeDtypeStruct((sources * rows, TOKB), jnp.int32),
            jax.ShapeDtypeStruct((own_spans, 2 * SPAN), f32),
        ),
        in_specs=[pl.BlockSpec(memory_space=pltpu.SMEM), vm],
        out_specs=(vm, vm),
        scratch_shapes=[
            pltpu.VMEM((16, TOKB), f32),
            pltpu.VMEM((16, TOKB), f32),
            pltpu.VMEM((BUCKETS + 1, 16, TOKB), f32),
        ],
        compiler_params=pltpu.CompilerParams(vmem_limit_bytes=VMEM_LIMIT),
        name="sorted_layout",
        cost_estimate=takes(5),
    )(first, codes)


def parts_kernel(
    row_pair_ref, row_far_ref, inner_pair_ref, inner_far_ref,
    hidden_pair_ref, hidden_far_ref, grad_pair_ref, grad_far_ref, out_ref,
):
    inner = against(row_pair_ref[...], inner_pair_ref[...])
    inner += against(row_far_ref[...], inner_far_ref[...])
    out_ref[0, 0] = inner.astype(bf)
    outer = against(hidden_pair_ref[...], grad_pair_ref[...])
    outer += against(hidden_far_ref[...], grad_far_ref[...])
    out_ref[0, 1] = outer.astype(bf)


def parts_product(row_pair, row_far, inner_pair, inner_far, hidden_pair, hidden_far, grads):
    rows, width = row_pair.shape
    units = hidden_pair.shape[1]
    block = pl.BlockSpec((rows, TOKB), lambda i: (0, i))

    def whole(columns):
        return pl.BlockSpec((rows, columns), lambda i: (0, 0), pipeline_mode=pl.Buffered(1))

    return pl.pallas_call(
        parts_kernel,
        grid=(width // TOKB,),
        out_shape=jax.ShapeDtypeStruct((width // TOKB, 2, TOKB, width), bf),
        in_specs=[block, block, whole(units), whole(units), block, block]
        + [whole(width), whole(width)],
        out_specs=pl.BlockSpec((1, 2, TOKB, width), lambda i: (i, 0, 0, 0)),
        compiler_params=pltpu.CompilerParams(vmem_limit_bytes=VMEM_LIMIT),
        name="parts_product",
        cost_estimate=takes(0),
    )(row_pair, row_far, inner_pair, inner_far, hidden_pair, hidden_far, *grads)


ALL = ("hd", "kk", "ry", "rc")
SEQ = ("hd", "kk")
ROUND = ("ry", "rc")
SWAP = [(0, 1), (1, 0)]
RING = (0, 2, 4, 6, 7, 5, 3, 1)
UP = [(RING[i], RING[(i + 1) % HEADS]) for i in range(HEADS)]
DOWN = [(RING[(i + 1) % HEADS], RING[i]) for i in range(HEADS)]
STEPS = ((0, -1, 1, -2, 2), (-3, 3, 4))
BUCKETS = 32


def normalised(values):
    centre = values - jnp.mean(values, axis=-1, keepdims=True)
    spread = jnp.mean(centre * centre, axis=-1, keepdims=True)
    inverse = lax.rsqrt(spread + NORM_EPS)
    return centre * inverse, inverse


def norm_back(unit, inverse, grad):
    along = jnp.mean(grad * unit, axis=-1, keepdims=True)
    return inverse * (grad - jnp.mean(grad, axis=-1, keepdims=True) - unit * along)


def together(*values):
    return lax.optimization_barrier(values)


def exchange(parts, axes="hd"):
    return lax.all_to_all(parts, axes, split_axis=0, concat_axis=0, tiled=True)


def swapped(value, axis):
    return lax.ppermute(value, axis, SWAP)


def over_groups(mine):
    if lax.axis_size("kk") > 1:
        return lax.all_gather(mine, "kk", axis=0, tiled=False)
    return mine[None]


def sum_groups(parts):
    if lax.axis_size("kk") > 1:
        return lax.psum_scatter(parts, "kk", scatter_dimension=0, tiled=False)
    return parts[0]


def pair_sum(keep, give, axis):
    return (keep.astype(f32) + swapped(give, axis).astype(f32)).astype(bf)


def spread_pair(mine):
    pair = jnp.stack([mine, swapped(mine, "ry")])
    return pair, swapped(pair, "rc")


def chip_pair(mine):
    return jnp.concatenate([mine, swapped(mine, "rc")], axis=0)


def sum_pair(own, peer):
    total = pair_sum(own, peer, "rc")
    return pair_sum(total[0], total[1], "ry")


def ordered(mine, axis, dim):
    return pair_order(mine, swapped(mine, axis), axis, dim)


def pair_order(mine, got, axis, dim):
    is_first = lax.axis_index(axis) == 0
    return jnp.stack([jnp.where(is_first, mine, got), jnp.where(is_first, got, mine)], axis=dim)


def scattered(parts, axis, dim):
    me = lax.axis_index(axis)
    keep = lax.dynamic_index_in_dim(parts, me, dim, keepdims=False)
    give = lax.dynamic_index_in_dim(parts, 1 - me, dim, keepdims=False)
    return pair_sum(keep, give, axis)


def ring_step(up, down):
    return lax.ppermute(up, "hd", UP), lax.ppermute(down, "hd", DOWN)


def ring_order():
    position = jnp.array([RING.index(i) for i in range(HEADS)], jnp.int32)[lax.axis_index("hd")]
    offsets = jnp.array([o for step in STEPS for o in step], jnp.int32)
    return jnp.array(RING, jnp.int32)[(position + offsets) % HEADS]


def wide_scattered(parts, axis, dim):
    me = lax.axis_index(axis)
    keep = lax.dynamic_index_in_dim(parts, me, dim, keepdims=False)
    return keep + swapped(lax.dynamic_index_in_dim(parts, 1 - me, dim, keepdims=False), axis)


def traded(parts, axis, dim):
    me = lax.axis_index(axis)
    got = swapped(lax.dynamic_index_in_dim(parts, 1 - me, dim, keepdims=True), axis)
    return lax.dynamic_update_slice_in_dim(parts, got, 1 - me, dim)


def index_codes(slots, buckets, slot_rows):
    first_bucket = slots // slot_rows * BUCKETS
    return jnp.concatenate([slots // 256, slots % 256, buckets - first_bucket]).astype(bf)


def sorted_layout(codes, slot_rows, own_spans):
    heads = lax.axis_size("hd")
    codes = codes.astype(jnp.int32)
    slot_grid = codes[:, :, 0] * 256 + codes[:, :, 1]
    before = lax.axis_index("kk") * heads - 1
    target = slot_grid // slot_rows
    block = target - before
    local_place = slot_grid - target * slot_rows
    category = (block * (BUCKETS + 1) + codes[:, :, 2]).reshape(1, -1)
    categories = jnp.arange((heads + 1) * (BUCKETS + 1), dtype=jnp.int32)[:, None]
    members = jnp.sum((category == categories).astype(jnp.int32), axis=1)
    members = members.reshape(heads + 1, BUCKETS + 1)
    counts = jnp.sum(members, axis=1)
    last_start = jnp.maximum(counts[:1] - 1, 0) // SPAN * SPAN
    span_counts = -(-counts[1:] // SPAN)
    own_start = (1 + jnp.cumsum(span_counts) - span_counts) * SPAN
    start = jnp.concatenate([-last_start, own_start])
    lowest = jnp.concatenate([last_start, jnp.zeros_like(own_start)])
    dump = (own_spans + 1) * SPAN
    numbers = jnp.arange(heads + 1, dtype=jnp.int32)[:, None]
    local_place, block = local_place.reshape(1, -1), block.reshape(1, -1)
    here = (block == numbers) & (local_place >= lowest[:, None])
    place = jnp.sum(jnp.where(here, local_place + start[:, None] - dump, 0), axis=0) + dump
    ends = (start[:, None] + jnp.cumsum(members, axis=1)).reshape(-1, 1)
    rows = jnp.arange(dump, dtype=jnp.int32)[None, :]
    passed = jnp.sum((ends <= rows).astype(jnp.int32), axis=0)
    row_block = jnp.sum((own_start[:, None] <= rows).astype(jnp.int32), axis=0)
    local_bucket = passed - row_block * (BUCKETS + 1)
    row_bucket = jnp.where(
        local_bucket <= BUCKETS, (before + row_block) * BUCKETS + local_bucket, -1
    )
    span_bucket = row_bucket.astype(f32).reshape(-1, SPAN)
    return place, jnp.concatenate([span_bucket[:-1], span_bucket[1:]], axis=1)


def chunk_tables(groups):
    order = ring_order()
    flip = jnp.stack([lax.axis_index("rc"), lax.axis_index("ry")])

    def number(dc, dy, kk, hd):
        return ((hd * groups + kk) * 2 + (dy ^ flip[1])) * 2 + (dc ^ flip[0])

    def column(values):
        return jnp.array(values, jnp.int32)

    offsets = [list(range(sum(map(len, STEPS[:i])), sum(map(len, STEPS[: i + 1])))) for i in range(len(STEPS))]
    coming = [
        (dc, dy, kk, at)
        for dc in range(2)
        for part in offsets
        for dy in range(2)
        for kk in range(groups)
        for at in part
    ]
    going = [
        (dc, dy, kk, hd)
        for dc in range(2)
        for dy in range(2)
        for kk in range(groups)
        for hd in range(HEADS)
    ]
    dc, dy, kk, at = map(column, zip(*coming))
    in_table = number(dc, dy, kk, order[at])
    return in_table, number(*map(column, zip(*going)))


def per_device(
    first_half,
    second_half,
    qk_weight,
    value_weight,
    output_weight,
    inner_weight,
    outer_weight,
    attn_gain,
    attn_shift,
    ffn_gain,
    ffn_shift,
    buckets,
    slots,
    first_grad,
    second_grad,
):
    heads = lax.axis_size("hd")
    groups = lax.axis_size("kk")
    seq_count = heads * groups
    round_count = lax.axis_size("ry") * lax.axis_size("rc")
    device_count = seq_count * round_count
    own_rows, model_width = first_half.shape
    weight_rows, hidden_width = inner_weight.shape
    group_rows = own_rows * round_count
    slot_rows = 2 * group_rows
    tokens = group_rows * seq_count
    own_spans = min((tokens + (SPAN - 1) * heads) // SPAN, heads * slot_rows // SPAN)
    own_spans = -(-own_spans // UNROLL) * UNROLL
    piece = hidden_width // device_count
    blocks = own_rows // TOKB
    both = 2 * HEADD

    vectors = jnp.stack([attn_gain, attn_shift, ffn_gain, ffn_shift], axis=1)
    vectors = jnp.pad(vectors, ((0, 0), (0, HEADD - 4)))
    wide = both + HEADD
    head_shard = jnp.concatenate(
        [
            qk_weight.reshape(weight_rows, heads, HEADD),
            value_weight.reshape(weight_rows, heads, HEADD),
            jnp.broadcast_to(vectors[:, None], (weight_rows, heads, HEADD)),
        ],
        axis=2,
    )
    code_rows = 3 * group_rows // wide
    codes = index_codes(slots, buckets, slot_rows).reshape(code_rows, wide)
    codes = jnp.pad(codes, ((0, -code_rows % PAD), (0, 0)))
    codes = jnp.broadcast_to(codes[None], (heads,) + codes.shape)
    starter = jnp.concatenate([jnp.transpose(head_shard, (1, 0, 2)), codes], axis=1)

    second_later, starter = together(second_half, starter)
    second_in = second_later.astype(f32)
    unit, unit_scale = normalised(second_in)
    unit_low = unit.astype(bf)
    inner_split = inner_weight.reshape(weight_rows, seq_count, round_count, piece)
    inner_split = jnp.transpose(inner_split, (2, 0, 1, 3)).reshape(2, 2, weight_rows, -1)
    ring = [(unit_low,)]
    up, down = ring_step(unit_low, unit_low)
    inner_rows = traded(traded(inner_split, "rc", 1), "ry", 0)
    cut = round_count * weight_rows
    output_rows = ordered(ordered(output_weight, "rc", 0), "ry", 0).reshape(cut, model_width)
    shard = jnp.stack([inner_rows.reshape(cut, -1), outer_weight, output_rows])
    up, down, starter, shard = together(up, down, exchange(starter), shard)
    ring.append((up, down))

    up, down = ring_step(up, down)
    starter = jnp.transpose(over_groups(starter), (1, 0, 2, 3))
    codes = starter[:, :, weight_rows : weight_rows + code_rows].reshape(heads, groups, 3, -1)
    head_weight = ordered(ordered(starter[:, :, :weight_rows], "ry", 2), "rc", 3)
    head_weight = head_weight.reshape(model_width, wide)
    vectors_full = head_weight[:, both : both + 4].astype(f32)
    attn_gain_col, attn_shift_col = vectors_full[:, :1], vectors_full[:, 1:2]
    ffn_gain_row, ffn_shift_row = vectors_full[:, 2][None], vectors_full[:, 3][None]
    head_float = head_weight[:, :both].astype(f32)
    head_scaled = (head_float * attn_gain_col).astype(bf)
    head_offset = jnp.sum(head_float * attn_shift_col, axis=0, keepdims=True)
    up, down, head_scaled, head_offset, shard, second_later = together(
        up, down, head_scaled, head_offset, shard, second_grad
    )
    ring.append((up, down))

    def head_part(parts):
        rows = [product(part, head_scaled) + head_offset for part in parts]
        return over_groups(jnp.concatenate(rows, axis=0).astype(bf))

    up, down = ring_step(up, down)
    first_heads = head_part([part for step in ring for part in step])
    up, down, codes, shard = together(up, down, codes, shard)
    ring.append((up, down))

    half = own_rows // 2
    up, down = ring_step(up[:half], down[half:])
    up, down, first_swapped = together(up, down, swapped(first_heads, "ry"))
    ring.append((up, down))
    last_heads = head_part(ring[3] + ring[4])
    head_own = [first_heads, first_swapped, last_heads, swapped(last_heads, "ry")]
    head_own = jnp.concatenate([part.reshape(-1, both) for part in head_own], axis=0)
    place, key_bucket = sorted_layout(codes, slot_rows, own_spans)
    in_table, out_table = chunk_tables(groups)
    head_own, place, key_bucket, in_table, out_table = together(
        head_own, place, key_bucket, in_table, out_table
    )
    head_peer = swapped(head_own, "rc")

    grad_peer = swapped(second_later, "rc")
    grad_far = swapped(second_later, "ry")
    grad_last = swapped(grad_far, "rc")
    shards = lax.all_gather(shard, SEQ, axis=0, tiled=False)

    payload_own, payload_peer, sorted_q, sorted_k, sorted_v, probs, token_sums = attend_forward(
        in_table,
        out_table,
        place,
        key_bucket,
        head_own,
        head_peer,
        own_rows,
    )
    packed = (2, groups, heads, own_rows + PAD, HEADD)
    head_sums = sum_pair(payload_own.reshape(packed), payload_peer.reshape(packed))
    mixed_parts = exchange(sum_groups(head_sums))
    mixed_parts, shards = together(mixed_parts, shards)
    mixed_low, first_sum, ffn_unit, ffn_scale, ffn_low = mix_rows(
        mixed_parts, shards, first_half, ffn_gain_row, ffn_shift_row
    )
    ffn_low, qkv_rows = together(ffn_low, jnp.stack([qk_weight, value_weight]))
    qkv_rows = exchange(jnp.broadcast_to(qkv_rows[None], (heads,) + qkv_rows.shape))
    ffn_far = swapped(ffn_low, "ry")
    pair = feed_forward(ffn_low, swapped(ffn_low, "rc"), second_later, grad_peer, shards)
    ffn_far, pair = together(ffn_far, pair)
    far = feed_forward(ffn_far, swapped(ffn_far, "rc"), grad_far, grad_last, shards)
    pair, far = together(pair, far)
    ffn_pair, grad_pair, hidden_pair, inner_pair, *back_pair = pair
    ffn_far, grad_far, hidden_far, inner_far, *back_far = far
    far_sum = swapped(pair_sum(back_far[0], back_far[1], "rc"), "ry")
    near_sum = pair_sum(back_pair[0], back_pair[1], "rc")
    second_far = pair_sum(back_far[2], back_far[3], "rc")
    second_pair = pair_sum(back_pair[2], back_pair[3], "rc")
    part_sums = parts_product(
        ffn_pair,
        ffn_far,
        inner_pair,
        inner_far,
        hidden_pair,
        hidden_far,
        (grad_pair, grad_far),
    )
    part_sums = part_sums.reshape(-1, 2, TOKB // cut, cut, model_width)
    part_sums = jnp.transpose(part_sums, (0, 2, 1, 3, 4)).reshape(seq_count, 2, cut, model_width)
    near_sum, far_sum, part_sums, qkv_rows = together(near_sum, far_sum, part_sums, qkv_rows)
    part_grads = lax.psum_scatter(part_sums, SEQ, scatter_dimension=0, tiled=False)
    carry_low, back_parts = carry_rows(
        near_sum,
        far_sum,
        ffn_gain_row,
        ffn_unit,
        ffn_scale,
        first_grad,
        shards,
        mixed_low,
        mixed_parts,
    )
    back_parts = exchange(back_parts)
    output_part = against(mixed_low, carry_low).astype(bf)
    output_part = output_part.reshape(heads, groups, 2, 2, weight_rows, model_width)
    output_part = scattered(scattered(output_part, "rc", 3), "ry", 2)
    back_parts, output_part, second_pair, second_far, qkv_rows = together(
        back_parts, output_part, second_pair, second_far, qkv_rows
    )
    qkv_rows = jnp.transpose(over_groups(qkv_rows), (2, 1, 0, 3, 4))
    back_own, back_peer = spread_pair(over_groups(back_parts))
    back_own, second_far, qkv_rows, output_part = together(
        back_own, second_far, qkv_rows, output_part
    )
    output_rows = exchange(sum_groups(jnp.transpose(output_part, (1, 0, 2, 3))))
    second_far = swapped(second_far, "ry")
    qkv_got = swapped(qkv_rows, "ry")
    query_value_own, query_value_peer = attend_backward(
        out_table,
        place,
        back_own.reshape(-1, HEADD),
        back_peer.reshape(-1, HEADD),
        token_sums,
        sorted_q,
        sorted_k,
        sorted_v,
        probs,
        own_rows,
    )
    vector_rows = back_parts[:, own_rows + 2 * blocks : own_rows + 2 * blocks + 2]
    packed = (2, groups, heads, own_rows, both)
    vector_rows = back_parts[:, own_rows + 2 * blocks : own_rows + 2 * blocks + 2]
    packed = (2, groups, heads, own_rows, both)
    query_value_peer, qkv_got, second_far, output_rows = together(
        query_value_peer, qkv_got, second_far, output_rows
    )
    second_sum = second_in + second_pair.astype(f32) + second_far.astype(f32)
    query_value_own = query_value_own.reshape(packed)
    query_value_peer = swapped(query_value_peer.reshape(packed), "rc")

    def summed(part):
        return (query_value_own[part].astype(f32) + query_value_peer[part].astype(f32)).astype(bf)

    head_send = summed(1)
    head_send, output_rows, vector_rows, qkv_rows, qkv_got = together(
        head_send, output_rows, vector_rows, qkv_rows, qkv_got
    )
    qkv_rows = pair_order(qkv_rows, qkv_got, "ry", 3)
    qkv_full = ordered(qkv_rows, "rc", 4).reshape(2, model_width, model_width)
    head_got, qkv_full, head_keep = together(swapped(head_send, "ry"), qkv_full, summed(0))
    output_grad = jnp.sum(output_rows.astype(f32), axis=0)
    head_back = sum_groups(add_rows(head_keep, head_got))
    own_back = exchange(head_back)
    vector_sums = jnp.sum(vector_rows.astype(f32), axis=0)
    if groups > 1:
        vector_sums = lax.psum_scatter(
            vector_sums.reshape(2, groups, -1), "kk", scatter_dimension=1, tiled=False
        )
    vector_sums = jnp.pad(
        vector_sums.reshape(2, 2, 2, weight_rows), ((0, 6), (0, 0), (0, 0), (0, HEADD - weight_rows))
    )
    pieces = [part for step in ring for part in step]
    qkv_part, col_part = weight_part(ring_order(), head_back, pieces)
    qkv_part = qkv_part.reshape(heads, groups, 2, 2, weight_rows, both)
    col_part = jnp.broadcast_to(col_part[0], (heads, groups, 2, 2, PAD, both))
    qkv_part = jnp.concatenate([qkv_part, col_part], axis=4).astype(bf)
    qkv_part = scattered(scattered(qkv_part, "rc", 3), "ry", 2)
    qkv_part = sum_groups(jnp.transpose(qkv_part, (1, 0, 2, 3)))
    outer_grad = part_grads[1].astype(f32)
    turned = part_grads[0].reshape(2, 2, weight_rows, -1)
    turned = traded(traded(turned, "ry", 0), "rc", 1)
    vector_sums = wide_scattered(wide_scattered(vector_sums, "rc", 2), "ry", 1)
    vector_grads = vector_sums[:2, :weight_rows]
    own_back, qkv_part, turned = together(own_back, qkv_part, turned)
    inner_cols = turned.reshape(round_count, weight_rows, seq_count, piece)
    inner_grad = jnp.transpose(inner_cols, (1, 2, 0, 3)).reshape(weight_rows, hidden_width)
    qkv_rows = exchange(qkv_part).astype(f32)
    qkv_rows = qkv_rows.reshape(heads, weight_rows + PAD, 2, HEADD)
    qkv_rows = jnp.transpose(qkv_rows, (2, 1, 0, 3)).reshape(2, weight_rows + PAD, model_width)
    unit_grads, col_sums = qkv_rows[:, :weight_rows], qkv_rows[:, weight_rows]
    own_weights = jnp.stack([qk_weight, value_weight]).astype(f32)
    gain_own = attn_gain.astype(f32)[:, None]
    shift_own = attn_shift.astype(f32)[:, None]
    qkv_grads = unit_grads * gain_own + shift_own * col_sums[:, None]
    attn_gain_grad = jnp.sum(own_weights * unit_grads, axis=(0, 2))
    attn_shift_grad = jnp.sum(own_weights * col_sums[:, None], axis=(0, 2))

    second_carry = last_rows(
        own_back, qkv_full, attn_gain_col.reshape(1, -1), unit, unit_scale, second_grad
    )

    return (
        first_sum,
        second_sum.astype(bf),
        carry_low,
        second_carry,
        qkv_grads[0],
        qkv_grads[1],
        output_grad,
        inner_grad.astype(f32),
        outer_grad,
        attn_gain_grad,
        attn_shift_grad,
        vector_grads[0],
        vector_grads[1],
    )


def solution(mesh):
    seq_count, round_count = mesh.devices.shape
    shape = (HEADS, seq_count // HEADS, round_count // 2, 2)
    split_mesh = Mesh(mesh.devices.reshape(shape), ALL)
    rows = P(ALL, None)
    vector = P(ALL)
    table = P(ROUND, SEQ)
    in_specs = (rows,) * 7 + (vector,) * 4 + (table,) * 2 + (rows,) * 2
    out_specs = (rows,) * 9 + (vector,) * 4
    return jax.shard_map(
        per_device, mesh=split_mesh, in_specs=in_specs, out_specs=out_specs, check_vma=False
    )
```
